32 devices in a mesh: rep: 4 (over z), fsdp: 8 (over y, x, core).
Axes of the slice: x: 2, y: 2, z: 4, core: 2. Of those that a mesh axis runs over, the one named last changes fastest.
Arguments:
- latents: float32 [2, 32, 256, 16], P(None, ('rep', 'fsdp')), may hold values from -6 to 6
- noise: float32 [2, 32, 256, 16], P(None, ('rep', 'fsdp')), may hold values from -6 to 6
- timesteps: int32 [2, 32], P(None, ('rep', 'fsdp')), may hold values from 0 to 999
- labels: int32 [2, 32], P(None, ('rep', 'fsdp')), may hold values from 0 to 1000
- patch_state: float32 [2, 16, 384], P(None, None, 'fsdp'), may hold values from -1 to 1, as said below
- time1_w: float32 [256, 384], P('fsdp'), may hold values from -0.375 to 0.375
- time1_f: float32 [640], replicated, may hold values from 0.001 to 1
- time2_w: float32 [384, 384], P('fsdp'), may hold values from -0.3125 to 0.3125
- time2_f: float32 [768], replicated, may hold values from 0.001 to 1
- table_w: float32 [1001, 384], P(None, 'fsdp'), may hold values from -4 to 4
- table_f: float32 [1385], replicated, may hold values from 0.001 to 1
- mod_w: float32 [384, 3072], P('fsdp'), may hold values from -0.3125 to 0.3125
- mod_f: float32 [3456], replicated, may hold values from 0.001 to 1
- qkv_w: float32 [384, 1152], P('fsdp'), may hold values from -0.3125 to 0.3125
- qkv_f: float32 [1536], replicated, may hold values from 0.001 to 1
- proj_w: float32 [384, 384], P('fsdp'), may hold values from -1.25 to 1.25
- proj_f: float32 [768], replicated, may hold values from 0.001 to 1
- fc1_w: float32 [384, 1536], P('fsdp'), may hold values from -0.3125 to 0.3125
- fc1_f: float32 [1920], replicated, may hold values from 0.001 to 1
- fc2_w: float32 [1536, 384], P('fsdp'), may hold values from -0.15625 to 0.15625
- fc2_f: float32 [1920], replicated, may hold values from 0.001 to 1
- out_state: float32 [2, 384, 32], P(None, 'fsdp'), may hold values from -1 to 1, as said below
Outputs:
- new_patch: float32 [2, 16, 384], P(None, None, 'fsdp')
- new_time1: float32 [256, 384], P('fsdp')
- new_time1_f: float32 [640], replicated
- new_time2: float32 [384, 384], P('fsdp')
- new_time2_f: float32 [768], replicated
- new_table: float32 [1001, 384], P(None, 'fsdp')
- new_table_f: float32 [1385], replicated
- new_mod: float32 [384, 3072], P('fsdp')
- new_mod_f: float32 [3456], replicated
- new_qkv: float32 [384, 1152], P('fsdp')
- new_qkv_f: float32 [1536], replicated
- new_proj: float32 [384, 384], P('fsdp')
- new_proj_f: float32 [768], replicated
- new_fc1: float32 [384, 1536], P('fsdp')
- new_fc1_f: float32 [1920], replicated
- new_fc2: float32 [1536, 384], P('fsdp')
- new_fc2_f: float32 [1920], replicated
- new_out: float32 [2, 384, 32], P(None, 'fsdp')
- loss: float32 [], replicated
- update_rms: float32 [10], replicated
The draws below stay inside these ranges and needn't reach their ends.
Inputs may be any that keep to these rules, and one draw needn't show every extreme that they name: `patch_state`: the first slice holds weights, the second positive second moments. `out_state`: the first slice holds weights, the second positive second moments.
All inputs are finite; a program needn't handle non-finite values.
Results may differ from the reference program's by a relative error of at most 0.0085.
The reference program's roundings to bfloat16 on the way count: a program that leaves them out, or rounds other values in their place, can miss the bound.
Values may be sent and summed in bfloat16 or wider, within the bound.
No kernel may reach another device: no remote copies, remote signals or barrier semaphores. Data moves between devices by JAX's collectives and lax.ppermute only.
A program may use at most 128 MiB of HBM per device.

```python
import math
import jax
import jax.numpy as jnp
from jax import lax

D = 384
HEADS = 6
HEAD_DIM = 64
FF = 1536
TFREQ = 256
GRID = 16
PIN = 16
POUT = 32
CLASSES = 1001
STEPS = 1000
MICRO = 2
TOK_IMG = 256
IMG_MB = 32
IMAGES = 64


def state_pair(key, row_count, col_count, spread):
    weight_key = jax.random.fold_in(key, 11)
    moment_key = jax.random.fold_in(key, 12)
    weight_part = jnp.clip(jax.random.normal(weight_key, (row_count, col_count), jnp.float32) * spread, -4.0 * spread, 4.0 * spread)
    moment_part = jnp.exp(jax.random.uniform(moment_key, (row_count, col_count), jnp.float32, math.log(0.001), 0.0))
    return jnp.stack([weight_part, moment_part]).astype(jnp.float32)


def draw_patch_state(key, part):
    return state_pair(key, PIN, D, PIN ** (-0.5))


def draw_out_state(key, part):
    return state_pair(key, D, POUT, D ** (-0.5))


def with_ends(result, key, least, largest):
    place = [jax.random.randint(jax.random.fold_in(key, axis), (), 0, length) for axis, length in enumerate(result.shape)]
    main_axis = result.shape.index(max(result.shape))
    neighbour = place[:main_axis] + [(place[main_axis] + 1) % result.shape[main_axis]] + place[main_axis + 1:]
    return result.at[tuple(place)].set(least).at[tuple(neighbour)].set(largest)


def levels(own_key, extent, cuts, low, high):
    gain = 1.0
    for dim, blocks in cuts:
        draws = jax.random.uniform(jax.random.fold_in(jax.random.fold_in(own_key, 6), dim), (blocks,), jnp.float32, low / len(cuts), high / len(cuts))
        gain = gain * jnp.repeat(jnp.exp(draws), extent[dim] // blocks).reshape((-1,) + (1,) * (len(extent) - 1 - dim))
    return gain


def normal_values(key, extent, scale, bound, cuts=(), held_as=jnp.bfloat16):
    result = scale * jax.random.normal(key, extent, jnp.float32)
    if cuts:
        result = result * levels(key, extent, cuts, -0.22, 0.18)
    return jnp.clip(result, -bound, bound).astype(held_as)


def setup_inputs(seed: int = 0) -> dict:
    splits = jax.random.split(jax.random.key(seed), 23)
    return {
        "latents": normal_values(splits[0], (MICRO, IMG_MB, TOK_IMG, PIN), 1.0, 6.0, ((1, 32),), jnp.float32),
        "noise": normal_values(splits[1], (MICRO, IMG_MB, TOK_IMG, PIN), 1.0, 6.0, ((1, 32),), jnp.float32),
        "timesteps": with_ends(jax.random.randint(splits[2], (MICRO, IMG_MB), 0, STEPS), jax.random.fold_in(splits[2], 1), 0, STEPS - 1).astype(jnp.int32),
        "labels": with_ends(jax.random.randint(splits[3], (MICRO, IMG_MB), 0, CLASSES), jax.random.fold_in(splits[3], 1), 0, CLASSES - 1).astype(jnp.int32),
        "patch_state": draw_patch_state(jax.random.fold_in(splits[22], 71), 0),
        "time1_w": normal_values(splits[5], (TFREQ, D), TFREQ ** -0.5, 0.375, ((0, 8),), jnp.float32),
        "time1_f": jnp.clip(jnp.exp(jax.random.uniform(splits[6], (TFREQ + D,), jnp.float32, math.log(0.001), math.log(1.0))), 0.001, 1.0),
        "time2_w": normal_values(splits[7], (D, D), D ** -0.5, 0.3125, ((0, 8),), jnp.float32),
        "time2_f": jnp.clip(jnp.exp(jax.random.uniform(splits[8], (2 * D,), jnp.float32, math.log(0.001), math.log(1.0))), 0.001, 1.0),
        "table_w": normal_values(splits[9], (CLASSES, D), 1.0, 4.0, ((1, 8),), jnp.float32),
        "table_f": jnp.clip(jnp.exp(jax.random.uniform(splits[10], (CLASSES + D,), jnp.float32, math.log(0.001), math.log(1.0))), 0.001, 1.0),
        "mod_w": normal_values(splits[11], (D, 8 * D), D ** -0.5, 0.3125, ((0, 8),), jnp.float32),
        "mod_f": jnp.clip(jnp.exp(jax.random.uniform(splits[12], (9 * D,), jnp.float32, math.log(0.001), math.log(1.0))), 0.001, 1.0),
        "qkv_w": normal_values(splits[13], (D, 3 * D), D ** -0.5, 0.3125, ((0, 8),), jnp.float32),
        "qkv_f": jnp.clip(jnp.exp(jax.random.uniform(splits[14], (4 * D,), jnp.float32, math.log(0.001), math.log(1.0))), 0.001, 1.0),
        "proj_w": normal_values(splits[15], (D, D), (D // 16) ** -0.5, 1.25, ((0, 8),), jnp.float32),
        "proj_f": jnp.clip(jnp.exp(jax.random.uniform(splits[16], (2 * D,), jnp.float32, math.log(0.001), math.log(1.0))), 0.001, 1.0),
        "fc1_w": normal_values(splits[17], (D, FF), D ** -0.5, 0.3125, ((0, 8),), jnp.float32),
        "fc1_f": jnp.clip(jnp.exp(jax.random.uniform(splits[18], (D + FF,), jnp.float32, math.log(0.001), math.log(1.0))), 0.001, 1.0),
        "fc2_w": normal_values(splits[19], (FF, D), FF ** -0.5, 0.15625, ((0, 8),), jnp.float32),
        "fc2_f": jnp.clip(jnp.exp(jax.random.uniform(splits[20], (FF + D,), jnp.float32, math.log(0.001), math.log(1.0))), 0.001, 1.0),
        "out_state": draw_out_state(jax.random.fold_in(splits[22], 71), 0),
    }


@jax.custom_vjp
def low(v):
    return lax.optimization_barrier(v.astype(jnp.bfloat16)).astype(jnp.float32)

@jax.custom_vjp
def low_back(v):
    return v

def low_keep(v):
    return (low(v), None)

def low_pass(kept, grad):
    return (grad,)

def back_keep(v):
    return (v, None)

def back_low(kept, grad):
    return (low(grad),)
low.defvjp(low_keep, low_pass)
low_back.defvjp(back_keep, back_low)
decay_rate = 0.5
clip_level = 1.0
step_rate = 0.5
grad_floor = 1e-30
norm_floor = 1e-06
top_precision = lax.Precision.HIGHEST

def product(left, right):
    return jnp.matmul(left, right, precision=top_precision)

def diffusion_tables():
    position = jnp.arange(STEPS, dtype=jnp.float32)
    betas = 0.0001 + (0.02 - 0.0001) * position / (STEPS - 1)
    log_bar = jnp.cumsum(jnp.log1p(-betas))
    log_prev = jnp.concatenate([jnp.zeros((1,), jnp.float32), log_bar[:-1]])
    posterior = betas * -jnp.expm1(log_prev) / -jnp.expm1(log_bar)
    posterior = jnp.where(position == 0.0, posterior[1], posterior)
    return (betas, log_bar, jnp.log(posterior))

def step_constants(tsteps):
    betas, log_bar, log_post = diffusion_tables()
    picks = tsteps[:, None] == jnp.arange(STEPS, dtype=jnp.int32)[None, :]

    def choose(table):
        return lax.optimization_barrier(jnp.sum(jnp.where(picks, table[None, :], 0.0), axis=1))
    beta_now = choose(betas)
    bar_log = choose(log_bar)
    post_log = choose(log_post)
    remain = -jnp.expm1(bar_log)
    coef_sq = beta_now * beta_now / ((1.0 - beta_now) * remain)
    return (jnp.exp(0.5 * bar_log), jnp.sqrt(remain), jnp.log(beta_now), post_log, coef_sq)

def time_features(tsteps):
    halfway = TFREQ // 2
    frequency = jnp.exp(-math.log(10000.0) * jnp.arange(halfway, dtype=jnp.float32) / halfway)
    angles = tsteps.astype(jnp.float32)[:, None] * frequency[None, :]
    return jnp.concatenate([jnp.cos(angles), jnp.sin(angles)], axis=1)

def grid_positions():
    quarter = D // 4
    omegas = jnp.exp(-math.log(10000.0) * jnp.arange(quarter, dtype=jnp.float32) / quarter)
    tokens = jnp.arange(TOK_IMG, dtype=jnp.int32)
    row_pos = (tokens // GRID).astype(jnp.float32)[:, None] * omegas[None, :]
    col_pos = (tokens % GRID).astype(jnp.float32)[:, None] * omegas[None, :]
    return jnp.concatenate([jnp.sin(row_pos), jnp.cos(row_pos), jnp.sin(col_pos), jnp.cos(col_pos)], axis=1)

def layer_norm(x):
    average = lax.optimization_barrier(jnp.mean(x, axis=-1, keepdims=True))
    centred = x - average
    variance = lax.optimization_barrier(jnp.mean(centred * centred, axis=-1, keepdims=True))
    return centred * lax.rsqrt(variance + norm_floor)

def modulate(hidden, modulation, slot):
    offset = modulation[:, slot * D:(slot + 1) * D][:, None, :]
    stretch = modulation[:, (slot + 1) * D:(slot + 2) * D][:, None, :]
    return layer_norm(hidden) * (1.0 + stretch) + offset

def image_losses(output, noise, consts):
    log_beta = consts[2][:, None, None]
    post_log = consts[3][:, None, None]
    guess = output[..., :PIN]
    mixing = (output[..., PIN:] + 1.0) * 0.5
    log_var = mixing * log_beta + (1.0 - mixing) * post_log
    miss_noise = guess - noise
    squared = miss_noise * miss_noise
    diverge = 0.5 * (-1.0 + log_var - post_log + jnp.exp(post_log - log_var) + consts[4][:, None, None] * squared * jnp.exp(-log_var))
    return lax.optimization_barrier(jnp.mean(squared + diverge, axis=(1, 2)))

def group_loss(weights, latents, noise, tsteps, labels):
    w_patch, w_time1, w_time2, w_table, w_mod, w_qkv, w_proj, w_fc1, w_fc2, w_out = weights
    images = latents.shape[0]
    consts = step_constants(tsteps)
    noisy = consts[0][:, None, None] * latents + consts[1][:, None, None] * noise
    hidden0 = low_back(product(low(noisy), w_patch)) + grid_positions()[None]
    time_hidden = low_back(product(low(time_features(tsteps)), w_time1))
    time_emb = low_back(product(low(jax.nn.silu(time_hidden)), w_time2))
    condition = time_emb + jnp.take(w_table, labels, axis=0)
    modulation = low_back(product(low(jax.nn.silu(condition)), w_mod))
    attn_in = low(modulate(hidden0, modulation, 0))
    qkv = low_back(product(attn_in, w_qkv))
    queries = low(qkv[..., :D]).reshape(images, TOK_IMG, HEADS, HEAD_DIM)
    keyset = low(qkv[..., D:2 * D]).reshape(images, TOK_IMG, HEADS, HEAD_DIM)
    values = low(qkv[..., 2 * D:]).reshape(images, TOK_IMG, HEADS, HEAD_DIM)
    scores = low_back(jnp.einsum('nqhd,nkhd->nhqk', queries, keyset, precision=top_precision) * 0.125)
    attn_prob = low(jax.nn.softmax(scores, axis=-1))
    mixture = jnp.einsum('nhqk,nkhd->nqhd', attn_prob, values, precision=top_precision).reshape(images, TOK_IMG, D)
    mixture = low(low_back(mixture))
    branch = low_back(product(mixture, w_proj))
    hidden1 = hidden0 + modulation[:, None, 2 * D:3 * D] * branch
    mlp_in = low(modulate(hidden1, modulation, 3))
    inner_pre = low_back(product(mlp_in, w_fc1))
    activated = low(jax.nn.gelu(inner_pre, approximate=True))
    outer_out = low_back(product(activated, w_fc2))
    hidden2 = hidden1 + modulation[:, None, 5 * D:6 * D] * outer_out
    final_in = low(modulate(hidden2, modulation, 6))
    output = low_back(product(final_in, w_out))
    return image_losses(output, noise, consts)

def factored_step(grad, master, previous):
    row_count, col_count = grad.shape
    squares = grad * grad + grad_floor
    fresh_means = jnp.concatenate([lax.optimization_barrier(jnp.mean(squares, axis=1)), lax.optimization_barrier(jnp.mean(squares, axis=0))])
    renewed = decay_rate * previous + (1.0 - decay_rate) * fresh_means
    row_part = renewed[:row_count]
    col_part = renewed[row_count:]
    estimate = row_part[:, None] * col_part[None, :] / jnp.mean(row_part)
    update = grad * lax.rsqrt(estimate)
    size_rms = jnp.sqrt(jnp.mean(update * update))
    weight_rms = jnp.sqrt(jnp.mean(master * master))
    renewed_master = master - step_rate * weight_rms * update / jnp.maximum(1.0, size_rms / clip_level)
    return (renewed_master, fresh_means, size_rms)

def plain_step(grad, state):
    master = state[0]
    squares = grad * grad + grad_floor
    renewed = decay_rate * state[1] + (1.0 - decay_rate) * squares
    update = grad * lax.rsqrt(renewed)
    size_rms = jnp.sqrt(jnp.mean(update * update))
    weight_rms = jnp.sqrt(jnp.mean(master * master))
    renewed_master = master - step_rate * weight_rms * update / jnp.maximum(1.0, size_rms / clip_level)
    return (jnp.stack([renewed_master, renewed]), size_rms)

def reference(latents, noise, timesteps, labels, patch_state, time1_w, time1_f, time2_w, time2_f, table_w, table_f, mod_w, mod_f, qkv_w, qkv_f, proj_w, proj_f, fc1_w, fc1_f, fc2_w, fc2_f, out_state):
    masters = (patch_state[0], time1_w, time2_w, table_w, mod_w, qkv_w, proj_w, fc1_w, fc2_w, out_state[0])
    image_total = MICRO * IMG_MB
    group_size = math.gcd(16, image_total)
    group_count = image_total // group_size
    latent_groups = latents.reshape(group_count, group_size, TOK_IMG, PIN)
    noise_groups = noise.reshape(group_count, group_size, TOK_IMG, PIN)
    step_groups = timesteps.reshape(group_count, group_size)
    label_groups = labels.reshape(group_count, group_size)

    def objective(weights):
        rounded = tuple((low(w) for w in weights))

        def group_step(carry, pieces):
            return (carry + jnp.sum(group_loss(rounded, pieces[0], pieces[1], pieces[2], pieces[3])), None)
        summed, _ = lax.scan(jax.checkpoint(group_step), jnp.zeros((), jnp.float32), (latent_groups, noise_groups, step_groups, label_groups))
        return summed
    summed, pullback = jax.vjp(objective, masters)
    gradients = pullback(jnp.ones((), jnp.float32))[0]
    new_patch, rms_patch = plain_step(gradients[0], patch_state)
    new_time1, new_time1_f, rms_time1 = factored_step(gradients[1], time1_w, time1_f)
    new_time2, new_time2_f, rms_time2 = factored_step(gradients[2], time2_w, time2_f)
    new_table, new_table_f, rms_table = factored_step(gradients[3], table_w, table_f)
    new_mod, new_mod_f, rms_mod = factored_step(gradients[4], mod_w, mod_f)
    new_qkv, new_qkv_f, rms_qkv = factored_step(gradients[5], qkv_w, qkv_f)
    new_proj, new_proj_f, rms_proj = factored_step(gradients[6], proj_w, proj_f)
    new_fc1, new_fc1_f, rms_fc1 = factored_step(gradients[7], fc1_w, fc1_f)
    new_fc2, new_fc2_f, rms_fc2 = factored_step(gradients[8], fc2_w, fc2_f)
    new_out, rms_out = plain_step(gradients[9], out_state)
    loss = summed / IMAGES
    update_rms = jnp.stack([rms_patch, rms_time1, rms_time2, rms_table, rms_mod, rms_qkv, rms_proj, rms_fc1, rms_fc2, rms_out])
    return (new_patch, new_time1, new_time1_f, new_time2, new_time2_f, new_table, new_table_f, new_mod, new_mod_f, new_qkv, new_qkv_f, new_proj, new_proj_f, new_fc1, new_fc1_f, new_fc2, new_fc2_f, new_out, loss, update_rms)
```

```python
import math

import jax
import jax.numpy as jnp
import numpy as np
from jax import lax
from jax.sharding import PartitionSpec as P

D = 384
HEADS = 6
HEAD_DIM = 64
FF = 1536
TFREQ = 256
GRID = 16
PIN = 16
POUT = 32
CLASSES = 1001
STEPS = 1000
TOK_IMG = 256

decay_rate = 0.5
clip_level = 1.0
step_rate = 0.5
grad_floor = 1e-30
norm_floor = 1e-06
f32 = jnp.float32
bf16 = jnp.bfloat16


def plan_table():
    s = np.arange(STEPS, dtype=np.float64)
    beta = 1e-4 + (0.02 - 1e-4) * s / (STEPS - 1)
    lbar = np.cumsum(np.log1p(-beta))
    lprev = np.concatenate([[0.0], lbar[:-1]])
    post = beta * -np.expm1(lprev) / -np.expm1(lbar)
    post[0] = post[1]
    remain = -np.expm1(lbar)
    coef = beta * beta / ((1.0 - beta) * remain)
    rows = [np.exp(0.5 * lbar), np.sqrt(remain), np.log(beta), np.log(post), coef]
    return np.stack(rows + [np.zeros(STEPS)] * 3, axis=1).astype(np.float32)


def time_table():
    half = TFREQ // 2
    freq = np.exp(np.float32(-math.log(10000.0)) * np.arange(half, dtype=np.float32) / np.float32(half)).astype(np.float32)
    angles = np.arange(STEPS, dtype=np.float32)[:, None] * freq[None, :]
    wide = angles.astype(np.float64)
    return np.concatenate([np.cos(wide), np.sin(wide)], axis=1).astype(np.float32)


def place_table():
    quarter = D // 4
    om = np.exp(np.float32(-math.log(10000.0)) * np.arange(quarter, dtype=np.float32) / np.float32(quarter)).astype(np.float32)
    n = np.arange(TOK_IMG)
    row = ((n // GRID).astype(np.float32)[:, None] * om[None, :]).astype(np.float64)
    col = ((n % GRID).astype(np.float32)[:, None] * om[None, :]).astype(np.float64)
    return np.concatenate([np.sin(row), np.cos(row), np.sin(col), np.cos(col)], axis=1).astype(np.float32)


def pick(index, count):
    return (index[:, None] == jnp.arange(count, dtype=jnp.int32)[None, :]).astype(bf16)


def silu_pair(v):
    s = 1.0 / (1.0 + jnp.exp(-v))
    return v * s, s * (1.0 + v * (1.0 - s))


def norm_parts(x):
    mean = jnp.mean(x, axis=-1, keepdims=True)
    cen = x - mean
    inv = lax.rsqrt(jnp.mean(cen * cen, axis=-1, keepdims=True) + norm_floor)
    return cen * inv, inv


def norm_back(d_norm, normed, inv):
    a = jnp.mean(d_norm, axis=-1, keepdims=True)
    b = jnp.mean(d_norm * normed, axis=-1, keepdims=True)
    return inv * (d_norm - a - normed * b)


def dot(a, b):
    return jnp.dot(a, b, preferred_element_type=f32)


def dot_nt(a, b):
    return lax.dot_general(a, b, (((1,), (1,)), ((), ())), preferred_element_type=f32)


def dot_tn(a, b):
    return lax.dot_general(a, b, (((0,), (0,)), ((), ())), preferred_element_type=f32)


def flip(x, bit, axis="fsdp"):
    size = lax.axis_size(axis)
    return lax.ppermute(x, axis, [(i, i ^ bit) for i in range(size)])


def rep_gather(x):
    size = lax.axis_size("rep")
    me = lax.axis_index("rep")
    parts = jnp.stack([x] + [flip(x, k, "rep") for k in range(1, size)])
    return jnp.stack([lax.dynamic_index_in_dim(parts, me ^ j, 0, keepdims=False) for j in range(size)])


def rep_sum(x16):
    size = lax.axis_size("rep")
    parts = [x16.astype(f32)] + [flip(x16, k, "rep").astype(f32) for k in range(1, size)]
    while len(parts) > 1:
        parts = [parts[i] + parts[i + 1] for i in range(0, len(parts), 2)]
    return parts[0]


def sum_scatter(grad):
    size = lax.axis_size("fsdp")
    rows = grad.shape[0] // size
    if size != 8:
        return lax.psum_scatter(grad.astype(f32), "fsdp", scatter_dimension=0, tiled=True)
    me = lax.axis_index("fsdp")
    core, chip = me & 1, me >> 1
    g = grad.reshape(4, 2, rows, -1)
    keep = lax.dynamic_index_in_dim(g, core, 1, keepdims=False)
    send = lax.dynamic_index_in_dim(g, 1 - core, 1, keepdims=False).astype(bf16)
    both = keep.astype(f32) + flip(send, 1).astype(f32)
    own = lax.dynamic_index_in_dim(both, chip, 0, keepdims=False)
    low = both.astype(bf16)
    total = own
    for k in range(1, 4):
        total = total + flip(lax.dynamic_index_in_dim(low, chip ^ k, 0, keepdims=False), 2 * k).astype(f32)
    return total


def gather_rows(x):
    return lax.all_gather(x, "fsdp", axis=0, tiled=True)


def modulated(normed, mod, slot):
    return normed * (1.0 + mod[:, None, (slot + 1) * D : (slot + 2) * D]) + mod[:, None, slot * D : (slot + 1) * D]


def per_device(
    latents,
    noise,
    timesteps,
    labels,
    patch_state,
    time1_w,
    time1_f,
    time2_w,
    time2_f,
    table_w,
    table_f,
    mod_w,
    mod_f,
    qkv_w,
    qkv_f,
    proj_w,
    proj_f,
    fc1_w,
    fc1_f,
    fc2_w,
    fc2_f,
    out_state,
):
    reps, parts = lax.axis_size("rep"), lax.axis_size("fsdp")
    position = lax.axis_index("fsdp")
    masters = (patch_state[0], time1_w, time2_w, table_w, mod_w, qkv_w, proj_w, fc1_w, fc2_w, out_state[0])
    images = latents.shape[0] * latents.shape[1]
    latents = latents.reshape(images, TOK_IMG, PIN)
    noise = noise.reshape(images, TOK_IMG, PIN)
    tsteps = timesteps.reshape(images)
    labels = labels.reshape(images)
    own_d = D // parts
    own_t = TFREQ // parts

    info = jnp.stack([tsteps // 32, tsteps % 32, labels // 32, labels % 32]).reshape(1, 4 * images)
    info_row = jnp.pad(info.astype(bf16), ((0, 0), (0, D - 4 * images)))
    bundle = jnp.concatenate([time1_w.astype(bf16), time2_w.astype(bf16), info_row], axis=0)
    bundle = gather_rows(bundle).reshape(parts, own_t + own_d + 1, D)
    w_time1 = bundle[:, :own_t].reshape(TFREQ, D)
    w_time2 = bundle[:, own_t : own_t + own_d].reshape(D, D)
    info_rep = bundle[:, own_t + own_d, : 4 * images]

    head = jnp.pad(
        jnp.concatenate([patch_state[0].T, out_state[0]], axis=1), ((0, 0), (0, 128 - PIN - POUT))
    )
    w_rows = gather_rows(jnp.concatenate([qkv_w, proj_w, fc1_w, head], axis=1).astype(bf16))
    w_fc2 = gather_rows(fc2_w.astype(bf16))
    w_qkv = w_rows[:, : 3 * D]
    w_proj = w_rows[:, 3 * D : 4 * D]
    w_fc1 = w_rows[:, 4 * D : 4 * D + FF]
    w_patch_t = w_rows[:, 4 * D + FF : 4 * D + FF + PIN]
    w_out = w_rows[:, 4 * D + FF + PIN : 4 * D + FF + PIN + POUT]

    info_all = rep_gather(info_rep).reshape(reps * parts, 4, images).astype(jnp.int32)
    w_mod16 = mod_w.astype(bf16)
    w_table16 = table_w.astype(bf16)
    times = jnp.asarray(time_table(), bf16)

    def condition_path(info_any):
        ts = (info_any[:, 0] * 32 + info_any[:, 1]).reshape(-1)
        lab = (info_any[:, 2] * 32 + info_any[:, 3]).reshape(-1)
        feats16 = dot(pick(ts, STEPS), times).astype(bf16)
        time_act, time_slope = silu_pair(dot(feats16, w_time1))
        time_act16 = time_act.astype(bf16)
        time_emb = dot(time_act16, w_time2)
        own_emb = lax.dynamic_slice(time_emb, (0, position * own_d), (time_emb.shape[0], own_d))
        picks = pick(lab, CLASSES)
        cond_act, cond_slope = silu_pair(own_emb + dot(picks, w_table16))
        return feats16, time_act16, time_slope, picks, cond_act.astype(bf16), cond_slope

    info_here = info_rep.reshape(parts, 4, images).astype(jnp.int32)
    cond_here = condition_path(info_here)[4]
    shares = dot(cond_here, w_mod16).reshape(parts, images * 8 * D)
    mod = jnp.sum(lax.all_to_all(shares, "fsdp", 0, 0, tiled=True).reshape(parts, images, 8 * D), axis=0)

    plan = jnp.asarray(plan_table())
    consts = jnp.stack([lax.dynamic_index_in_dim(plan, tsteps[i], 0, keepdims=False) for i in range(images)])
    keep_s, keep_n, log_beta, post_log, coef = (consts[:, i][:, None, None] for i in range(5))

    def tok(x):
        return x.reshape(images * TOK_IMG, -1)

    def img(x):
        return x.reshape(images, TOK_IMG, -1)

    noisy16 = tok((keep_s * latents + keep_n * noise).astype(bf16))
    hidden0 = img(dot_nt(noisy16, w_patch_t)) + jnp.asarray(place_table())[None]
    norm0, inv0 = norm_parts(hidden0)
    attn16 = modulated(norm0, mod, 0).astype(bf16)
    qkv16 = dot(tok(attn16), w_qkv).astype(bf16)
    heads = qkv16.reshape(images, TOK_IMG, 3, HEADS, HEAD_DIM)
    q, k, v = (heads[:, :, i].transpose(0, 2, 1, 3) for i in range(3))
    scores = jnp.einsum("nhqd,nhkd->nhqk", q, k, preferred_element_type=f32) * 0.125
    prob = jnp.exp(scores - jnp.max(scores, axis=-1, keepdims=True))
    prob = prob / jnp.sum(prob, axis=-1, keepdims=True)
    prob16 = prob.astype(bf16)
    mixture16 = (
        jnp.einsum("nhqk,nhkd->nhqd", prob16, v, preferred_element_type=f32)
        .transpose(0, 2, 1, 3)
        .reshape(images * TOK_IMG, D)
        .astype(bf16)
    )
    gate1 = mod[:, None, 2 * D : 3 * D]
    gate2 = mod[:, None, 5 * D : 6 * D]
    branch = img(dot(mixture16, w_proj))
    hidden1 = hidden0 + gate1 * branch
    norm1, inv1 = norm_parts(hidden1)
    mlp16 = modulated(norm1, mod, 3).astype(bf16)
    inner = dot(tok(mlp16), w_fc1)
    cube = inner * inner
    bend = jnp.tanh(math.sqrt(2.0 / math.pi) * inner * (1.0 + 0.044715 * cube))
    act16 = (0.5 * inner * (1.0 + bend)).astype(bf16)
    slope = 0.5 * (1.0 + bend) + 0.5 * inner * (1.0 - bend * bend) * math.sqrt(2.0 / math.pi) * (
        1.0 + 3 * 0.044715 * cube
    )
    outer = img(dot(act16, w_fc2))
    hidden2 = hidden1 + gate2 * outer
    norm2, inv2 = norm_parts(hidden2)
    fin16 = modulated(norm2, mod, 6).astype(bf16)
    output = img(dot(tok(fin16), w_out))

    miss = output[..., :PIN] - noise
    mixing = (output[..., PIN:] + 1.0) * 0.5
    log_var = mixing * log_beta + (1.0 - mixing) * post_log
    ratio = jnp.exp(post_log - log_var)
    weigh = coef * jnp.exp(-log_var)
    square = miss * miss
    loss_part = jnp.sum(square + 0.5 * (-1.0 + log_var - post_log + ratio + weigh * square)) / (TOK_IMG * PIN)
    share = 1.0 / (TOK_IMG * PIN)
    d_guess = share * miss * (2.0 + weigh)
    d_logvar = share * 0.5 * (1.0 - ratio - weigh * square)
    d_mixed = d_logvar * (log_beta - post_log) * 0.5
    d_output16 = tok(jnp.concatenate([d_guess, d_mixed], axis=-1)).astype(bf16)

    g_out = dot_tn(tok(fin16), d_output16)
    d_fin = img(dot_nt(d_output16, w_out))
    d_off3 = jnp.sum(d_fin, axis=1)
    d_str3 = jnp.sum(d_fin * norm2, axis=1)
    d_h2 = norm_back(d_fin * (1.0 + mod[:, None, 7 * D :]), norm2, inv2)
    d_gate2 = jnp.sum(d_h2 * outer, axis=1)
    d_outer16 = tok((gate2 * d_h2).astype(bf16))
    g_fc2 = dot_tn(act16, d_outer16)
    d_inner16 = (dot_nt(d_outer16, w_fc2) * slope).astype(bf16)
    g_fc1 = dot_tn(tok(mlp16), d_inner16)
    d_mlp = img(dot_nt(d_inner16, w_fc1))
    d_off2 = jnp.sum(d_mlp, axis=1)
    d_str2 = jnp.sum(d_mlp * norm1, axis=1)
    d_h1 = d_h2 + norm_back(d_mlp * (1.0 + mod[:, None, 4 * D : 5 * D]), norm1, inv1)
    d_gate1 = jnp.sum(d_h1 * branch, axis=1)
    d_branch16 = tok((gate1 * d_h1).astype(bf16))
    g_proj = dot_tn(mixture16, d_branch16)
    d_mix16 = dot_nt(d_branch16, w_proj).astype(bf16)
    d_mix = d_mix16.reshape(images, TOK_IMG, HEADS, HEAD_DIM).transpose(0, 2, 1, 3)
    d_v = jnp.einsum("nhqk,nhqd->nhkd", prob16, d_mix, preferred_element_type=f32)
    d_prob = jnp.einsum("nhqd,nhkd->nhqk", d_mix, v, preferred_element_type=f32)
    d_scores16 = (prob * (d_prob - jnp.sum(d_prob * prob, axis=-1, keepdims=True))).astype(bf16)
    d_q = jnp.einsum("nhqk,nhkd->nhqd", d_scores16, k, preferred_element_type=f32) * 0.125
    d_k = jnp.einsum("nhqk,nhqd->nhkd", d_scores16, q, preferred_element_type=f32) * 0.125
    d_qkv16 = (
        jnp.stack([d_q, d_k, d_v]).transpose(1, 3, 0, 2, 4).reshape(images * TOK_IMG, 3 * D).astype(bf16)
    )
    g_qkv = dot_tn(tok(attn16), d_qkv16)
    d_attn = img(dot_nt(d_qkv16, w_qkv))
    d_off1 = jnp.sum(d_attn, axis=1)
    d_str1 = jnp.sum(d_attn * norm0, axis=1)
    d_h0 = d_h1 + norm_back(d_attn * (1.0 + mod[:, None, D : 2 * D]), norm0, inv0)
    g_patch_t = dot_tn(tok(d_h0.astype(bf16)), noisy16)

    d_mod16 = jnp.concatenate([d_off1, d_str1, d_gate1, d_off2, d_str2, d_gate2, d_off3, d_str3], axis=1).astype(bf16)
    d_mod_all = rep_gather(d_mod16).reshape(1, -1)
    d_mod_all = gather_rows(d_mod_all).reshape(parts, reps, images, 8 * D)
    d_mod_all = d_mod_all.transpose(1, 0, 2, 3).reshape(reps * parts * images, 8 * D)
    feats16, time_act16, time_slope, picks, cond16, cond_slope = condition_path(info_all)
    d_cond = dot_nt(d_mod_all, w_mod16) * cond_slope
    g_mod = dot_tn(cond16, d_mod_all)
    g_table = lax.dot_general(
        picks.astype(f32), d_cond, (((0,), (0,)), ((), ())), precision=lax.Precision.HIGHEST
    )
    d_time16 = lax.all_gather(d_cond.astype(bf16), "fsdp", axis=0)
    d_time16 = d_time16.transpose(1, 0, 2).reshape(-1, D)
    own_act16 = lax.dynamic_slice(time_act16, (0, position * own_d), (time_act16.shape[0], own_d))
    g_time2 = dot_tn(own_act16, d_time16)
    d_hid16 = (dot_nt(d_time16, w_time2) * time_slope).astype(bf16)
    own_feat16 = lax.dynamic_slice(feats16, (0, position * own_t), (feats16.shape[0], own_t))
    g_time1 = dot_tn(own_feat16, d_hid16)

    g_tail = sum_scatter(jnp.concatenate([g_qkv, g_patch_t, g_out, jnp.zeros((D, 128 - PIN - POUT), f32)], axis=1))
    g_mid = sum_scatter(jnp.concatenate([g_fc1, g_proj], axis=1))
    g_big = sum_scatter(g_fc2)
    g_fc2 = rep_sum(g_big.astype(bf16))
    g_mid = rep_sum(g_mid.astype(bf16))
    g_tail = rep_sum(g_tail.astype(bf16))
    grads = (
        g_tail[:, 3 * D : 3 * D + PIN].T,
        g_time1,
        g_time2,
        g_table,
        g_mod,
        g_tail[:, : 3 * D],
        g_mid[:, FF:],
        g_mid[:, :FF],
        g_fc2,
        g_tail[:, 3 * D + PIN : 3 * D + PIN + POUT],
    )
    loss_part = lax.psum(loss_part, "rep")
    olds = (time1_f, time2_f, table_f, mod_f, qkv_f, proj_f, fc1_f, fc2_f)
    dims = (0, 0, 1, 0, 0, 0, 0, 0)

    packs = []
    for slot in range(8):
        grad, dim = grads[slot + 1], dims[slot]
        squares = grad * grad + grad_floor
        near = jnp.sum(squares, axis=1 - dim)
        far = jnp.sum(squares, axis=dim)
        spread = lax.dynamic_update_slice(
            jnp.zeros((near.shape[0] * parts,), f32), near / far.shape[0], (position * near.shape[0],)
        )
        far = far / (near.shape[0] * parts)
        packs.append(jnp.concatenate([spread, far] if dim == 0 else [far, spread]))
    tail = jnp.stack([jnp.sum(m * m) for m in masters] + [loss_part])
    lengths = [pack.shape[0] for pack in packs]
    totals = lax.psum(jnp.concatenate(packs + [tail]), "fsdp")
    fresh = []
    start = 0
    for length in lengths:
        fresh.append(totals[start : start + length])
        start += length
    square_tot = totals[start : start + 10]
    loss = totals[start + 10] / (images * reps * parts)

    updates, counts = [], []
    plain = []
    for slot in range(10):
        grad = grads[slot]
        if slot in (0, 9):
            state = patch_state if slot == 0 else out_state
            moment = decay_rate * state[1] + (1.0 - decay_rate) * (grad * grad + grad_floor)
            plain.append(moment)
            updates.append(grad * lax.rsqrt(moment))
            counts.append(grad.size * parts)
            continue
        dim = dims[slot - 1]
        renewed = decay_rate * olds[slot - 1] + (1.0 - decay_rate) * fresh[slot - 1]
        rows = grad.shape[0] * (parts if dim == 0 else 1)
        row, col = renewed[:rows], renewed[rows:]
        mean_row = jnp.mean(row)
        if dim == 0:
            row = lax.dynamic_slice(row, (position * grad.shape[0],), (grad.shape[0],))
        else:
            col = lax.dynamic_slice(col, (position * grad.shape[1],), (grad.shape[1],))
        updates.append(grad * lax.rsqrt(row[:, None] * col[None, :] / mean_row))
        counts.append(grad.size * parts)
    update_tot = lax.psum(jnp.stack([jnp.sum(u * u) for u in updates]), "fsdp")
    sizes = np.asarray(counts, np.float32)
    size_rms = jnp.sqrt(update_tot / sizes)
    factor = step_rate * jnp.sqrt(square_tot / sizes) / jnp.maximum(1.0, size_rms / clip_level)
    new = [masters[s] - factor[s] * updates[s] for s in range(10)]
    result = [jnp.stack([new[0], plain[0]])]
    for slot in range(8):
        result += [new[slot + 1], fresh[slot]]
    return tuple(result) + (jnp.stack([new[9], plain[1]]), loss, size_rms)


def solution(mesh):
    images = P(None, ("rep", "fsdp"), None, None)
    singles = P(None, ("rep", "fsdp"))
    rows, cols = P("fsdp", None), P(None, "fsdp")
    placed = (images, images, singles, singles, P(None, None, "fsdp"))
    placed += (rows, P(), rows, P(), cols, P()) + (rows, P()) * 5 + (P(None, "fsdp", None),)
    results = (P(None, None, "fsdp"), rows, P(), rows, P(), cols, P()) + (rows, P()) * 5
    results += (P(None, "fsdp", None), P(), P())
    return jax.shard_map(per_device, mesh=mesh, in_specs=placed, out_specs=results, check_vma=False)
```

```python
import math

import jax
import jax.numpy as jnp
import numpy as np
from jax import lax
from jax.experimental import pallas as pl
from jax.experimental.pallas import tpu as pltpu
from jax.sharding import PartitionSpec as P

D = 384
HEADS = 6
HEAD_DIM = 64
FF = 1536
TFREQ = 256
GRID = 16
PIN = 16
POUT = 32
CLASSES = 1001
STEPS = 1000
TOK_IMG = 256

decay_rate = 0.5
clip_level = 1.0
step_rate = 0.5
grad_floor = 1e-30
norm_floor = 1e-06
f32 = jnp.float32
bf16 = jnp.bfloat16


def plan_table():
    s = np.arange(STEPS, dtype=np.float64)
    beta = 1e-4 + (0.02 - 1e-4) * s / (STEPS - 1)
    lbar = np.cumsum(np.log1p(-beta))
    lprev = np.concatenate([[0.0], lbar[:-1]])
    post = beta * -np.expm1(lprev) / -np.expm1(lbar)
    post[0] = post[1]
    remain = -np.expm1(lbar)
    coef = beta * beta / ((1.0 - beta) * remain)
    rows = [np.exp(0.5 * lbar), np.sqrt(remain), np.log(beta), np.log(post), coef]
    return np.stack(rows + [np.zeros(STEPS)] * 3, axis=1).astype(np.float32)


def time_table():
    half = TFREQ // 2
    freq = np.exp(np.float32(-math.log(10000.0)) * np.arange(half, dtype=np.float32) / np.float32(half)).astype(np.float32)
    angles = np.arange(STEPS, dtype=np.float32)[:, None] * freq[None, :]
    wide = angles.astype(np.float64)
    return np.concatenate([np.cos(wide), np.sin(wide)], axis=1).astype(np.float32)


def place_table():
    quarter = D // 4
    om = np.exp(np.float32(-math.log(10000.0)) * np.arange(quarter, dtype=np.float32) / np.float32(quarter)).astype(np.float32)
    n = np.arange(TOK_IMG)
    row = ((n // GRID).astype(np.float32)[:, None] * om[None, :]).astype(np.float64)
    col = ((n % GRID).astype(np.float32)[:, None] * om[None, :]).astype(np.float64)
    return np.concatenate([np.sin(row), np.cos(row), np.sin(col), np.cos(col)], axis=1).astype(np.float32)


def pick(index, count):
    return (index[:, None] == jnp.arange(count, dtype=jnp.int32)[None, :]).astype(bf16)


def silu_pair(v):
    s = 1.0 / (1.0 + jnp.exp(-v))
    return v * s, s * (1.0 + v * (1.0 - s))


def norm_parts(x):
    mean = jnp.mean(x, axis=-1, keepdims=True)
    cen = x - mean
    inv = lax.rsqrt(jnp.mean(cen * cen, axis=-1, keepdims=True) + norm_floor)
    return cen * inv, inv


def norm_back(d_norm, normed, inv):
    a = jnp.mean(d_norm, axis=-1, keepdims=True)
    b = jnp.mean(d_norm * normed, axis=-1, keepdims=True)
    return inv * (d_norm - a - normed * b)


def dot(a, b):
    return jnp.dot(a, b, preferred_element_type=f32)


def dot_nt(a, b):
    return lax.dot_general(a, b, (((1,), (1,)), ((), ())), preferred_element_type=f32)


def dot_tn(a, b):
    return lax.dot_general(a, b, (((0,), (0,)), ((), ())), preferred_element_type=f32)


def flip(x, bit, axis="fsdp"):
    size = lax.axis_size(axis)
    return lax.ppermute(x, axis, [(i, i ^ bit) for i in range(size)])


def rep_gather(x):
    size = lax.axis_size("rep")
    me = lax.axis_index("rep")
    parts = jnp.stack([x] + [flip(x, k, "rep") for k in range(1, size)])
    return jnp.stack([lax.dynamic_index_in_dim(parts, me ^ j, 0, keepdims=False) for j in range(size)])


def rep_sum(x16):
    size = lax.axis_size("rep")
    parts = [x16.astype(f32)] + [flip(x16, k, "rep").astype(f32) for k in range(1, size)]
    while len(parts) > 1:
        parts = [parts[i] + parts[i + 1] for i in range(0, len(parts), 2)]
    return parts[0]


def sum_scatter(grad):
    return lax.psum_scatter(grad, "fsdp", scatter_dimension=0, tiled=True)


def gather_rows(x):
    return lax.all_gather(x, "fsdp", axis=0, tiled=True)


def lane_half(shape, which):
    lane = lax.broadcasted_iota(jnp.int32, shape, 1)
    return (lane < HEAD_DIM) if which == 0 else (lane >= HEAD_DIM)


FLOPS_US = 1_150_000_000


def kernel_call(body, outs, operands, micros, scratch=(), places=None, after=(), room=16):
    vmem = pl.BlockSpec(memory_space=pltpu.VMEM)
    smem = pl.BlockSpec(memory_space=pltpu.SMEM)
    places = places or "v" * len(operands)
    count = len(operands)

    def run(*refs):
        body(*refs[:count], *refs[count + len(after) :])

    return pl.pallas_call(
        run,
        out_shape=[jax.ShapeDtypeStruct(s, t) for s, t in outs],
        in_specs=[{"s": smem, "v": vmem, "h": pl.BlockSpec(memory_space=pltpu.HBM)}[p] for p in places] + [pl.BlockSpec(memory_space=pl.ANY)] * len(after),
        out_specs=[vmem] * len(outs),
        scratch_shapes=list(scratch),
        compiler_params=pltpu.CompilerParams(vmem_limit_bytes=room * 2**20),
        cost_estimate=pl.CostEstimate(flops=int(micros * FLOPS_US), bytes_accessed=1_000_000, transcendentals=0),
    )(*operands, *after)


HEAD = PIN + POUT
CAST_ROOM = 48
INFO = 80
BUNDLE = 96
TAIL = 3 * D + 128
SENT = TAIL + D + 2 * FF


def piece_owner(at, n):
    return jnp.bitwise_xor(at[0], 2 * (n % 4) + n // 4)


def attention_forward(tsteps, lat, noi, plan, grid, weights, shares, place, after=()):
    images = lat.shape[0]
    fast = len(weights) == 8

    def body(ts, at, lat_r, noi_r, plan_r, grid_r, share_r, *refs):
        if fast:
            wq_r, head_r, head_s = refs[8], refs[9], refs[-1]
            for n in range(8):
                owner = piece_owner(at, n)
                rows = pl.ds(pl.multiple_of(owner * 48, 48), 48)
                wq_r[rows, :] = refs[n][:, 0 : 3 * D]
                head_s[owner] = refs[n][:, 3 * D : 3 * D + 48]
            for p in range(8):
                head_r[:, p * 48 : (p + 1) * 48] = head_s[p]
            refs = refs[10:-1]
        else:
            wq_r, head_r = refs[:2]
            refs = refs[2:]
        mod_r, con_r, noisy_r, h0_r, attn_r, qkv_r, total_r, mix_r = refs
        total = share_r[0]
        for p in range(1, share_r.shape[0]):
            total = total + share_r[p]
        width = total.shape[1]
        for n in range(8):
            i, col = divmod(n * width, 8 * D)
            mod_r[i : i + 1, col : col + width] = total[n : n + 1]
        for i in range(images):
            row = plan_r[pl.ds(ts[i], 1), :]
            con_r[i : i + 1, :] = row
            noisy = (row[:, 0:1] * lat_r[i] + row[:, 1:2] * noi_r[i]).astype(bf16)
            noisy_r[i] = noisy
            h0 = dot_tn(noisy, head_r[0:PIN, :]) + grid_r[...]
            h0_r[i] = h0
            norm, _ = norm_parts(h0)
            attn = (norm * (1.0 + mod_r[i : i + 1, D : 2 * D]) + mod_r[i : i + 1, 0:D]).astype(bf16)
            attn_r[i] = attn
            for part in range(3):
                qkv_r[i, :, part * D : (part + 1) * D] = dot(attn, wq_r[:, part * D : (part + 1) * D]).astype(bf16)
        lane = lax.broadcasted_iota(jnp.int32, (TOK_IMG, 128), 1)
        logs = [jnp.zeros((TOK_IMG, 128), f32)] * images
        for pair in range(HEADS // 2):
            for i in range(images):
                q = qkv_r[i, :, pair * 128 : pair * 128 + 128]
                k = qkv_r[i, :, D + pair * 128 : D + pair * 128 + 128]
                v = qkv_r[i, :, 2 * D + pair * 128 : 2 * D + pair * 128 + 128]
                mixed = None
                for half in range(2):
                    own = lane_half(q.shape, half)
                    zero = jnp.zeros_like(q)
                    s = dot_nt(jnp.where(own, q, zero), k) * 0.125
                    top = jnp.max(s, axis=-1, keepdims=True)
                    p = jnp.exp(s - top)
                    total = jnp.sum(p, axis=-1, keepdims=True)
                    p = p * (1.0 / total)
                    logs[i] = jnp.where(lane == pair * 2 + half, top + jnp.log(total), logs[i])
                    o = dot(p.astype(bf16), jnp.where(own, v, zero))
                    mixed = o if mixed is None else mixed + o
                mix_r[i, :, pair * 128 : pair * 128 + 128] = mixed.astype(bf16)
        for i in range(images):
            total_r[i] = logs[i]

    outs = [
        ((images, 8 * D), f32),
        ((images, 8), f32),
        ((images, PIN, TOK_IMG), bf16),
        ((images, TOK_IMG, D), f32),
        ((images, TOK_IMG, D), bf16),
        ((images, TOK_IMG, 3 * D), bf16),
        ((images, TOK_IMG, 128), f32),
        ((images, TOK_IMG, D), bf16),
    ]
    scratch = []
    if fast:
        outs = [((D, 3 * D), bf16), ((HEAD, D), bf16)] + outs
        scratch = [pltpu.VMEM((8, HEAD, 48), bf16)]
    ops = (tsteps, place, lat, noi, plan, grid, shares, *weights)
    return kernel_call(
        body, outs, ops, 8, scratch=scratch, places="ss" + "v" * (len(ops) - 2), after=after
    )


BLOCK = 384


def mlp_pass(noi, con, mod, h0_all, mix_all, head, weights, place, after=()):
    images = noi.shape[0]
    bend_scale = math.sqrt(2.0 / math.pi)
    share = 1.0 / (TOK_IMG * PIN)

    fast = len(weights) == 8

    def body(at, noi_r, con_r, mod_r, h0_r, mix_r, head_r, *refs):
        if fast:
            wp_r, w1_r, w2_r = refs[-3:]
            for n in range(8):
                owner = piece_owner(at, n)
                rows = pl.ds(pl.multiple_of(owner * 48, 48), 48)
                wp_r[rows, :] = refs[n][:, TAIL : TAIL + D]
                w1_r[rows, :] = refs[n][:, TAIL + D : TAIL + D + FF]
                for b in range(4):
                    w2_r[pl.ds(pl.multiple_of(owner * 192 + b * 48, 48), 48), :] = refs[n][:, TAIL + D + FF + b * D : TAIL + D + FF + (b + 1) * D]
            refs = refs[8:-3]
        else:
            wp_r, w1_r, w2_r = refs[:3]
            refs = refs[3:]
        g_refs, refs = refs[: 2 if fast else 3], refs[2 if fast else 3 :]
        glast_r, dmix_r, dh1_r, dmod_r, loss_r, mlp_r, act_r, dinner_r, douter_r, dbr_r, slope_r = refs
        g_last = None
        wo = head_r[PIN:HEAD, :]
        losses = jnp.zeros((1, 1), f32)
        dmod_r[:, 0 : 2 * D] = jnp.zeros((images, 2 * D), f32)
        for i in range(images):
            def m(slot):
                return mod_r[i : i + 1, slot * D : (slot + 1) * D]

            def put(slot, value):
                dmod_r[i : i + 1, slot * D : (slot + 1) * D] = jnp.sum(value, axis=0, keepdims=True)

            branch = dot(mix_r[i], wp_r[...])
            h1 = h0_r[i] + m(2) * branch
            norm1, inv1 = norm_parts(h1)
            mlp = (norm1 * (1.0 + m(4)) + m(3)).astype(bf16)
            tokens = slice(i * TOK_IMG, (i + 1) * TOK_IMG)
            mlp_r[tokens, :] = mlp
            outer = None
            for b in range(FF // BLOCK):
                cols = slice(b * BLOCK, (b + 1) * BLOCK)
                x = dot(mlp, w1_r[:, cols])
                sq = x * x
                t = jnp.tanh(bend_scale * x * (1.0 + 0.044715 * sq))
                hx = 0.5 * x
                act = (hx * (1.0 + t)).astype(bf16)
                act_r[tokens, cols] = act
                slope_r[:, cols] = 0.5 * (1.0 + t) + hx * (1.0 - t * t) * (bend_scale + (3 * 0.044715 * bend_scale) * sq)
                part = dot(act, w2_r[cols, :])
                outer = part if outer is None else outer + part
            h2 = h1 + m(5) * outer
            norm2, inv2 = norm_parts(h2)
            fin = (norm2 * (1.0 + m(7)) + m(6)).astype(bf16)
            out = dot_nt(wo, fin)
            log_beta, post_log, coef = (con_r[i : i + 1, n : n + 1] for n in (2, 3, 4))
            miss = out[:PIN] - noi_r[i]
            mixing = (out[PIN:] + 1.0) * 0.5
            log_var = mixing * log_beta + (1.0 - mixing) * post_log
            ratio = jnp.exp(post_log - log_var)
            square = miss * miss
            weigh = coef * jnp.exp(-log_var)
            terms = square + 0.5 * (-1.0 + log_var - post_log + ratio + weigh * square)
            losses += share * jnp.sum(jnp.sum(terms, axis=0, keepdims=True), axis=1, keepdims=True)
            d_guess = share * miss * (2.0 + weigh)
            d_mixed = (share * 0.25) * (1.0 - ratio - weigh * square) * (log_beta - post_log)
            d_out = jnp.concatenate([d_guess, d_mixed], axis=0).astype(bf16)
            piece = dot(d_out, fin)
            g_last = piece if g_last is None else g_last + piece
            d_fin = dot_tn(d_out, wo)
            put(6, d_fin)
            put(7, d_fin * norm2)
            d_h2 = norm_back(d_fin * (1.0 + m(7)), norm2, inv2)
            put(5, d_h2 * outer)
            d_outer = (m(5) * d_h2).astype(bf16)
            douter_r[tokens, :] = d_outer
            d_mlp = None
            for b in range(FF // BLOCK):
                cols = slice(b * BLOCK, (b + 1) * BLOCK)
                d_in = (dot_nt(d_outer, w2_r[cols, :]) * slope_r[:, cols]).astype(bf16)
                dinner_r[tokens, cols] = d_in
                part = dot_nt(d_in, w1_r[:, cols])
                d_mlp = part if d_mlp is None else d_mlp + part
            put(3, d_mlp)
            put(4, d_mlp * norm1)
            d_h1 = d_h2 + norm_back(d_mlp * (1.0 + m(4)), norm1, inv1)
            dh1_r[i] = d_h1
            put(2, d_h1 * branch)
            d_br = (m(2) * d_h1).astype(bf16)
            dbr_r[tokens, :] = d_br
            dmix_r[i] = dot_nt(d_br, wp_r[...]).astype(bf16)
        loss_r[...] = jnp.broadcast_to(losses, loss_r.shape)
        glast_r[...] = g_last
        mix = jnp.concatenate([mix_r[i] for i in range(images)], axis=0)
        if not fast:
            g_refs[0][...] = dot_tn(mix, dbr_r[...])
        else:
            deal_rows(*g_refs, dot_tn(mix, dbr_r[...]), at[1], 0)
        for b in range(FF // BLOCK):
            cols = slice(b * BLOCK, (b + 1) * BLOCK)
            g_in = dot_tn(mlp_r[...], dinner_r[:, cols])
            g_out = dot_tn(act_r[:, cols], douter_r[...])
            if not fast:
                g_refs[1][:, cols] = g_in
                g_refs[2][cols, :] = g_out
                continue
            deal_rows(*g_refs, g_in, at[1], D + b * BLOCK)
            deal(*g_refs, g_out[0:192], g_out[192:384], at[1], b, D + FF, 4)

    if fast:
        outs = [((4, 48, D + 2 * FF), f32), ((4, 48, D + 2 * FF), bf16)]
    else:
        outs = [((D, D), f32), ((D, FF), f32), ((FF, D), f32)]
    outs += [
        ((POUT, D), f32),
        ((images, TOK_IMG, D), bf16),
        ((images, TOK_IMG, D), f32),
        ((images, 8 * D), f32),
        ((8, 128), f32),
    ]
    ops = (place, noi, con, mod, h0_all, mix_all, head, *weights)
    many = images * TOK_IMG
    scratch = [pltpu.VMEM((many, n), bf16) for n in (D, FF, FF, D, D)] + [pltpu.VMEM((TOK_IMG, FF), f32)]
    if fast:
        scratch += [pltpu.VMEM(shape, bf16) for shape in ((D, D), (D, FF), (FF, D))]
    return kernel_call(body, outs, ops, 13, scratch=scratch, places="s" + "v" * (len(ops) - 1), after=after, room=32)


def deal(keep_r, send_r, left, right, core, chip, lanes, blocks=1):
    rows, width = left.shape[0] // blocks, left.shape[1]
    kept = jnp.where(core == 0, left, right)
    sent = jnp.where(core == 0, right, left).astype(bf16)
    for b in range(blocks):
        cols = slice(lanes + b * width, lanes + (b + 1) * width)
        keep_r[chip, :, cols] = kept[b * rows : (b + 1) * rows]
        send_r[chip, :, cols] = sent[b * rows : (b + 1) * rows]


def deal_rows(keep_r, send_r, grad, core, lanes):
    for c in range(4):
        deal(keep_r, send_r, grad[c * 96 : c * 96 + 48], grad[c * 96 + 48 : c * 96 + 96], core, c, lanes)


MOD_ROWS, MOD_LANES = 16, 512


def attention_back(mod, h0_all, qkv_all, total_all, dmix_all, dh1_all, dmod_all, w_qkv, loss_tile, info, after=()):
    images = mod.shape[0]

    def body(mod_r, h0_r, qkv_r, total_r, dmix_r, dh1_r, dmod_in, wq_r, loss_r, *refs):
        dqkv_r, dmod_r, dh0_r, line = refs[-4:]
        for pair in range(HEADS // 2):
            at = slice(pair * 128, pair * 128 + 128)
            for i in range(images):
                q = qkv_r[i, :, pair * 128 : pair * 128 + 128]
                k = qkv_r[i, :, D + pair * 128 : D + pair * 128 + 128]
                v = qkv_r[i, :, 2 * D + pair * 128 : 2 * D + pair * 128 + 128]
                do = dmix_r[i, :, at]
                dq = dk = dv = None
                for half in range(2):
                    own = lane_half(q.shape, half)
                    zero = jnp.zeros_like(q)
                    do_h = jnp.where(own, do, zero)
                    q_h = jnp.where(own, q, zero)
                    head = pair * 2 + half
                    p = jnp.exp(dot_nt(q_h, k) * 0.125 - total_r[i, :, head : head + 1])
                    dp = dot_nt(do_h, v)
                    ds = (p * (dp - jnp.sum(dp * p, axis=-1, keepdims=True))).astype(bf16)
                    a = dot(ds, jnp.where(own, k, zero))
                    b = dot_tn(ds, q_h)
                    c = dot_tn(p.astype(bf16), do_h)
                    dq, dk, dv = (a, b, c) if dq is None else (dq + a, dk + b, dv + c)
                rows = slice(i * TOK_IMG, (i + 1) * TOK_IMG)
                for part, value in enumerate((dq * 0.125, dk * 0.125, dv)):
                    dqkv_r[rows, part * D + pair * 128 : part * D + pair * 128 + 128] = value.astype(bf16)
        for i in range(images):
            rows = slice(i * TOK_IMG, (i + 1) * TOK_IMG)
            d_attn = None
            for part in range(3):
                cols = slice(part * D, (part + 1) * D)
                piece = dot_nt(dqkv_r[rows, cols], wq_r[:, cols])
                d_attn = piece if d_attn is None else d_attn + piece
            norm, inv = norm_parts(h0_r[i])
            line[i : i + 1, 0:D] = jnp.sum(d_attn, axis=0, keepdims=True)
            line[i : i + 1, D : 2 * D] = jnp.sum(d_attn * norm, axis=0, keepdims=True)
            line[i : i + 1, 2 * D :] = dmod_in[i : i + 1, 2 * D :]
            dh0_r[i] = (dh1_r[i] + norm_back(d_attn * (1.0 + mod_r[i : i + 1, D : 2 * D]), norm, inv)).astype(bf16)
        if info is not None:
            each = 8 * D // MOD_LANES
            block = [line[i : i + 1, n * MOD_LANES : (n + 1) * MOD_LANES] for i in range(images) for n in range(each)]
            lane = lax.broadcasted_iota(jnp.int32, (1, MOD_LANES), 1)
            loss = loss_r[0:1, 0:1]
            high = loss.astype(bf16).astype(f32)
            mid = (loss - high).astype(bf16).astype(f32)
            low = loss - high - mid
            block.append(jnp.where(lane == 0, high, jnp.where(lane == 1, mid, jnp.where(lane == 2, low, 0.0))))
            told = refs[0][INFO:BUNDLE, :].astype(f32)[0:1]
            block.append(jnp.concatenate([told, jnp.zeros((1, MOD_LANES - D), f32)], axis=1))
            block.append(jnp.zeros((MOD_ROWS - len(block), MOD_LANES), f32))
            dmod_r[...] = jnp.concatenate(block, axis=0).astype(bf16)
        else:
            dmod_r[...] = line[...].astype(bf16)

    outs = [((images * TOK_IMG, 3 * D), bf16)]
    outs += [((images, 8 * D) if info is None else (MOD_ROWS, MOD_LANES), bf16), ((images, TOK_IMG, D), bf16)]
    ops = (mod, h0_all, qkv_all, total_all, dmix_all, dh1_all, dmod_all, w_qkv, loss_tile)
    if info is not None:
        ops += (info,)
    return kernel_call(body, outs, ops, 7, scratch=[pltpu.VMEM((images, 8 * D), f32)], after=after)


def tail_grad(attn_all, dqkv, noisy_all, dh0_all, g_last, place, fast, after=()):
    images = noisy_all.shape[0]

    def body(at, attn_r, dqkv_r, noisy_r, dh0_r, last_r, *refs):
        for part in range(3):
            cols = slice(part * D, (part + 1) * D)
            grad = dot_tn(attn_r[...], dqkv_r[:, cols])
            if fast:
                deal_rows(*refs[:2], grad, at[1], part * D)
            else:
                refs[0][:, cols] = grad
        patch = None
        for i in range(images):
            piece = dot(noisy_r[i], dh0_r[i])
            patch = piece if patch is None else patch + piece
        head = jnp.concatenate([patch, last_r[...]], axis=0)
        if not fast:
            refs[1][...] = head
            return
        none = jnp.zeros((HEAD, 128 - 48), f32)
        for c in range(4):
            left = jnp.concatenate([head[:, c * 96 : c * 96 + 48], none], axis=1)
            right = jnp.concatenate([head[:, c * 96 + 48 : c * 96 + 96], none], axis=1)
            deal(*refs[:2], left, right, at[1], c, 3 * D)

    outs = [((4, 48, TAIL), f32), ((4, 48, TAIL), bf16)] if fast else [((D, 3 * D), f32), ((HEAD, D), f32)]
    ops = (place, attn_all.reshape(-1, D), dqkv, noisy_all, dh0_all, g_last)
    return kernel_call(body, outs, ops, 2, places="s" + "v" * 5, after=after)


def bundle_rows(tsteps, labels, time1_w, time2_w):
    images = tsteps.shape[0]

    def body(ts_h, lab_h, t1_h, t2_h, out_r, ts, lab, t1_r, t2_r, sems):
        copies = [
            pltpu.make_async_copy(a, b, sems.at[n])
            for n, (a, b) in enumerate(((ts_h, ts), (lab_h, lab), (t1_h, t1_r), (t2_h, t2_r)))
        ]
        for copy in copies:
            copy.start()
        for copy in copies:
            copy.wait()
        rows = t1_r.shape[0]
        out_r[0:rows, :] = t1_r[...].astype(bf16)
        out_r[rows:INFO, :] = t2_r[...].astype(bf16)
        lane = lax.broadcasted_iota(jnp.int32, (BUNDLE - INFO, D), 1)
        info = jnp.zeros((BUNDLE - INFO, D), jnp.int32)
        for i in range(images):
            for n, value in enumerate((ts[i] // 32, ts[i] % 32, lab[i] // 32, lab[i] % 32)):
                info = jnp.where(lane == n * images + i, value, info)
        out_r[INFO:BUNDLE, :] = info.astype(f32).astype(bf16)

    ops = (tsteps, labels, time1_w, time2_w)
    scratch = [pltpu.SMEM((images,), jnp.int32)] * 2 + [pltpu.VMEM(a.shape, f32) for a in ops[2:]] + [pltpu.SemaphoreType.DMA((4,))]
    return kernel_call(body, [((BUNDLE, D), bf16)], ops, 1.5, places="hhhh", scratch=scratch)[0]


def cast_weights(patch_state, out_t, time1_w, time2_w, table_t, mod_w, qkv_w, proj_w, fc1_w, fc2_w, after=()):
    def body(pa, ou, t1, t2, ta, mo, qk, pr, f1, f2, w_r, mod16, tab16, sums):
        w_r[:, 0 : 3 * D] = qk[...].astype(bf16)
        head = jnp.concatenate([pa[0], ou[0]], axis=0)
        w_r[:, 3 * D : TAIL] = jnp.concatenate([head, jnp.zeros((HEAD, 128 - 48), f32)], axis=1).astype(bf16)
        w_r[:, TAIL : TAIL + D] = pr[...].astype(bf16)
        w_r[:, TAIL + D : TAIL + D + FF] = f1[...].astype(bf16)
        for b in range(4):
            w_r[:, TAIL + D + FF + b * D : TAIL + D + FF + (b + 1) * D] = f2[b * 48 : (b + 1) * 48, :].astype(bf16)
        mod16[...] = mo[...].astype(bf16)
        tab16[...] = ta[...].astype(bf16)
        lane = lax.broadcasted_iota(jnp.int32, (8, D), 1)
        line = jnp.zeros((8, D), f32)
        for n, m in enumerate((pa[0], t1[...], t2[...], ta[...], mo[...], qk[...], pr[...], f1[...], f2[...], ou[0])):
            line = jnp.where(lane == n, jnp.sum(jnp.sum(m * m, axis=0, keepdims=True), axis=1, keepdims=True), line)
        sums[...] = line

    outs = [((48, SENT), bf16), (mod_w.shape, bf16), (table_t.shape, bf16), ((8, D), f32)]
    ops = (patch_state, out_t, time1_w, time2_w, table_t, mod_w, qkv_w, proj_w, fc1_w, fc2_w)
    return kernel_call(body, outs, ops, 2.5, after=after, room=CAST_ROOM)


def picked(index, count):
    lane = lax.broadcasted_iota(jnp.int32, (index.shape[0], count), 1)
    return (lane == index).astype(f32).astype(bf16)


def one_hot(shape, test):
    row, col = lax.broadcasted_iota(jnp.int32, shape, 0), lax.broadcasted_iota(jnp.int32, shape, 1)
    return test(row, col).astype(f32).astype(bf16)


def condition_body(infos, images, w1, w2, times_r, tab_r, position):
    own_d = tab_r.shape[0]
    ts, lab = [], []
    for i in range(images):
        for whole in infos:
            ts.append((whole[:, i : i + 1] * 32.0 + whole[:, images + i : images + i + 1]).astype(jnp.int32))
            lab.append((whole[:, 2 * images + i : 2 * images + i + 1] * 32.0 + whole[:, 3 * images + i : 3 * images + i + 1]).astype(jnp.int32))
    ts, lab = jnp.concatenate(ts, axis=0), jnp.concatenate(lab, axis=0)
    feats = dot(picked(ts, STEPS), times_r[...]).astype(bf16)
    act, time_slope = silu_pair(dot(feats, w1))
    act = act.astype(bf16)
    own = one_hot((D, own_d), lambda r, c: r == c + position * own_d)
    emb = dot(act, dot(w2, own).astype(bf16))
    picks = picked(lab, CLASSES)
    cond, cond_slope = silu_pair(emb + dot_nt(picks, tab_r[...]))
    return feats, act, time_slope, picks, cond.astype(bf16), cond_slope, own


def modulation_shares(place, pieces, times, tab16, mod16, images):
    parts = 8
    width = images * D

    def body(at, *refs):
        times_r, tab_r, mod_r, out_r, w1_r, w2_r, info_r = refs[8:]
        for n in range(8):
            owner = piece_owner(at, n)
            w1_r[pl.ds(pl.multiple_of(owner * 32, 32), 32), :] = refs[n][0:32, :]
            w2_r[pl.ds(pl.multiple_of(owner * 48, 48), 48), :] = refs[n][32:INFO, :]
            info_r[pl.ds(owner, 1), :] = refs[n][INFO:BUNDLE, 0:128].astype(f32)[0:1]
        cond = condition_body([info_r[...]], images, w1_r[...], w2_r[...], times_r, tab_r, at[0])[4]
        for s in range(8):
            i, col = divmod(s * width, 8 * D)
            value = dot(cond[i * parts : (i + 1) * parts], mod_r[:, col : col + width])
            for p in range(parts):
                out_r[p, s : s + 1, :] = value[p : p + 1]

    outs = [((parts, 8, width), f32), ((TFREQ, D), bf16), ((D, D), bf16)]
    ops = (place, *pieces, times, tab16, mod16)
    return kernel_call(body, outs, ops, 3, places="s" + "v" * 11, scratch=[pltpu.VMEM((parts, 128), f32)])


def condition_back(place, own_mod, oth_mod, w1, w2, times, tab16, mod16, reps, parts, images):
    groups = own_mod.shape[0]
    devices = 2 * groups
    count = devices * images
    own_t, own_d = TFREQ // parts, D // parts
    each = 8 * D // MOD_LANES

    def body(at, own_r, oth_r, w1_r, w2_r, times_r, tab_r, mod_r, gm_r, gt_r, dc_r, loss_r, feat_r, act_r, slope_r, all_s, dmod_s):
        for g in range(groups):
            mine = pl.multiple_of((2 * g + at[1]) * MOD_ROWS, MOD_ROWS)
            its = pl.multiple_of((2 * g + 1 - at[1]) * MOD_ROWS, MOD_ROWS)
            all_s[pl.ds(mine, MOD_ROWS), :] = own_r[g]
            all_s[pl.ds(its, MOD_ROWS), :] = oth_r[g]
        rows = all_s[...]
        take = one_hot((devices, devices * MOD_ROWS), lambda r, c: c == r * MOD_ROWS + images * each + 1)
        infos = dot(take, rows)
        feats, act, time_slope, picks, cond, cond_slope, own = condition_body([infos], images, w1_r[...], w2_r[...], times_r, tab_r, at[0])
        near = one_hot((TFREQ, own_t), lambda r, c: r == c + at[0] * own_t)
        feat_r[...] = dot(feats, near).astype(bf16)
        act_r[...] = dot(act, own).astype(bf16)
        slope_r[...] = time_slope
        for n in range(each):
            take = one_hot((count, devices * MOD_ROWS), lambda r, c: c == (r % devices) * MOD_ROWS + (r // devices) * each + n)
            dmod_s[:, n * MOD_LANES : (n + 1) * MOD_LANES] = dot(take, rows).astype(bf16)
        take = one_hot((8, devices * MOD_ROWS), lambda r, c: c % MOD_ROWS == images * each)
        loss = dot(take, rows)
        loss_r[...] = jnp.broadcast_to(loss[:, 0:1] + loss[:, 1:2] + loss[:, 2:3], loss_r.shape)
        d_mod = dmod_s[...]
        d_cond = dot_nt(d_mod, mod_r[...]) * cond_slope
        wide = jnp.concatenate([d_cond, jnp.zeros((count, 128 - own_d), f32)], axis=1).astype(bf16)
        for p in range(parts):
            dc_r[p] = wide
        gm_r[...] = dot_tn(cond, d_mod)
        high = d_cond.astype(bf16)
        rest = d_cond - high.astype(f32)
        mid = rest.astype(bf16)
        low = (rest - mid.astype(f32)).astype(bf16)
        gt_r[...] = dot_tn(high, picks) + (dot_tn(mid, picks) + dot_tn(low, picks))

    outs = [((own_d, 8 * D), f32), ((own_d, CLASSES), f32), ((parts, count, 128), bf16), ((8, 128), f32)]
    outs += [((count, own_t), bf16), ((count, own_d), bf16), ((count, D), f32)]
    ops = (place, own_mod, oth_mod, w1, w2, times, tab16, mod16)
    scratch = [pltpu.VMEM((devices * MOD_ROWS, MOD_LANES), bf16), pltpu.VMEM((count, 8 * D), bf16)]
    return kernel_call(body, outs, ops, 4, scratch=scratch, places="s" + "v" * 7)


def time_back(d_time, w2, act16, slope, feat16):
    parts, own_d = d_time.shape[0], act16.shape[1]
    own_t = TFREQ // parts

    def body(dt_r, w2_r, act_r, slope_r, feat_r, g1_r, g2_r):
        d_all = jnp.concatenate([dt_r[p, :, 0:own_d].astype(f32) for p in range(parts)], axis=1).astype(bf16)
        g2_r[...] = dot_tn(act_r[...], d_all)
        d_hid = (dot_nt(d_all, w2_r[...]) * slope_r[...]).astype(bf16)
        g1_r[...] = dot_tn(feat_r[...], d_hid)

    outs = [((own_t, D), f32), ((own_d, D), f32)]
    return kernel_call(body, outs, (d_time, w2, act16, slope, feat16), 2)


FAR = {"time1": (0, 1), "time2": (1, 1), "mod": (2, 8), "qkv": (10, 3), "proj": (13, 1), "fc1": (14, 4), "fc2": (18, 1), "table": (26, 3)}
NEAR = {"time1": 19, "time2": 20, "mod": 21, "qkv": 22, "proj": 23, "fc1": 24, "fc2": 25, "table": 29}
SUMS, LINES = 30, 32
ORDER = ("time1", "time2", "table", "mod", "qkv", "proj", "fc1", "fc2")


def lanes_of(rows_by_cols):
    ones = jnp.ones((8, rows_by_cols.shape[1]), f32)
    return lax.dot_general(ones, rows_by_cols, (((1,), (1,)), ((), ())), precision=lax.Precision.HIGHEST, preferred_element_type=f32)[0:1]


def put_sums(pack, name, g):
    sq = g * g + grad_floor
    line, count = FAR[name]
    col = jnp.sum(sq, axis=0, keepdims=True)
    for n in range(count):
        size = min(D, g.shape[1] - n * D)
        pack[line + n : line + n + 1, 0:size] = col[:, n * D : n * D + size]
    pack[NEAR[name] : NEAR[name] + 1, 0 : g.shape[0]] = lanes_of(sq)


def copies_sum(refs):
    a, b, c, d = (r[...].astype(f32) for r in refs)
    return (a + b) + (c + d)


def sums_early(place, parts):
    def body(at, a, b, c, d, gm, gf, pack, cuts):
        for n, part in enumerate((a, b, c, d)):
            cuts[jnp.bitwise_xor(at[2], n)] = part[...].astype(f32)
        pack[...] = jnp.zeros((LINES, D), f32)
        gm[:, 0:D] = jnp.concatenate([cuts[j][:, 768 : 768 + 96] for j in range(4)], axis=1)
        for j in range(4):
            gm[:, D + j * 384 : D + (j + 1) * 384] = cuts[j][:, 0:384]
            gf[j * 48 : (j + 1) * 48, :] = cuts[j][:, 384:768]
        put_sums(pack, "proj", gm[:, 0:D])
        put_sums(pack, "fc1", gm[:, D : D + FF])
        put_sums(pack, "fc2", gf[...])

    outs = [((48, D + FF), f32), ((192, D), f32), ((LINES, D), f32)]
    return kernel_call(body, outs, (place, *parts), 2, scratch=[pltpu.VMEM((4, 48, Z_LANES), f32)], places="svvvv")


def sums_middle(pack, g_table, g_mod, sums, loss, after=()):
    def body(old, tab, mod, sums_r, loss_r, pack_r):
        pack_r[...] = old[...]
        put_sums(pack_r, "mod", mod[...])
        put_sums(pack_r, "table", tab[...])
        lane = lax.broadcasted_iota(jnp.int32, (1, D), 1)
        pack_r[SUMS : SUMS + 1, :] = jnp.where(lane == 10, loss_r[0:1, 0:1], sums_r[0:1, :])

    return kernel_call(body, [((LINES, D), f32)], (pack, g_table, g_mod, sums, loss), 2, after=after)[0]


def sums_late(pack, tail, g_time1, g_time2):
    def body(old, q0, q1, q2, q3, t1, t2, gq, pack_r):
        pack_r[...] = old[...]
        gq[...] = copies_sum((q0, q1, q2, q3))
        put_sums(pack_r, "qkv", gq[:, 0 : 3 * D])
        put_sums(pack_r, "time1", t1[...])
        put_sums(pack_r, "time2", t2[...])

    outs = [(tail[0].shape, f32), ((LINES, D), f32)]
    return kernel_call(body, outs, (pack, *tail, g_time1, g_time2), 2)


def scaled_updates(place, packs, g_time1, g_time2, g_table, g_mod, gq, gm, gf, olds, patch_state, out_t):
    parts = packs.shape[0]
    shapes = [(g_time1.shape), g_time2.shape, g_table.shape, g_mod.shape, (48, 3 * D), (48, D), (48, FF), gf.shape]

    def body(at, pk, t1, t2, tab, mod, q, m, f, *refs):
        old_rs, (pat, ost), fresh_rs, u_rs = refs[0:8], refs[8:10], refs[10:18], refs[18:26]
        u_pat, u_out, m_pat, m_out, usq, head, line_s = refs[26:]
        total = jnp.sum(pk[...], axis=0)
        lane = lax.broadcasted_iota(jnp.int32, (1, D), 1)
        grads = (t1[...], t2[...], tab[...], mod[...], q[:, 0 : 3 * D], m[:, 0:D], m[:, D : D + FF], f[...])
        sizes = []

        def size_of(u):
            return jnp.sum(jnp.sum(u * u, axis=0, keepdims=True), axis=1, keepdims=True)

        for name, g, old_r, fresh_r, u_r in zip(ORDER, grads, old_rs, fresh_rs, u_rs):
            rows, cols = g.shape
            many = rows * parts
            line, count = FAR[name]
            far_at, near_at = (0, cols) if name == "table" else (many, 0)
            for p in range(parts):
                line_s[:, near_at + p * rows : near_at + (p + 1) * rows] = pk[p, NEAR[name] : NEAR[name] + 1, 0:rows] / cols
            for n in range(count):
                wide = min(D, cols - n * D)
                line_s[:, far_at + n * D : far_at + n * D + wide] = total[line + n : line + n + 1, 0:wide] / many
            fresh = line_s[:, 0 : many + cols]
            fresh_r[...] = jnp.sum(fresh, axis=0)
            renewed = decay_rate * old_r[...].reshape(1, many + cols) + (1.0 - decay_rate) * fresh
            near, far = renewed[:, near_at : near_at + many], renewed[:, far_at : far_at + cols]
            mean = jnp.mean(far if name == "table" else near, axis=1, keepdims=True)
            shape = (rows, many)
            mine = lax.broadcasted_iota(jnp.int32, shape, 1) == lax.broadcasted_iota(jnp.int32, shape, 0) + at[0] * rows
            own = jnp.sum(jnp.where(mine, near, 0.0), axis=1, keepdims=True)
            u = g * lax.rsqrt(own / mean) * lax.rsqrt(far)
            u_r[...] = u
            sizes.append(size_of(u))
        ends = []
        for lo, wide, old, moment_r, u_r in ((0, PIN, pat, m_pat, u_pat), (PIN, POUT, ost, m_out, u_out)):
            g = q[lo : lo + wide, 3 * D : 3 * D + 48]
            moment = decay_rate * old[1] + (1.0 - decay_rate) * (g * g + grad_floor)
            moment_r[...] = moment
            u = g * lax.rsqrt(moment)
            u_r[...] = u
            ends.append(size_of(u))
        line = jnp.zeros((1, D), f32)
        for n, value in enumerate([ends[0], *sizes, ends[1]]):
            line = jnp.where(lane == n, value, line)
        for p in range(parts):
            usq[p] = jnp.broadcast_to(line[:, 0:128], (8, 128))
        head[...] = total[SUMS : SUMS + 1, :] * jnp.where(lane == 10, 1.0 / parts, 1.0)

    outs = [((o.shape[0],), f32) for o in olds] + [(s, f32) for s in shapes]
    outs += [((PIN, 48), f32), ((POUT, 48), f32)] * 2 + [((parts, 8, 128), f32), ((1, D), f32)]
    ops = (place, packs, g_time1, g_time2, g_table, g_mod, gq, gm, gf, *olds, patch_state, out_t)
    scratch = [pltpu.VMEM((1, 9 * D + 128), f32)]
    return kernel_call(body, outs, ops, 3.5, scratch=scratch, places="s" + "v" * (len(ops) - 1))


def new_weights(usq, head, counts, images, updates, weights, patch_state, out_t, m_patch, m_out):
    def body(usq_r, head_r, mp, mo, pat, ost, *refs):
        us, ms, news = refs[0:10], refs[10:18], refs[18:26]
        new_p, new_o, loss_r, rms_r = refs[26:]
        total = usq_r[0, 0:1, :]
        for p in range(1, usq_r.shape[0]):
            total = total + usq_r[p, 0:1, :]
        lane = lax.broadcasted_iota(jnp.int32, (1, 128), 1)
        size = jnp.ones((1, 128), f32)
        for n, count in enumerate(counts):
            size = jnp.where(lane == n, float(count), size)
        rms = jnp.sqrt(total / size)
        step = step_rate * jnp.sqrt(head_r[:, 0:128] / size) / jnp.maximum(1.0, rms / clip_level)
        for n in range(8):
            news[n][...] = ms[n][...] - step[:, n + 1 : n + 2] * us[n + 1][...]
        new_p[0] = pat[0] - step[:, 0:1] * us[0][...]
        new_p[1] = mp[...]
        new_o[0] = ost[0] - step[:, 9:10] * us[9][...]
        new_o[1] = mo[...]
        rms_r[...] = jnp.sum(rms[:, 0:10], axis=0)
        loss_r[...] = jnp.sum(head_r[:, 10:11], axis=0) / images

    outs = [(m.shape, f32) for m in weights] + [(patch_state.shape, f32), (out_t.shape, f32), ((1,), f32), ((10,), f32)]
    ops = (usq, head, m_patch, m_out, patch_state, out_t, *updates, *weights)
    return kernel_call(body, outs, ops, 3.5)


def gather_pieces(x):
    near = [x, flip(x, 2), flip(x, 4), flip(x, 6)]
    return near + [flip(a, 1) for a in near]


def chip_blocks(place, keep, sent, micros, spread=None, copies=0):
    def body(at, keep_r, sent_r, *refs):
        if copies:
            for c in range(copies):
                refs[-1][c] = refs[0][...]
            refs = refs[1:-1]
        for n, out in enumerate(refs):
            chip = jnp.bitwise_xor(at[0] // 2, n)
            out[...] = (keep_r[chip] + sent_r[chip].astype(f32)).astype(out.dtype)

    shape = keep.shape[1:]
    outs, ops = [(shape, f32)] + [(shape, bf16)] * 3, (place, keep, sent)
    if copies:
        outs.append(((copies,) + spread.shape, spread.dtype))
        ops += (spread,)
    return kernel_call(body, outs, ops, micros, places="s" + "v" * (len(ops) - 1))


Z_LANES = 384 + 384 + 128


def copy_blocks(place, parts, after=()):
    def body(at, a, b, c, d, own, one, two, three, cuts):
        total = (a[...] + b[...].astype(f32)) + (c[...].astype(f32) + d[...].astype(f32))
        none = jnp.zeros((48, 32), f32)
        for j in range(4):
            cuts[j, :, 0:384] = total[:, D + j * 384 : D + (j + 1) * 384]
            cuts[j, :, 384:768] = total[:, D + FF + j * 384 : D + FF + (j + 1) * 384]
            cuts[j, :, 768:] = jnp.concatenate([total[:, j * 96 : (j + 1) * 96], none], axis=1)
        for n, out in enumerate((own, one, two, three)):
            out[...] = cuts[jnp.bitwise_xor(at[2], n)].astype(out.dtype)

    outs = [((48, Z_LANES), f32)] + [((48, Z_LANES), bf16)] * 3
    return kernel_call(body, outs, (place, *parts), 2, scratch=[pltpu.VMEM((4, 48, Z_LANES), f32)], places="svvvv", after=after)


def chips_sum(blocks):
    total = blocks[0]
    for n in range(1, 4):
        total = total + flip(blocks[n], 2 * n).astype(f32)
    return total.astype(bf16)


def other_copies(total):
    return (total, flip(total, 1, "rep"), flip(total, 2, "rep"), flip(total, 3, "rep"))


def eight_by_four(
    latents, noise, tsteps, labels, patch_state, time1_w, time2_w, table_t, mod_w, qkv_w, proj_w, fc1_w, fc2_w, out_t, olds, place, plan, grid, times
):
    reps, parts = 4, 8
    images = tsteps.shape[0]
    bundle = bundle_rows(tsteps, labels, time1_w, time2_w)
    pieces = gather_pieces(bundle)
    w_own, mod16, tab16, sums = cast_weights(
        patch_state, out_t, time1_w, time2_w, table_t, mod_w, qkv_w, proj_w, fc1_w, fc2_w, after=pieces[1:4]
    )
    w_pieces = gather_pieces(w_own)
    shares, w1, w2 = modulation_shares(place, pieces, times, tab16, mod16, images)
    shares = lax.all_to_all(shares, "fsdp", 0, 0)

    w_qkv, head, mod, con, noisy, hidden0, attn16, qkv16, totals, mixture16 = attention_forward(
        tsteps, latents, noise, plan, grid, w_pieces, shares, place
    )
    keep, send, g_last, d_mix16, d_h1, d_mod, loss_tile = mlp_pass(
        noise, con, mod, hidden0, mixture16, head, w_pieces, place
    )
    send = flip(send, 1)
    d_qkv16, d_mod16, d_h0 = attention_back(
        mod, hidden0, qkv16, totals, d_mix16, d_h1, d_mod, w_qkv, loss_tile, bundle, after=(keep,)
    )
    *blocks, d_mod16 = chip_blocks(place, keep, send, 2, d_mod16, reps * parts // 2)
    everyone = [[r * parts + c * 2 + side for r in range(reps) for c in range(parts // 2)] for side in range(2)]
    own_mod = lax.all_to_all(d_mod16, ("rep", "fsdp"), 0, 0, axis_index_groups=everyone)
    oth_mod = flip(own_mod, 1)
    keep, send = tail_grad(attn16, d_qkv16, noisy, d_h0, g_last, place, True, after=(blocks[1],))
    send = flip(send, 1)
    g_mod, g_table, d_time, loss, feat16, act16_t, time_slope = condition_back(
        place, own_mod, oth_mod, w1, w2, times, tab16, mod16, reps, parts, images
    )
    cuts = copy_blocks(place, [blocks[0]] + [flip(blocks[n], 2 * n) for n in range(1, 4)], after=(loss,))
    mid = (cuts[0] + flip(cuts[1], 1, "rep").astype(f32)) + (flip(cuts[2], 2, "rep").astype(f32) + flip(cuts[3], 3, "rep").astype(f32))
    mid = other_copies(mid.astype(bf16))
    tail = other_copies(chips_sum(chip_blocks(place, keep, send, 1)))
    gm, gf, pack = sums_early(place, mid)
    d_time = lax.all_to_all(d_time, "fsdp", 0, 0)
    pack = sums_middle(pack, g_table, g_mod, sums, loss)
    g_time1, g_time2 = time_back(d_time, w2, act16_t, time_slope, feat16)
    gq, pack = sums_late(pack, tail, g_time1, g_time2)
    packs = gather_rows(pack).reshape(parts, LINES, D)
    result = scaled_updates(place, packs, g_time1, g_time2, g_table, g_mod, gq, gm, gf, olds, patch_state, out_t)
    fresh, updates = result[:8], result[8:16]
    u_patch, u_out, m_patch, m_out, usq, sums = result[16:]
    usq = lax.all_to_all(usq, "fsdp", 0, 0)
    weights = (time1_w, time2_w, table_t, mod_w, qkv_w, proj_w, fc1_w, fc2_w)
    counts = [w.size * parts for w in (patch_state[0], *weights, out_t[0])]
    *news, new_patch, new_out, loss, rms = new_weights(
        usq, sums, counts, images * reps * parts, (u_patch, *updates, u_out), weights, patch_state, out_t, m_patch, m_out
    )
    news[2] = news[2].T
    outs = [new_patch]
    for n in range(8):
        outs += [news[n], fresh[n]]
    return tuple(outs) + (new_out.transpose(0, 2, 1), loss.reshape(()), rms)


def per_device(
    latents,
    noise,
    timesteps,
    labels,
    patch_state,
    time1_w,
    time1_f,
    time2_w,
    time2_f,
    table_w,
    table_f,
    mod_w,
    mod_f,
    qkv_w,
    qkv_f,
    proj_w,
    proj_f,
    fc1_w,
    fc1_f,
    fc2_w,
    fc2_f,
    out_state,
):
    reps, parts = lax.axis_size("rep"), lax.axis_size("fsdp")
    position = lax.axis_index("fsdp")
    masters = (patch_state[0], time1_w, time2_w, table_w, mod_w, qkv_w, proj_w, fc1_w, fc2_w, out_state[0])
    images = latents.shape[0] * latents.shape[1]
    latents = latents.reshape(images, TOK_IMG, PIN).transpose(0, 2, 1)
    noise = noise.reshape(images, TOK_IMG, PIN).transpose(0, 2, 1)
    out_t = out_state.transpose(0, 2, 1)
    tsteps = timesteps.reshape(images)
    labels = labels.reshape(images)
    own_d = D // parts
    own_t = TFREQ // parts
    place = jnp.stack([position, position & 1, lax.axis_index("rep")]).astype(jnp.int32)
    plan, grid = jnp.asarray(plan_table()), jnp.asarray(place_table())
    times = jnp.asarray(time_table(), bf16)
    olds = (time1_f, time2_f, table_f, mod_f, qkv_f, proj_f, fc1_f, fc2_f)

    if parts == 8 and reps == 4:
        return eight_by_four(
            latents, noise, tsteps, labels, patch_state, time1_w, time2_w, table_w.T, mod_w, qkv_w, proj_w, fc1_w, fc2_w, out_t, olds, place, plan, grid, times
        )

    info = jnp.stack([tsteps // 32, tsteps % 32, labels // 32, labels % 32]).reshape(1, 4 * images)
    info_row = jnp.pad(info.astype(bf16), ((0, 0), (0, D - 4 * images)))
    bundle = jnp.concatenate([time1_w.astype(bf16), time2_w.astype(bf16), info_row], axis=0)
    bundle = gather_rows(bundle).reshape(parts, own_t + own_d + 1, D)
    w_time1 = bundle[:, :own_t].reshape(TFREQ, D)
    w_time2 = bundle[:, own_t : own_t + own_d].reshape(D, D)
    info_rep = bundle[:, own_t + own_d, : 4 * images]

    head = lax.all_gather(jnp.concatenate([patch_state[0], out_t[0]], axis=0).astype(bf16), "fsdp", axis=1, tiled=True)
    w_rows = gather_rows(jnp.concatenate([qkv_w, proj_w, fc1_w], axis=1).astype(bf16))
    w_fc2 = gather_rows(fc2_w.astype(bf16))
    w_qkv, w_proj, w_fc1 = w_rows[:, : 3 * D], w_rows[:, 3 * D : 4 * D], w_rows[:, 4 * D :]

    info_all = rep_gather(info_rep).reshape(reps * parts, 4, images).astype(jnp.int32)
    w_mod16 = mod_w.astype(bf16)
    w_table16 = table_w.astype(bf16)

    def condition_path(info_any):
        ts = (info_any[:, 0] * 32 + info_any[:, 1]).reshape(-1)
        lab = (info_any[:, 2] * 32 + info_any[:, 3]).reshape(-1)
        feats16 = dot(pick(ts, STEPS), times).astype(bf16)
        time_act, time_slope = silu_pair(dot(feats16, w_time1))
        time_act16 = time_act.astype(bf16)
        time_emb = dot(time_act16, w_time2)
        own_emb = lax.dynamic_slice(time_emb, (0, position * own_d), (time_emb.shape[0], own_d))
        picks = pick(lab, CLASSES)
        cond_act, cond_slope = silu_pair(own_emb + dot(picks, w_table16))
        return feats16, time_act16, time_slope, picks, cond_act.astype(bf16), cond_slope

    info_here = info_rep.reshape(parts, 4, images).astype(jnp.int32)
    cond_here = condition_path(info_here)[4]
    shares = dot(cond_here, w_mod16).reshape(parts, 8, images * D)
    shares = lax.all_to_all(shares, "fsdp", 0, 0, tiled=True)

    mod, con, noisy, hidden0, attn16, qkv16, totals, mixture16 = attention_forward(
        tsteps, latents, noise, plan, grid, (w_qkv, head), shares, place
    )
    g_proj, g_fc1, g_fc2, g_last, d_mix16, d_h1, d_mod, loss_tile = mlp_pass(
        noise, con, mod, hidden0, mixture16, head, (w_proj, w_fc1, w_fc2), place
    )
    loss_part = loss_tile[0, 0]
    d_qkv16, d_mod16, d_h0 = attention_back(
        mod, hidden0, qkv16, totals, d_mix16, d_h1, d_mod, w_qkv, loss_tile, None
    )
    g_tail, g_head = tail_grad(attn16, d_qkv16, noisy, d_h0, g_last, place, False)

    d_mod_all = rep_gather(d_mod16).reshape(1, -1)
    d_mod_all = gather_rows(d_mod_all).reshape(parts, reps, images, 8 * D)
    d_mod_all = d_mod_all.transpose(1, 0, 2, 3).reshape(reps * parts * images, 8 * D)
    feats16, time_act16, time_slope, picks, cond16, cond_slope = condition_path(info_all)
    d_cond = dot_nt(d_mod_all, w_mod16) * cond_slope
    g_mod = dot_tn(cond16, d_mod_all)
    g_table = lax.dot_general(
        picks.astype(f32), d_cond, (((0,), (0,)), ((), ())), precision=lax.Precision.HIGHEST
    )
    d_time16 = lax.all_gather(d_cond.astype(bf16), "fsdp", axis=0)
    d_time16 = d_time16.transpose(1, 0, 2).reshape(-1, D)
    own_act16 = lax.dynamic_slice(time_act16, (0, position * own_d), (time_act16.shape[0], own_d))
    g_time2 = dot_tn(own_act16, d_time16)
    d_hid16 = (dot_nt(d_time16, w_time2) * time_slope).astype(bf16)
    own_feat16 = lax.dynamic_slice(feats16, (0, position * own_t), (feats16.shape[0], own_t))
    g_time1 = dot_tn(own_feat16, d_hid16)

    g_head = lax.psum_scatter(g_head, "fsdp", scatter_dimension=1, tiled=True)
    g_tail, g_proj, g_fc1, g_fc2 = (sum_scatter(g) for g in (g_tail, g_proj, g_fc1, g_fc2))
    g_proj, g_fc1, g_fc2 = (rep_sum(g.astype(bf16)) for g in (g_proj, g_fc1, g_fc2))
    g_tail = rep_sum(g_tail.astype(bf16))
    g_head = rep_sum(g_head)
    grads = (
        g_head[:PIN],
        g_time1,
        g_time2,
        g_table,
        g_mod,
        g_tail,
        g_proj,
        g_fc1,
        g_fc2,
        g_head[PIN:].T,
    )
    loss_part = lax.psum(loss_part, "rep")
    dims = (0, 0, 1, 0, 0, 0, 0, 0)

    packs = []
    for slot in range(8):
        grad, dim = grads[slot + 1], dims[slot]
        squares = grad * grad + grad_floor
        near = jnp.sum(squares, axis=1 - dim)
        far = jnp.sum(squares, axis=dim)
        spread = lax.dynamic_update_slice(
            jnp.zeros((near.shape[0] * parts,), f32), near / far.shape[0], (position * near.shape[0],)
        )
        far = far / (near.shape[0] * parts)
        packs.append(jnp.concatenate([spread, far] if dim == 0 else [far, spread]))
    tail = jnp.stack([jnp.sum(m * m) for m in masters] + [loss_part])
    lengths = [pack.shape[0] for pack in packs]
    totals = lax.psum(jnp.concatenate(packs + [tail]), "fsdp")
    fresh = []
    start = 0
    for length in lengths:
        fresh.append(totals[start : start + length])
        start += length
    square_tot = totals[start : start + 10]
    loss = totals[start + 10] / (images * reps * parts)

    updates, counts = [], []
    plain = []
    for slot in range(10):
        grad = grads[slot]
        if slot in (0, 9):
            state = patch_state if slot == 0 else out_state
            moment = decay_rate * state[1] + (1.0 - decay_rate) * (grad * grad + grad_floor)
            plain.append(moment)
            updates.append(grad * lax.rsqrt(moment))
            counts.append(grad.size * parts)
            continue
        dim = dims[slot - 1]
        renewed = decay_rate * olds[slot - 1] + (1.0 - decay_rate) * fresh[slot - 1]
        rows = grad.shape[0] * (parts if dim == 0 else 1)
        row, col = renewed[:rows], renewed[rows:]
        mean_row = jnp.mean(row)
        if dim == 0:
            row = lax.dynamic_slice(row, (position * grad.shape[0],), (grad.shape[0],))
        else:
            col = lax.dynamic_slice(col, (position * grad.shape[1],), (grad.shape[1],))
        updates.append(grad * lax.rsqrt(row[:, None] * col[None, :] / mean_row))
        counts.append(grad.size * parts)
    update_tot = lax.psum(jnp.stack([jnp.sum(u * u) for u in updates]), "fsdp")
    sizes = np.asarray(counts, np.float32)
    size_rms = jnp.sqrt(update_tot / sizes)
    factor = step_rate * jnp.sqrt(square_tot / sizes) / jnp.maximum(1.0, size_rms / clip_level)
    new = [masters[s] - factor[s] * updates[s] for s in range(10)]
    result = [jnp.stack([new[0], plain[0]])]
    for slot in range(8):
        result += [new[slot + 1], fresh[slot]]
    return tuple(result) + (jnp.stack([new[9], plain[1]]), loss, size_rms)


def solution(mesh):
    images = P(None, ("rep", "fsdp"), None, None)
    singles = P(None, ("rep", "fsdp"))
    rows, cols = P("fsdp", None), P(None, "fsdp")
    placed = (images, images, singles, singles, P(None, None, "fsdp"))
    placed += (rows, P(), rows, P(), cols, P()) + (rows, P()) * 5 + (P(None, "fsdp", None),)
    results = (P(None, None, "fsdp"), rows, P(), rows, P(), cols, P()) + (rows, P()) * 5
    results += (P(None, "fsdp", None), P(), P())
    return jax.shard_map(per_device, mesh=mesh, in_specs=placed, out_specs=results, check_vma=False)
```

```python
import math

import jax
import jax.numpy as jnp
import numpy as np
from jax import lax
from jax.experimental import pallas as pl
from jax.experimental.pallas import tpu as pltpu
from jax.sharding import PartitionSpec as P

D = 384
HEADS = 6
HEAD_DIM = 64
FF = 1536
TFREQ = 256
GRID = 16
PIN = 16
POUT = 32
CLASSES = 1001
STEPS = 1000
TOK_IMG = 256

decay_rate = 0.5
clip_level = 1.0
step_rate = 0.5
grad_floor = 1e-30
norm_floor = 1e-06
f32 = jnp.float32
bf16 = jnp.bfloat16


def plan_table():
    s = np.arange(STEPS, dtype=np.float64)
    beta = 1e-4 + (0.02 - 1e-4) * s / (STEPS - 1)
    lbar = np.cumsum(np.log1p(-beta))
    lprev = np.concatenate([[0.0], lbar[:-1]])
    post = beta * -np.expm1(lprev) / -np.expm1(lbar)
    post[0] = post[1]
    remain = -np.expm1(lbar)
    coef = beta * beta / ((1.0 - beta) * remain)
    rows = [np.exp(0.5 * lbar), np.sqrt(remain), np.log(beta), np.log(post), coef]
    return np.stack(rows + [np.zeros(STEPS)] * 3, axis=1).astype(np.float32)


def time_table():
    half = TFREQ // 2
    freq = np.exp(np.float32(-math.log(10000.0)) * np.arange(half, dtype=np.float32) / np.float32(half)).astype(np.float32)
    angles = np.arange(STEPS, dtype=np.float32)[:, None] * freq[None, :]
    wide = angles.astype(np.float64)
    return np.concatenate([np.cos(wide), np.sin(wide)], axis=1).astype(np.float32)


def place_table():
    quarter = D // 4
    om = np.exp(np.float32(-math.log(10000.0)) * np.arange(quarter, dtype=np.float32) / np.float32(quarter)).astype(np.float32)
    n = np.arange(TOK_IMG)
    row = ((n // GRID).astype(np.float32)[:, None] * om[None, :]).astype(np.float64)
    col = ((n % GRID).astype(np.float32)[:, None] * om[None, :]).astype(np.float64)
    return np.concatenate([np.sin(row), np.cos(row), np.sin(col), np.cos(col)], axis=1).astype(np.float32)


def pick(index, count):
    return (index[:, None] == jnp.arange(count, dtype=jnp.int32)[None, :]).astype(bf16)


def silu_pair(v):
    s = 1.0 / (1.0 + jnp.exp(-v))
    return v * s, s * (1.0 + v * (1.0 - s))


def norm_parts(x):
    mean = jnp.mean(x, axis=-1, keepdims=True)
    cen = x - mean
    inv = lax.rsqrt(jnp.mean(cen * cen, axis=-1, keepdims=True) + norm_floor)
    return cen * inv, inv


def norm_back(d_norm, normed, inv):
    a = jnp.mean(d_norm, axis=-1, keepdims=True)
    b = jnp.mean(d_norm * normed, axis=-1, keepdims=True)
    return inv * (d_norm - a - normed * b)


def dot(a, b):
    return jnp.dot(a, b, preferred_element_type=f32)


def dot_nt(a, b):
    return lax.dot_general(a, b, (((1,), (1,)), ((), ())), preferred_element_type=f32)


def dot_tn(a, b):
    return lax.dot_general(a, b, (((0,), (0,)), ((), ())), preferred_element_type=f32)


def flip(x, bit, axis="fsdp"):
    size = lax.axis_size(axis)
    return lax.ppermute(x, axis, [(i, i ^ bit) for i in range(size)])


def rep_gather(x):
    size = lax.axis_size("rep")
    me = lax.axis_index("rep")
    parts = jnp.stack([x] + [flip(x, k, "rep") for k in range(1, size)])
    return jnp.stack([lax.dynamic_index_in_dim(parts, me ^ j, 0, keepdims=False) for j in range(size)])


def rep_sum(x16):
    size = lax.axis_size("rep")
    parts = [x16.astype(f32)] + [flip(x16, k, "rep").astype(f32) for k in range(1, size)]
    while len(parts) > 1:
        parts = [parts[i] + parts[i + 1] for i in range(0, len(parts), 2)]
    return parts[0]


def sum_scatter(grad):
    return lax.psum_scatter(grad, "fsdp", scatter_dimension=0, tiled=True)


def gather_rows(x):
    return lax.all_gather(x, "fsdp", axis=0, tiled=True)


def lane_half(shape, which):
    lane = lax.broadcasted_iota(jnp.int32, shape, 1)
    return (lane < HEAD_DIM) if which == 0 else (lane >= HEAD_DIM)


FLOPS_US = 1_150_000_000


def kernel_call(body, outs, operands, micros, scratch=(), places=None, after=(), room=16):
    vmem = pl.BlockSpec(memory_space=pltpu.VMEM)
    smem = pl.BlockSpec(memory_space=pltpu.SMEM)
    places = places or "v" * len(operands)
    count = len(operands)

    def run(*refs):
        body(*refs[:count], *refs[count + len(after) :])

    return pl.pallas_call(
        run,
        out_shape=[jax.ShapeDtypeStruct(s, t) for s, t in outs],
        in_specs=[{"s": smem, "v": vmem, "h": pl.BlockSpec(memory_space=pltpu.HBM)}[p] for p in places] + [pl.BlockSpec(memory_space=pl.ANY)] * len(after),
        out_specs=[vmem] * len(outs),
        scratch_shapes=list(scratch),
        compiler_params=pltpu.CompilerParams(vmem_limit_bytes=room * 2**20),
        cost_estimate=pl.CostEstimate(flops=int(micros * FLOPS_US), bytes_accessed=1_000_000, transcendentals=0),
    )(*(pltpu.with_memory_space_constraint(x, pltpu.HBM) if p == "h" else x for x, p in zip(operands, places)), *after)


HEAD = PIN + POUT
CAST_ROOM = 48
INFO = 80
BUNDLE = 96
TAIL = 3 * D + 128
SENT = TAIL + D + 2 * FF


def piece_owner(at, n):
    return jnp.bitwise_xor(at[0], 2 * (n % 4) + n // 4)


def shards_of(refs):
    return list(refs[:5]) + [refs[5].at[n] for n in range(3)]


def attention_forward(tsteps, lat, noi, plan, grid, weights, shares, place, after=()):
    images = lat.shape[0]
    fast = len(weights) == 6

    def body(ts, at, lat_r, noi_r, plan_r, grid_r, share_r, *refs):
        if fast:
            wq_r, head_r, head_s = refs[6], refs[7], refs[-1]
            shards = shards_of(refs)
            for n in range(8):
                owner = piece_owner(at, n)
                rows = pl.ds(pl.multiple_of(owner * 48, 48), 48)
                wq_r[rows, :] = shards[n][:, 0 : 3 * D]
                head_s[owner] = shards[n][:, 3 * D : 3 * D + 48]
            for p in range(8):
                head_r[:, p * 48 : (p + 1) * 48] = head_s[p]
            refs = refs[8:-1]
        else:
            wq_r, head_r = refs[:2]
            refs = refs[2:]
        mod_r, con_r, noisy_r, h0_r, attn_r, qkv_r, total_r, mix_r = refs
        total = share_r[0]
        for p in range(1, share_r.shape[0]):
            total = total + share_r[p]
        width = total.shape[1]
        for n in range(8):
            i, col = divmod(n * width, 8 * D)
            mod_r[i : i + 1, col : col + width] = total[n : n + 1]
        for i in range(images):
            row = plan_r[pl.ds(ts[i], 1), :]
            con_r[i : i + 1, :] = row
            noisy = (row[:, 0:1] * lat_r[i] + row[:, 1:2] * noi_r[i]).astype(bf16)
            noisy_r[i] = noisy
            h0 = dot_tn(noisy, head_r[0:PIN, :]) + grid_r[...]
            h0_r[i] = h0
            norm, _ = norm_parts(h0)
            attn = (norm * (1.0 + mod_r[i : i + 1, D : 2 * D]) + mod_r[i : i + 1, 0:D]).astype(bf16)
            attn_r[i] = attn
            for part in range(3):
                qkv_r[i, :, part * D : (part + 1) * D] = dot(attn, wq_r[:, part * D : (part + 1) * D]).astype(bf16)
        lane = lax.broadcasted_iota(jnp.int32, (TOK_IMG, 128), 1)
        logs = [jnp.zeros((TOK_IMG, 128), f32)] * images
        for pair in range(HEADS // 2):
            for i in range(images):
                q = qkv_r[i, :, pair * 128 : pair * 128 + 128]
                k = qkv_r[i, :, D + pair * 128 : D + pair * 128 + 128]
                v = qkv_r[i, :, 2 * D + pair * 128 : 2 * D + pair * 128 + 128]
                mixed = None
                for half in range(2):
                    own = lane_half(q.shape, half)
                    zero = jnp.zeros_like(q)
                    s = dot_nt(jnp.where(own, q, zero), k) * 0.125
                    top = jnp.max(s, axis=-1, keepdims=True)
                    p = jnp.exp(s - top)
                    total = jnp.sum(p, axis=-1, keepdims=True)
                    p = p * (1.0 / total)
                    logs[i] = jnp.where(lane == pair * 2 + half, top + jnp.log(total), logs[i])
                    o = dot(p.astype(bf16), jnp.where(own, v, zero))
                    mixed = o if mixed is None else mixed + o
                mix_r[i, :, pair * 128 : pair * 128 + 128] = mixed.astype(bf16)
        for i in range(images):
            total_r[i] = logs[i]

    outs = [
        ((images, 8 * D), f32),
        ((images, 8), f32),
        ((images, PIN, TOK_IMG), bf16),
        ((images, TOK_IMG, D), f32),
        ((images, TOK_IMG, D), bf16),
        ((images, TOK_IMG, 3 * D), bf16),
        ((images, TOK_IMG, 128), f32),
        ((images, TOK_IMG, D), bf16),
    ]
    scratch = []
    if fast:
        outs = [((D, 3 * D), bf16), ((HEAD, D), bf16)] + outs
        scratch = [pltpu.VMEM((8, HEAD, 48), bf16)]
    ops = (tsteps, place, lat, noi, plan, grid, shares, *weights)
    return kernel_call(
        body, outs, ops, 8, scratch=scratch, places="ss" + "v" * (len(ops) - 2), after=after
    )


BLOCK = 384
WIDE = 768


def mlp_pass(noi, con, mod, h0_all, mix_all, head, weights, place, after=()):
    images = noi.shape[0]
    bend_scale = math.sqrt(2.0 / math.pi)
    share = 1.0 / (TOK_IMG * PIN)

    fast = len(weights) == 6

    def body(at, noi_r, con_r, mod_r, h0_r, mix_r, head_r, *refs):
        if fast:
            wp_r, w1_r, w2_r = refs[-3:]
            shards = shards_of(refs)
            for n in range(8):
                owner = piece_owner(at, n)
                rows = pl.ds(pl.multiple_of(owner * 48, 48), 48)
                wp_r[rows, :] = shards[n][:, TAIL : TAIL + D]
                w1_r[rows, :] = shards[n][:, TAIL + D : TAIL + D + FF]
                for b in range(4):
                    w2_r[pl.ds(pl.multiple_of(owner * 192 + b * 48, 48), 48), :] = shards[n][:, TAIL + D + FF + b * D : TAIL + D + FF + (b + 1) * D]
            refs = refs[6:-3]
        else:
            wp_r, w1_r, w2_r = refs[:3]
            refs = refs[3:]
        g_refs, refs = refs[: 2 if fast else 3], refs[2 if fast else 3 :]
        glast_r, dmix_r, dh1_r, dmod_r, loss_r, mlp_r, act_r, dinner_r, douter_r, dbr_r, slope_r = refs
        g_last = None
        wo = head_r[PIN:HEAD, :]
        losses = jnp.zeros((1, 1), f32)
        dmod_r[:, 0 : 2 * D] = jnp.zeros((images, 2 * D), f32)
        for i in range(images):
            def m(slot):
                return mod_r[i : i + 1, slot * D : (slot + 1) * D]

            def put(slot, value):
                dmod_r[i : i + 1, slot * D : (slot + 1) * D] = jnp.sum(value, axis=0, keepdims=True)

            branch = dot(mix_r[i], wp_r[...])
            h1 = h0_r[i] + m(2) * branch
            norm1, inv1 = norm_parts(h1)
            mlp = (norm1 * (1.0 + m(4)) + m(3)).astype(bf16)
            tokens = slice(i * TOK_IMG, (i + 1) * TOK_IMG)
            mlp_r[tokens, :] = mlp
            outer = None
            for b in range(FF // WIDE):
                cols = slice(b * WIDE, (b + 1) * WIDE)
                x = dot(mlp, w1_r[:, cols])
                sq = x * x
                t = jnp.tanh(bend_scale * x * (1.0 + 0.044715 * sq))
                hx = 0.5 * x
                act = (hx * (1.0 + t)).astype(bf16)
                act_r[tokens, cols] = act
                slope_r[:, cols] = 0.5 * (1.0 + t) + hx * (1.0 - t * t) * (bend_scale + (3 * 0.044715 * bend_scale) * sq)
                part = dot(act, w2_r[cols, :])
                outer = part if outer is None else outer + part
            h2 = h1 + m(5) * outer
            norm2, inv2 = norm_parts(h2)
            fin = (norm2 * (1.0 + m(7)) + m(6)).astype(bf16)
            out = dot_nt(wo, fin)
            log_beta, post_log, coef = (con_r[i : i + 1, n : n + 1] for n in (2, 3, 4))
            miss = out[:PIN] - noi_r[i]
            mixing = (out[PIN:] + 1.0) * 0.5
            log_var = mixing * log_beta + (1.0 - mixing) * post_log
            ratio = jnp.exp(post_log - log_var)
            square = miss * miss
            weigh = coef * jnp.exp(-log_var)
            terms = square + 0.5 * (-1.0 + log_var - post_log + ratio + weigh * square)
            losses += share * jnp.sum(jnp.sum(terms, axis=0, keepdims=True), axis=1, keepdims=True)
            d_guess = share * miss * (2.0 + weigh)
            d_mixed = (share * 0.25) * (1.0 - ratio - weigh * square) * (log_beta - post_log)
            d_out = jnp.concatenate([d_guess, d_mixed], axis=0).astype(bf16)
            piece = dot(d_out, fin)
            g_last = piece if g_last is None else g_last + piece
            d_fin = dot_tn(d_out, wo)
            put(6, d_fin)
            put(7, d_fin * norm2)
            d_h2 = norm_back(d_fin * (1.0 + m(7)), norm2, inv2)
            put(5, d_h2 * outer)
            d_outer = (m(5) * d_h2).astype(bf16)
            douter_r[tokens, :] = d_outer
            d_mlp = None
            for b in range(FF // WIDE):
                cols = slice(b * WIDE, (b + 1) * WIDE)
                d_in = (dot_nt(d_outer, w2_r[cols, :]) * slope_r[:, cols]).astype(bf16)
                dinner_r[tokens, cols] = d_in
                part = dot_nt(d_in, w1_r[:, cols])
                d_mlp = part if d_mlp is None else d_mlp + part
            put(3, d_mlp)
            put(4, d_mlp * norm1)
            d_h1 = d_h2 + norm_back(d_mlp * (1.0 + m(4)), norm1, inv1)
            dh1_r[i] = d_h1
            put(2, d_h1 * branch)
            d_br = (m(2) * d_h1).astype(bf16)
            dbr_r[tokens, :] = d_br
            dmix_r[i] = dot_nt(d_br, wp_r[...]).astype(bf16)
        loss_r[...] = jnp.broadcast_to(losses, loss_r.shape)
        glast_r[...] = g_last
        mix = jnp.concatenate([mix_r[i] for i in range(images)], axis=0)
        if not fast:
            g_refs[0][...] = dot_tn(mix, dbr_r[...])
        else:
            deal_rows(*g_refs, dot_tn(mix, dbr_r[...]), at[1], 0)
        for b in range(FF // BLOCK):
            cols = slice(b * BLOCK, (b + 1) * BLOCK)
            g_in = dot_tn(mlp_r[...], dinner_r[:, cols])
            g_out = dot_tn(act_r[:, cols], douter_r[...])
            if not fast:
                g_refs[1][:, cols] = g_in
                g_refs[2][cols, :] = g_out
                continue
            deal_rows(*g_refs, g_in, at[1], D + b * BLOCK)
            deal(*g_refs, g_out[0:192], g_out[192:384], at[1], b, D + FF, 4)

    if fast:
        outs = [((4, 48, D + 2 * FF), f32), ((4, 48, D + 2 * FF), bf16)]
    else:
        outs = [((D, D), f32), ((D, FF), f32), ((FF, D), f32)]
    outs += [
        ((POUT, D), f32),
        ((images, TOK_IMG, D), bf16),
        ((images, TOK_IMG, D), f32),
        ((images, 8 * D), f32),
        ((8, 128), f32),
    ]
    ops = (place, noi, con, mod, h0_all, mix_all, head, *weights)
    many = images * TOK_IMG
    scratch = [pltpu.VMEM((many, n), bf16) for n in (D, FF, FF, D, D)] + [pltpu.VMEM((TOK_IMG, FF), f32)]
    if fast:
        scratch += [pltpu.VMEM(shape, bf16) for shape in ((D, D), (D, FF), (FF, D))]
    return kernel_call(body, outs, ops, 13, scratch=scratch, places="s" + "v" * (len(ops) - 1), after=after, room=32)


def deal(keep_r, send_r, left, right, core, chip, lanes, blocks=1):
    rows, width = left.shape[0] // blocks, left.shape[1]
    kept = jnp.where(core == 0, left, right)
    sent = jnp.where(core == 0, right, left).astype(bf16)
    for b in range(blocks):
        cols = slice(lanes + b * width, lanes + (b + 1) * width)
        keep_r[chip, :, cols] = kept[b * rows : (b + 1) * rows]
        send_r[chip, :, cols] = sent[b * rows : (b + 1) * rows]


def deal_rows(keep_r, send_r, grad, core, lanes):
    for c in range(4):
        deal(keep_r, send_r, grad[c * 96 : c * 96 + 48], grad[c * 96 + 48 : c * 96 + 96], core, c, lanes)


MOD_ROWS, MOD_LANES = 16, 512


def heads_back(qkv_all, total_all, dmix_all, after=()):
    images = qkv_all.shape[0]

    def body(qkv_r, total_r, dmix_r, dqkv_r):
        for pair in range(HEADS // 2):
            lanes = slice(pair * 128, pair * 128 + 128)
            for i in range(images):
                q = qkv_r[i, :, pair * 128 : pair * 128 + 128]
                k = qkv_r[i, :, D + pair * 128 : D + pair * 128 + 128]
                v = qkv_r[i, :, 2 * D + pair * 128 : 2 * D + pair * 128 + 128]
                do = dmix_r[i, :, lanes]
                dq = dk = dv = None
                for half in range(2):
                    own = lane_half(q.shape, half)
                    zero = jnp.zeros_like(q)
                    do_h = jnp.where(own, do, zero)
                    q_h = jnp.where(own, q, zero)
                    head = pair * 2 + half
                    p = jnp.exp(dot_nt(q_h, k) * 0.125 - total_r[i, :, head : head + 1])
                    dp = dot_nt(do_h, v)
                    ds = (p * (dp - jnp.sum(dp * p, axis=-1, keepdims=True))).astype(bf16)
                    a = dot(ds, jnp.where(own, k, zero))
                    b = dot_tn(ds, q_h)
                    c = dot_tn(p.astype(bf16), do_h)
                    dq, dk, dv = (a, b, c) if dq is None else (dq + a, dk + b, dv + c)
                rows = slice(i * TOK_IMG, (i + 1) * TOK_IMG)
                for part, value in enumerate((dq * 0.125, dk * 0.125, dv)):
                    dqkv_r[rows, part * D + pair * 128 : part * D + pair * 128 + 128] = value.astype(bf16)

    outs = [((images * TOK_IMG, 3 * D), bf16)]
    return kernel_call(body, outs, (qkv_all, total_all, dmix_all), 4, after=after)[0]


def attention_back(place, mod, h0_all, attn_all, dqkv, dh1_all, dmod_all, w_qkv, noisy_all, g_last, loss_tile, info, after=()):
    images = mod.shape[0]

    def body(at, mod_r, h0_r, attn_r, dqkv_r, dh1_r, dmod_in, wq_r, noisy_r, last_r, loss_r, *refs):
        *g_refs, dmod_r, line = refs if info is None else refs[1:]
        patch = None
        for i in range(images):
            rows = slice(i * TOK_IMG, (i + 1) * TOK_IMG)
            d_attn = None
            for part in range(3):
                cols = slice(part * D, (part + 1) * D)
                piece = dot_nt(dqkv_r[rows, cols], wq_r[:, cols])
                d_attn = piece if d_attn is None else d_attn + piece
            norm, inv = norm_parts(h0_r[i])
            line[i : i + 1, 0:D] = jnp.sum(d_attn, axis=0, keepdims=True)
            line[i : i + 1, D : 2 * D] = jnp.sum(d_attn * norm, axis=0, keepdims=True)
            line[i : i + 1, 2 * D :] = dmod_in[i : i + 1, 2 * D :]
            d_h0 = (dh1_r[i] + norm_back(d_attn * (1.0 + mod_r[i : i + 1, D : 2 * D]), norm, inv)).astype(bf16)
            piece = dot(noisy_r[i], d_h0)
            patch = piece if patch is None else patch + piece
        if info is not None:
            each = 8 * D // MOD_LANES
            block = [line[i : i + 1, n * MOD_LANES : (n + 1) * MOD_LANES] for i in range(images) for n in range(each)]
            lane = lax.broadcasted_iota(jnp.int32, (1, MOD_LANES), 1)
            loss = loss_r[0:1, 0:1]
            high = loss.astype(bf16).astype(f32)
            mid = (loss - high).astype(bf16).astype(f32)
            low = loss - high - mid
            block.append(jnp.where(lane == 0, high, jnp.where(lane == 1, mid, jnp.where(lane == 2, low, 0.0))))
            told = refs[0][INFO:BUNDLE, :].astype(f32)[0:1]
            block.append(jnp.concatenate([told, jnp.zeros((1, MOD_LANES - D), f32)], axis=1))
            block.append(jnp.zeros((MOD_ROWS - len(block), MOD_LANES), f32))
            block = jnp.concatenate(block, axis=0).astype(bf16)
            for c in range(4):
                dmod_r[c] = block
        else:
            dmod_r[...] = line[...].astype(bf16)
        for part in range(3):
            cols = slice(part * D, (part + 1) * D)
            grad = dot_tn(attn_r[...], dqkv_r[:, cols])
            if info is not None:
                deal_rows(*g_refs, grad, at[1], part * D)
            else:
                g_refs[0][:, cols] = grad
        head = jnp.concatenate([patch, last_r[...]], axis=0)
        if info is None:
            g_refs[1][...] = head
            return
        none = jnp.zeros((HEAD, 128 - 48), f32)
        for c in range(4):
            left = jnp.concatenate([head[:, c * 96 : c * 96 + 48], none], axis=1)
            right = jnp.concatenate([head[:, c * 96 + 48 : c * 96 + 96], none], axis=1)
            deal(*g_refs, left, right, at[1], c, 3 * D)

    if info is None:
        outs = [((D, 3 * D), f32), ((HEAD, D), f32), ((images, 8 * D), bf16)]
    else:
        outs = [((4, 48, TAIL), f32), ((4, 48, TAIL), bf16), ((4, MOD_ROWS, MOD_LANES), bf16)]
    ops = (place, mod, h0_all, attn_all.reshape(-1, D), dqkv, dh1_all, dmod_all, w_qkv, noisy_all, g_last, loss_tile)
    if info is not None:
        ops += (info,)
    scratch = [pltpu.VMEM((images, 8 * D), f32)]
    return kernel_call(body, outs, ops, 4, scratch=scratch, places="s" + "v" * (len(ops) - 1), after=after)


def bundle_rows(tsteps, labels, time1_w, time2_w):
    images = tsteps.shape[0]

    def body(ts_h, lab_h, t1_h, t2_h, out_r, ts, lab, t1_r, t2_r, sems):
        copies = [
            pltpu.make_async_copy(a, b, sems.at[n])
            for n, (a, b) in enumerate(((ts_h, ts), (lab_h, lab), (t1_h, t1_r), (t2_h, t2_r)))
        ]
        for copy in copies:
            copy.start()
        for copy in copies:
            copy.wait()
        rows = t1_r.shape[0]
        out_r[0:rows, :] = t1_r[...].astype(bf16)
        out_r[rows:INFO, :] = t2_r[...].astype(bf16)
        lane = lax.broadcasted_iota(jnp.int32, (BUNDLE - INFO, D), 1)
        info = jnp.zeros((BUNDLE - INFO, D), jnp.int32)
        for i in range(images):
            for n, value in enumerate((ts[i] // 32, ts[i] % 32, lab[i] // 32, lab[i] % 32)):
                info = jnp.where(lane == n * images + i, value, info)
        out_r[INFO:BUNDLE, :] = info.astype(f32).astype(bf16)

    ops = (tsteps, labels, time1_w, time2_w)
    scratch = [pltpu.SMEM((images,), jnp.int32)] * 2 + [pltpu.VMEM(a.shape, f32) for a in ops[2:]] + [pltpu.SemaphoreType.DMA((4,))]
    return kernel_call(body, [((BUNDLE, D), bf16)], ops, 1.5, places="hhhh", scratch=scratch)[0]


def cast_weights(patch_state, out_t, time1_w, time2_w, table_t, mod_w, qkv_w, proj_w, fc1_w, fc2_w, after=()):
    def body(pa, ou, t1, t2, ta, mo, qk, pr, f1, f2, w_r, mod16, tab16, sums):
        w_r[:, 0 : 3 * D] = qk[...].astype(bf16)
        head = jnp.concatenate([pa[0], ou[0]], axis=0)
        w_r[:, 3 * D : TAIL] = jnp.concatenate([head, jnp.zeros((HEAD, 128 - 48), f32)], axis=1).astype(bf16)
        w_r[:, TAIL : TAIL + D] = pr[...].astype(bf16)
        w_r[:, TAIL + D : TAIL + D + FF] = f1[...].astype(bf16)
        for b in range(4):
            w_r[:, TAIL + D + FF + b * D : TAIL + D + FF + (b + 1) * D] = f2[b * 48 : (b + 1) * 48, :].astype(bf16)
        mod16[...] = mo[...].astype(bf16)
        tab16[...] = ta[...].astype(bf16)
        lane = lax.broadcasted_iota(jnp.int32, (8, D), 1)
        line = jnp.zeros((8, D), f32)
        for n, m in enumerate((pa[0], t1[...], t2[...], ta[...], mo[...], qk[...], pr[...], f1[...], f2[...], ou[0])):
            line = jnp.where(lane == n, jnp.sum(jnp.sum(m * m, axis=0, keepdims=True), axis=1, keepdims=True), line)
        sums[...] = line

    outs = [((48, SENT), bf16), (mod_w.shape, bf16), (table_t.shape, bf16), ((8, D), f32)]
    ops = (patch_state, out_t, time1_w, time2_w, table_t, mod_w, qkv_w, proj_w, fc1_w, fc2_w)
    return kernel_call(body, outs, ops, 2.5, after=after, room=CAST_ROOM)


def picked(index, count):
    lane = lax.broadcasted_iota(jnp.int32, (index.shape[0], count), 1)
    return (lane == index).astype(f32).astype(bf16)


def one_hot(shape, test):
    row, col = lax.broadcasted_iota(jnp.int32, shape, 0), lax.broadcasted_iota(jnp.int32, shape, 1)
    return test(row, col).astype(f32).astype(bf16)


def condition_body(infos, images, w1, w2, times_r, tab_r, position):
    own_d = tab_r.shape[0]
    ts, lab = [], []
    for i in range(images):
        for whole in infos:
            ts.append((whole[:, i : i + 1] * 32.0 + whole[:, images + i : images + i + 1]).astype(jnp.int32))
            lab.append((whole[:, 2 * images + i : 2 * images + i + 1] * 32.0 + whole[:, 3 * images + i : 3 * images + i + 1]).astype(jnp.int32))
    ts, lab = jnp.concatenate(ts, axis=0), jnp.concatenate(lab, axis=0)
    feats = dot(picked(ts, STEPS), times_r[...]).astype(bf16)
    act, time_slope = silu_pair(dot(feats, w1))
    act = act.astype(bf16)
    own = one_hot((D, own_d), lambda r, c: r == c + position * own_d)
    emb = dot(act, dot(w2, own).astype(bf16))
    picks = picked(lab, CLASSES)
    cond, cond_slope = silu_pair(emb + dot_nt(picks, tab_r[...]))
    return feats, act, time_slope, picks, cond.astype(bf16), cond_slope, own


def modulation_shares(place, pieces, times, tab16, mod16, images):
    parts = 8
    width = images * D

    def body(at, *refs):
        times_r, tab_r, mod_r, out_r, w1_r, w2_r, info_r = refs[8:]
        for n in range(8):
            owner = piece_owner(at, n)
            w1_r[pl.ds(pl.multiple_of(owner * 32, 32), 32), :] = refs[n][0:32, :]
            w2_r[pl.ds(pl.multiple_of(owner * 48, 48), 48), :] = refs[n][32:INFO, :]
            info_r[pl.ds(owner, 1), :] = refs[n][INFO:BUNDLE, 0:128].astype(f32)[0:1]
        cond = condition_body([info_r[...]], images, w1_r[...], w2_r[...], times_r, tab_r, at[0])[4]
        for s in range(8):
            i, col = divmod(s * width, 8 * D)
            value = dot(cond[i * parts : (i + 1) * parts], mod_r[:, col : col + width])
            for p in range(parts):
                out_r[p, s : s + 1, :] = value[p : p + 1]

    outs = [((parts, 8, width), f32), ((TFREQ, D), bf16), ((D, D), bf16)]
    ops = (place, *pieces, times, tab16, mod16)
    return kernel_call(body, outs, ops, 3, places="s" + "v" * 11, scratch=[pltpu.VMEM((parts, 128), f32)])


def condition_back(place, own_mod, oth_mod, w1, w2, times, tab16, mod16, passed, reps, parts, images):
    devices = reps * parts
    count = devices * images
    own_t, own_d = TFREQ // parts, D // parts
    each = 8 * D // MOD_LANES

    def body(at, own_r, oth_r, w1_r, w2_r, times_r, tab_r, mod_r, in_r, gm_r, gt_r, dc_r, loss_r, feat_r, act_r, slope_r, out_r, all_s, dmod_s):
        out_r[...] = in_r[...]
        for r in range(reps):
            block = slice(r * MOD_ROWS, (r + 1) * MOD_ROWS)
            for c in range(parts // 2):
                mine = pl.multiple_of((r * parts + 2 * c + at[1]) * MOD_ROWS, MOD_ROWS)
                its = pl.multiple_of((r * parts + 2 * c + 1 - at[1]) * MOD_ROWS, MOD_ROWS)
                all_s[pl.ds(mine, MOD_ROWS), :] = own_r[c, block, :]
                all_s[pl.ds(its, MOD_ROWS), :] = oth_r[c, block, :]
        rows = all_s[...]
        take = one_hot((devices, devices * MOD_ROWS), lambda r, c: c == r * MOD_ROWS + images * each + 1)
        infos = dot(take, rows)
        feats, act, time_slope, picks, cond, cond_slope, own = condition_body([infos], images, w1_r[...], w2_r[...], times_r, tab_r, at[0])
        near = one_hot((TFREQ, own_t), lambda r, c: r == c + at[0] * own_t)
        feat_r[...] = dot(feats, near).astype(bf16)
        act_r[...] = dot(act, own).astype(bf16)
        slope_r[...] = time_slope
        for n in range(each):
            take = one_hot((count, devices * MOD_ROWS), lambda r, c: c == (r % devices) * MOD_ROWS + (r // devices) * each + n)
            dmod_s[:, n * MOD_LANES : (n + 1) * MOD_LANES] = dot(take, rows).astype(bf16)
        take = one_hot((8, devices * MOD_ROWS), lambda r, c: c % MOD_ROWS == images * each)
        loss = dot(take, rows)
        loss_r[...] = jnp.broadcast_to(loss[:, 0:1] + loss[:, 1:2] + loss[:, 2:3], loss_r.shape)
        d_mod = dmod_s[...]
        d_cond = dot_nt(d_mod, mod_r[...]) * cond_slope
        wide = jnp.concatenate([d_cond, jnp.zeros((count, 128 - own_d), f32)], axis=1).astype(bf16)
        for p in range(parts):
            dc_r[p] = wide
        gm_r[...] = dot_tn(cond, d_mod)
        high = d_cond.astype(bf16)
        rest = d_cond - high.astype(f32)
        mid = rest.astype(bf16)
        low = (rest - mid.astype(f32)).astype(bf16)
        gt_r[...] = dot_tn(high, picks) + (dot_tn(mid, picks) + dot_tn(low, picks))

    outs = [((own_d, 8 * D), f32), ((own_d, CLASSES), f32), ((parts, count, 128), bf16), ((8, 128), f32)]
    outs += [((count, own_t), bf16), ((count, own_d), bf16), ((count, D), f32), (passed.shape, passed.dtype)]
    ops = (place, own_mod, oth_mod, w1, w2, times, tab16, mod16, passed)
    scratch = [pltpu.VMEM((devices * MOD_ROWS, MOD_LANES), bf16), pltpu.VMEM((count, 8 * D), bf16)]
    return kernel_call(body, outs, ops, 4, scratch=scratch, places="s" + "v" * 8)


def time_back(d_time, w2, act16, slope, feat16):
    parts, own_d = d_time.shape[0], act16.shape[1]
    own_t = TFREQ // parts

    def body(dt_r, w2_r, act_r, slope_r, feat_r, g1_r, g2_r):
        d_all = jnp.concatenate([dt_r[p, :, 0:own_d].astype(f32) for p in range(parts)], axis=1).astype(bf16)
        g2_r[...] = dot_tn(act_r[...], d_all)
        d_hid = (dot_nt(d_all, w2_r[...]) * slope_r[...]).astype(bf16)
        g1_r[...] = dot_tn(feat_r[...], d_hid)

    outs = [((own_t, D), f32), ((own_d, D), f32)]
    return kernel_call(body, outs, (d_time, w2, act16, slope, feat16), 2)


FAR = {"time1": (0, 1), "time2": (1, 1), "mod": (2, 8), "qkv": (10, 3), "proj": (13, 1), "fc1": (14, 4), "fc2": (18, 1), "table": (26, 3)}
NEAR = {"time1": 19, "time2": 20, "mod": 21, "qkv": 22, "proj": 23, "fc1": 24, "fc2": 25, "table": 29}
SUMS, LINES = 30, 32
ORDER = ("time1", "time2", "table", "mod", "qkv", "proj", "fc1", "fc2")


def lanes_of(rows_by_cols):
    ones = jnp.ones((8, rows_by_cols.shape[1]), f32)
    return lax.dot_general(ones, rows_by_cols, (((1,), (1,)), ((), ())), precision=lax.Precision.HIGHEST, preferred_element_type=f32)[0:1]


def put_sums(pack, name, g):
    sq = g * g + grad_floor
    line, count = FAR[name]
    col = jnp.sum(sq, axis=0, keepdims=True)
    for n in range(count):
        size = min(D, g.shape[1] - n * D)
        pack[line + n : line + n + 1, 0:size] = col[:, n * D : n * D + size]
    pack[NEAR[name] : NEAR[name] + 1, 0 : g.shape[0]] = lanes_of(sq)


def copies_sum(refs):
    a, b, c, d = (r[...].astype(f32) for r in refs)
    return (a + b) + (c + d)


def sums_early(place, parts):
    def body(at, a, b, c, d, gm, gf, pack, cuts):
        for n, part in enumerate((a, b, c, d)):
            cuts[jnp.bitwise_xor(at[2], n)] = part[...].astype(f32)
        pack[...] = jnp.zeros((LINES, D), f32)
        gm[:, 0:D] = jnp.concatenate([cuts[j][:, 768 : 768 + 96] for j in range(4)], axis=1)
        for j in range(4):
            gm[:, D + j * 384 : D + (j + 1) * 384] = cuts[j][:, 0:384]
            gf[j * 48 : (j + 1) * 48, :] = cuts[j][:, 384:768]
        put_sums(pack, "proj", gm[:, 0:D])
        put_sums(pack, "fc1", gm[:, D : D + FF])
        put_sums(pack, "fc2", gf[...])

    outs = [((48, D + FF), f32), ((192, D), f32), ((LINES, D), f32)]
    return kernel_call(body, outs, (place, *parts), 2, scratch=[pltpu.VMEM((4, 48, Z_LANES), f32)], places="svvvv")


def sums_middle(pack, g_table, g_mod, sums, loss, after=()):
    def body(old, tab, mod, sums_r, loss_r, pack_r):
        pack_r[...] = old[...]
        put_sums(pack_r, "mod", mod[...])
        put_sums(pack_r, "table", tab[...])
        lane = lax.broadcasted_iota(jnp.int32, (1, D), 1)
        pack_r[SUMS : SUMS + 1, :] = jnp.where(lane == 10, loss_r[0:1, 0:1], sums_r[0:1, :])

    return kernel_call(body, [((LINES, D), f32)], (pack, g_table, g_mod, sums, loss), 2, after=after)[0]


def sums_late(pack, tail, g_time1, g_time2):
    def body(old, q0, q1, q2, q3, t1, t2, gq, pack_r):
        pack_r[...] = old[...]
        gq[...] = copies_sum((q0, q1, q2, q3))
        put_sums(pack_r, "qkv", gq[:, 0 : 3 * D])
        put_sums(pack_r, "time1", t1[...])
        put_sums(pack_r, "time2", t2[...])

    outs = [(tail[0].shape, f32), ((LINES, D), f32)]
    return kernel_call(body, outs, (pack, *tail, g_time1, g_time2), 2)


def scaled_updates(place, packs, g_time1, g_time2, g_table, g_mod, gq, gm, gf, olds, patch_state, out_t):
    parts = packs.shape[0]
    shapes = [(g_time1.shape), g_time2.shape, g_table.shape, g_mod.shape, (48, 3 * D), (48, D), (48, FF), gf.shape]

    def body(at, pk, t1, t2, tab, mod, q, m, f, *refs):
        old_rs, (pat, ost), fresh_rs, u_rs = refs[0:8], refs[8:10], refs[10:18], refs[18:26]
        u_pat, u_out, m_pat, m_out, usq, head, line_s = refs[26:]
        total = jnp.sum(pk[...], axis=0)
        lane = lax.broadcasted_iota(jnp.int32, (1, D), 1)
        grads = (t1[...], t2[...], tab[...], mod[...], q[:, 0 : 3 * D], m[:, 0:D], m[:, D : D + FF], f[...])
        sizes = []

        def size_of(u):
            return jnp.sum(jnp.sum(u * u, axis=0, keepdims=True), axis=1, keepdims=True)

        for name, g, old_r, fresh_r, u_r in zip(ORDER, grads, old_rs, fresh_rs, u_rs):
            rows, cols = g.shape
            many = rows * parts
            line, count = FAR[name]
            far_at, near_at = (0, cols) if name == "table" else (many, 0)
            for p in range(parts):
                line_s[:, near_at + p * rows : near_at + (p + 1) * rows] = pk[p, NEAR[name] : NEAR[name] + 1, 0:rows] / cols
            for n in range(count):
                wide = min(D, cols - n * D)
                line_s[:, far_at + n * D : far_at + n * D + wide] = total[line + n : line + n + 1, 0:wide] / many
            fresh = line_s[:, 0 : many + cols]
            fresh_r[...] = jnp.sum(fresh, axis=0)
            renewed = decay_rate * old_r[...].reshape(1, many + cols) + (1.0 - decay_rate) * fresh
            near, far = renewed[:, near_at : near_at + many], renewed[:, far_at : far_at + cols]
            mean = jnp.mean(far if name == "table" else near, axis=1, keepdims=True)
            shape = (rows, many)
            mine = lax.broadcasted_iota(jnp.int32, shape, 1) == lax.broadcasted_iota(jnp.int32, shape, 0) + at[0] * rows
            own = jnp.sum(jnp.where(mine, near, 0.0), axis=1, keepdims=True)
            u = g * lax.rsqrt(own / mean) * lax.rsqrt(far)
            u_r[...] = u
            sizes.append(size_of(u))
        ends = []
        for lo, wide, old, moment_r, u_r in ((0, PIN, pat, m_pat, u_pat), (PIN, POUT, ost, m_out, u_out)):
            g = q[lo : lo + wide, 3 * D : 3 * D + 48]
            moment = decay_rate * old[1] + (1.0 - decay_rate) * (g * g + grad_floor)
            moment_r[...] = moment
            u = g * lax.rsqrt(moment)
            u_r[...] = u
            ends.append(size_of(u))
        line = jnp.zeros((1, D), f32)
        for n, value in enumerate([ends[0], *sizes, ends[1]]):
            line = jnp.where(lane == n, value, line)
        for p in range(parts):
            usq[p] = jnp.broadcast_to(line[:, 0:128], (8, 128))
        head[...] = total[SUMS : SUMS + 1, :] * jnp.where(lane == 10, 1.0 / parts, 1.0)

    outs = [((o.shape[0],), f32) for o in olds] + [(s, f32) for s in shapes]
    outs += [((PIN, 48), f32), ((POUT, 48), f32)] * 2 + [((parts, 8, 128), f32), ((1, D), f32)]
    ops = (place, packs, g_time1, g_time2, g_table, g_mod, gq, gm, gf, *olds, patch_state, out_t)
    scratch = [pltpu.VMEM((1, 9 * D + 128), f32)]
    return kernel_call(body, outs, ops, 3.5, scratch=scratch, places="s" + "v" * (len(ops) - 1))


def new_weights(usq, head, counts, images, updates, weights, patch_state, out_t, m_patch, m_out):
    def body(usq_r, head_r, mp, mo, pat, ost, *refs):
        us, ms, news = refs[0:10], refs[10:18], refs[18:26]
        new_p, new_o, loss_r, rms_r = refs[26:]
        total = usq_r[0, 0:1, :]
        for p in range(1, usq_r.shape[0]):
            total = total + usq_r[p, 0:1, :]
        lane = lax.broadcasted_iota(jnp.int32, (1, 128), 1)
        size = jnp.ones((1, 128), f32)
        for n, count in enumerate(counts):
            size = jnp.where(lane == n, float(count), size)
        rms = jnp.sqrt(total / size)
        step = step_rate * jnp.sqrt(head_r[:, 0:128] / size) / jnp.maximum(1.0, rms / clip_level)
        for n in range(8):
            news[n][...] = ms[n][...] - step[:, n + 1 : n + 2] * us[n + 1][...]
        new_p[0] = pat[0] - step[:, 0:1] * us[0][...]
        new_p[1] = mp[...]
        new_o[0] = ost[0] - step[:, 9:10] * us[9][...]
        new_o[1] = mo[...]
        rms_r[...] = jnp.sum(rms[:, 0:10], axis=0)
        loss_r[...] = jnp.sum(head_r[:, 10:11], axis=0) / images

    outs = [(m.shape, f32) for m in weights] + [(patch_state.shape, f32), (out_t.shape, f32), ((1,), f32), ((10,), f32)]
    ops = (usq, head, m_patch, m_out, patch_state, out_t, *updates, *weights)
    return kernel_call(body, outs, ops, 3.5)


def gather_pieces(x):
    near = [x, flip(x, 2), flip(x, 4), flip(x, 6)]
    return near + [flip(a, 1) for a in near]


def stacked_pieces(pieces, after=()):
    def body(*refs):
        for n, ref in enumerate(refs[:-1]):
            refs[-1][n] = ref[...]

    shape = (len(pieces),) + pieces[0].shape
    return kernel_call(body, [(shape, pieces[0].dtype)], pieces, 1, after=after)[0]


def chip_blocks(place, keep, sent, micros, after=()):
    def body(at, keep_r, sent_r, *refs):
        for n, out in enumerate(refs):
            chip = jnp.bitwise_xor(at[0] // 2, n)
            out[...] = (keep_r[chip] + sent_r[chip].astype(f32)).astype(out.dtype)

    shape = keep.shape[1:]
    return kernel_call(body, [(shape, f32)] + [(shape, bf16)] * 3, (place, keep, sent), micros, places="svv", after=after)


def tail_blocks(place, keep, sent, d_mods, after=()):
    side = 4 * MOD_ROWS

    def body(at, keep_r, sent_r, *refs):
        outs, mods = refs[1:5], refs[5]
        for n in range(4):
            mods[n * MOD_ROWS : (n + 1) * MOD_ROWS, :] = refs[0][n]
        for n, out in enumerate(outs):
            chip = jnp.bitwise_xor(at[0] // 2, n)
            value = (keep_r[chip] + sent_r[chip].astype(f32)).astype(out.dtype)
            if n == 0:
                out[...] = value
                continue
            out[0:48, 0:TAIL] = value
            out[48:side, 0:TAIL] = jnp.zeros((side - 48, TAIL), bf16)
            out[:, TAIL:] = mods[...]

    outs = [((48, TAIL), f32)] + [((side, TAIL + MOD_LANES), bf16)] * 3 + [((side, MOD_LANES), bf16)]
    return kernel_call(body, outs, (place, keep, sent, d_mods), 1, places="svvv", after=after)


def tail_sum(place, own, arrived, mods, after=()):
    def body(at, own_r, a, b, c, mod_r, out, all_r):
        total = own_r[...] + a[0:48, 0:TAIL].astype(f32)
        out[...] = (total + (b[0:48, 0:TAIL].astype(f32) + c[0:48, 0:TAIL].astype(f32))).astype(bf16)
        chip = at[0] // 2
        all_r[chip] = mod_r[...]
        for n, ref in enumerate((a, b, c)):
            all_r[jnp.bitwise_xor(chip, n + 1)] = ref[:, TAIL:]

    outs = [((48, TAIL), bf16), ((4,) + mods.shape, bf16)]
    return kernel_call(body, outs, (place, own, *arrived, mods), 1, places="svvvvv", after=after)


Z_LANES = 384 + 384 + 128


def copy_blocks(place, parts, after=()):
    def body(at, a, b, c, d, own, one, two, three, cuts):
        total = (a[...] + b[...].astype(f32)) + (c[...].astype(f32) + d[...].astype(f32))
        none = jnp.zeros((48, 32), f32)
        for j in range(4):
            cuts[j, :, 0:384] = total[:, D + j * 384 : D + (j + 1) * 384]
            cuts[j, :, 384:768] = total[:, D + FF + j * 384 : D + FF + (j + 1) * 384]
            cuts[j, :, 768:] = jnp.concatenate([total[:, j * 96 : (j + 1) * 96], none], axis=1)
        for n, out in enumerate((own, one, two, three)):
            out[...] = cuts[jnp.bitwise_xor(at[2], n)].astype(out.dtype)

    outs = [((48, Z_LANES), f32)] + [((48, Z_LANES), bf16)] * 3
    return kernel_call(body, outs, (place, *parts), 2, scratch=[pltpu.VMEM((4, 48, Z_LANES), f32)], places="svvvv", after=after)


def four_sum(parts, after=()):
    def body(a, b, c, d, out):
        out[...] = ((a[...].astype(f32) + b[...].astype(f32)) + (c[...].astype(f32) + d[...].astype(f32))).astype(bf16)

    return kernel_call(body, [(parts[0].shape, bf16)], parts, 1, after=after)[0]


def other_copies(total):
    return (total, flip(total, 1, "rep"), flip(total, 2, "rep"), flip(total, 3, "rep"))


def eight_by_four(
    latents, noise, tsteps, labels, patch_state, time1_w, time2_w, table_t, mod_w, qkv_w, proj_w, fc1_w, fc2_w, out_t, olds, place, plan, grid, times
):
    reps, parts = 4, 8
    images = tsteps.shape[0]
    bundle = bundle_rows(tsteps, labels, time1_w, time2_w)
    pieces = gather_pieces(bundle)
    w_own, mod16, tab16, sums = cast_weights(
        patch_state, out_t, time1_w, time2_w, table_t, mod_w, qkv_w, proj_w, fc1_w, fc2_w, after=pieces[1:4]
    )
    w_near = [flip(w_own, k) for k in (2, 4, 6)]
    w_core = flip(w_own, 1)
    shares, w1, w2 = modulation_shares(place, pieces, times, tab16, mod16, images)
    shares = lax.all_to_all(shares, "fsdp", 0, 0)
    w_pieces = [w_own, *w_near, w_core, flip(stacked_pieces(w_near, after=(shares,)), 1)]

    w_qkv, head, mod, con, noisy, hidden0, attn16, qkv16, totals, mixture16 = attention_forward(
        tsteps, latents, noise, plan, grid, w_pieces, shares, place
    )
    keep, send, g_last, d_mix16, d_h1, d_mod, loss_tile = mlp_pass(
        noise, con, mod, hidden0, mixture16, head, w_pieces, place
    )
    send = flip(send, 1)
    d_qkv16 = heads_back(qkv16, totals, d_mix16, after=(keep,))
    blocks = chip_blocks(place, keep, send, 2, after=(d_qkv16,))
    q_keep, q_send, d_mod16 = attention_back(
        place, mod, hidden0, attn16, d_qkv16, d_h1, d_mod, w_qkv, noisy, g_last, loss_tile, bundle, after=(blocks[1],)
    )
    q_send = flip(q_send, 1)
    arrived = [flip(blocks[n], 2 * n) for n in range(1, 4)]
    cuts = copy_blocks(place, [blocks[0]] + arrived)
    q_own, *q_blocks, d_mods = tail_blocks(place, q_keep, q_send, lax.all_to_all(d_mod16, "rep", 0, 0), after=(cuts[1],))
    q_sum, own_mod = tail_sum(place, q_own, [flip(q_blocks[n], 2 * (n + 1)) for n in range(3)], d_mods)
    oth_mod = flip(own_mod, 1)
    g_mod, g_table, d_time, loss, feat16, act16_t, time_slope, q_sum = condition_back(
        place, own_mod, oth_mod, w1, w2, times, tab16, mod16, q_sum, reps, parts, images
    )
    mid = four_sum([cuts[0]] + [flip(cuts[n], n, "rep") for n in range(1, 4)])
    mid = other_copies(mid)
    tail = other_copies(q_sum)
    gm, gf, pack = sums_early(place, mid)
    d_time = lax.all_to_all(d_time, "fsdp", 0, 0)
    pack = sums_middle(pack, g_table, g_mod, sums, loss)
    g_time1, g_time2 = time_back(d_time, w2, act16_t, time_slope, feat16)
    gq, pack = sums_late(pack, tail, g_time1, g_time2)
    packs = gather_rows(pack).reshape(parts, LINES, D)
    result = scaled_updates(place, packs, g_time1, g_time2, g_table, g_mod, gq, gm, gf, olds, patch_state, out_t)
    fresh, updates = result[:8], result[8:16]
    u_patch, u_out, m_patch, m_out, usq, sums = result[16:]
    usq = lax.all_to_all(usq, "fsdp", 0, 0)
    weights = (time1_w, time2_w, table_t, mod_w, qkv_w, proj_w, fc1_w, fc2_w)
    counts = [w.size * parts for w in (patch_state[0], *weights, out_t[0])]
    *news, new_patch, new_out, loss, rms = new_weights(
        usq, sums, counts, images * reps * parts, (u_patch, *updates, u_out), weights, patch_state, out_t, m_patch, m_out
    )
    news[2] = news[2].T
    outs = [new_patch]
    for n in range(8):
        outs += [news[n], fresh[n]]
    return tuple(outs) + (new_out.transpose(0, 2, 1), loss.reshape(()), rms)


def per_device(
    latents,
    noise,
    timesteps,
    labels,
    patch_state,
    time1_w,
    time1_f,
    time2_w,
    time2_f,
    table_w,
    table_f,
    mod_w,
    mod_f,
    qkv_w,
    qkv_f,
    proj_w,
    proj_f,
    fc1_w,
    fc1_f,
    fc2_w,
    fc2_f,
    out_state,
):
    reps, parts = lax.axis_size("rep"), lax.axis_size("fsdp")
    position = lax.axis_index("fsdp")
    masters = (patch_state[0], time1_w, time2_w, table_w, mod_w, qkv_w, proj_w, fc1_w, fc2_w, out_state[0])
    images = latents.shape[0] * latents.shape[1]
    latents = latents.reshape(images, TOK_IMG, PIN).transpose(0, 2, 1)
    noise = noise.reshape(images, TOK_IMG, PIN).transpose(0, 2, 1)
    out_t = out_state.transpose(0, 2, 1)
    tsteps = timesteps.reshape(images)
    labels = labels.reshape(images)
    own_d = D // parts
    own_t = TFREQ // parts
    place = jnp.stack([position, position & 1, lax.axis_index("rep")]).astype(jnp.int32)
    plan, grid = jnp.asarray(plan_table()), jnp.asarray(place_table())
    times = jnp.asarray(time_table(), bf16)
    olds = (time1_f, time2_f, table_f, mod_f, qkv_f, proj_f, fc1_f, fc2_f)

    if parts == 8 and reps == 4:
        return eight_by_four(
            latents, noise, tsteps, labels, patch_state, time1_w, time2_w, table_w.T, mod_w, qkv_w, proj_w, fc1_w, fc2_w, out_t, olds, place, plan, grid, times
        )

    info = jnp.stack([tsteps // 32, tsteps % 32, labels // 32, labels % 32]).reshape(1, 4 * images)
    info_row = jnp.pad(info.astype(bf16), ((0, 0), (0, D - 4 * images)))
    bundle = jnp.concatenate([time1_w.astype(bf16), time2_w.astype(bf16), info_row], axis=0)
    bundle = gather_rows(bundle).reshape(parts, own_t + own_d + 1, D)
    w_time1 = bundle[:, :own_t].reshape(TFREQ, D)
    w_time2 = bundle[:, own_t : own_t + own_d].reshape(D, D)
    info_rep = bundle[:, own_t + own_d, : 4 * images]

    head = lax.all_gather(jnp.concatenate([patch_state[0], out_t[0]], axis=0).astype(bf16), "fsdp", axis=1, tiled=True)
    w_rows = gather_rows(jnp.concatenate([qkv_w, proj_w, fc1_w], axis=1).astype(bf16))
    w_fc2 = gather_rows(fc2_w.astype(bf16))
    w_qkv, w_proj, w_fc1 = w_rows[:, : 3 * D], w_rows[:, 3 * D : 4 * D], w_rows[:, 4 * D :]

    info_all = rep_gather(info_rep).reshape(reps * parts, 4, images).astype(jnp.int32)
    w_mod16 = mod_w.astype(bf16)
    w_table16 = table_w.astype(bf16)

    def condition_path(info_any):
        ts = (info_any[:, 0] * 32 + info_any[:, 1]).reshape(-1)
        lab = (info_any[:, 2] * 32 + info_any[:, 3]).reshape(-1)
        feats16 = dot(pick(ts, STEPS), times).astype(bf16)
        time_act, time_slope = silu_pair(dot(feats16, w_time1))
        time_act16 = time_act.astype(bf16)
        time_emb = dot(time_act16, w_time2)
        own_emb = lax.dynamic_slice(time_emb, (0, position * own_d), (time_emb.shape[0], own_d))
        picks = pick(lab, CLASSES)
        cond_act, cond_slope = silu_pair(own_emb + dot(picks, w_table16))
        return feats16, time_act16, time_slope, picks, cond_act.astype(bf16), cond_slope

    info_here = info_rep.reshape(parts, 4, images).astype(jnp.int32)
    cond_here = condition_path(info_here)[4]
    shares = dot(cond_here, w_mod16).reshape(parts, 8, images * D)
    shares = lax.all_to_all(shares, "fsdp", 0, 0, tiled=True)

    mod, con, noisy, hidden0, attn16, qkv16, totals, mixture16 = attention_forward(
        tsteps, latents, noise, plan, grid, (w_qkv, head), shares, place
    )
    g_proj, g_fc1, g_fc2, g_last, d_mix16, d_h1, d_mod, loss_tile = mlp_pass(
        noise, con, mod, hidden0, mixture16, head, (w_proj, w_fc1, w_fc2), place
    )
    loss_part = loss_tile[0, 0]
    g_tail, g_head, d_mod16 = attention_back(
        place, mod, hidden0, attn16, heads_back(qkv16, totals, d_mix16), d_h1, d_mod, w_qkv, noisy, g_last, loss_tile, None
    )

    d_mod_all = rep_gather(d_mod16).reshape(1, -1)
    d_mod_all = gather_rows(d_mod_all).reshape(parts, reps, images, 8 * D)
    d_mod_all = d_mod_all.transpose(1, 0, 2, 3).reshape(reps * parts * images, 8 * D)
    feats16, time_act16, time_slope, picks, cond16, cond_slope = condition_path(info_all)
    d_cond = dot_nt(d_mod_all, w_mod16) * cond_slope
    g_mod = dot_tn(cond16, d_mod_all)
    g_table = lax.dot_general(
        picks.astype(f32), d_cond, (((0,), (0,)), ((), ())), precision=lax.Precision.HIGHEST
    )
    d_time16 = lax.all_gather(d_cond.astype(bf16), "fsdp", axis=0)
    d_time16 = d_time16.transpose(1, 0, 2).reshape(-1, D)
    own_act16 = lax.dynamic_slice(time_act16, (0, position * own_d), (time_act16.shape[0], own_d))
    g_time2 = dot_tn(own_act16, d_time16)
    d_hid16 = (dot_nt(d_time16, w_time2) * time_slope).astype(bf16)
    own_feat16 = lax.dynamic_slice(feats16, (0, position * own_t), (feats16.shape[0], own_t))
    g_time1 = dot_tn(own_feat16, d_hid16)

    g_head = lax.psum_scatter(g_head, "fsdp", scatter_dimension=1, tiled=True)
    g_tail, g_proj, g_fc1, g_fc2 = (sum_scatter(g) for g in (g_tail, g_proj, g_fc1, g_fc2))
    g_proj, g_fc1, g_fc2 = (rep_sum(g.astype(bf16)) for g in (g_proj, g_fc1, g_fc2))
    g_tail = rep_sum(g_tail.astype(bf16))
    g_head = rep_sum(g_head)
    grads = (
        g_head[:PIN],
        g_time1,
        g_time2,
        g_table,
        g_mod,
        g_tail,
        g_proj,
        g_fc1,
        g_fc2,
        g_head[PIN:].T,
    )
    loss_part = lax.psum(loss_part, "rep")
    dims = (0, 0, 1, 0, 0, 0, 0, 0)

    packs = []
    for slot in range(8):
        grad, dim = grads[slot + 1], dims[slot]
        squares = grad * grad + grad_floor
        near = jnp.sum(squares, axis=1 - dim)
        far = jnp.sum(squares, axis=dim)
        spread = lax.dynamic_update_slice(
            jnp.zeros((near.shape[0] * parts,), f32), near / far.shape[0], (position * near.shape[0],)
        )
        far = far / (near.shape[0] * parts)
        packs.append(jnp.concatenate([spread, far] if dim == 0 else [far, spread]))
    tail = jnp.stack([jnp.sum(m * m) for m in masters] + [loss_part])
    lengths = [pack.shape[0] for pack in packs]
    totals = lax.psum(jnp.concatenate(packs + [tail]), "fsdp")
    fresh = []
    start = 0
    for length in lengths:
        fresh.append(totals[start : start + length])
        start += length
    square_tot = totals[start : start + 10]
    loss = totals[start + 10] / (images * reps * parts)

    updates, counts = [], []
    plain = []
    for slot in range(10):
        grad = grads[slot]
        if slot in (0, 9):
            state = patch_state if slot == 0 else out_state
            moment = decay_rate * state[1] + (1.0 - decay_rate) * (grad * grad + grad_floor)
            plain.append(moment)
            updates.append(grad * lax.rsqrt(moment))
            counts.append(grad.size * parts)
            continue
        dim = dims[slot - 1]
        renewed = decay_rate * olds[slot - 1] + (1.0 - decay_rate) * fresh[slot - 1]
        rows = grad.shape[0] * (parts if dim == 0 else 1)
        row, col = renewed[:rows], renewed[rows:]
        mean_row = jnp.mean(row)
        if dim == 0:
            row = lax.dynamic_slice(row, (position * grad.shape[0],), (grad.shape[0],))
        else:
            col = lax.dynamic_slice(col, (position * grad.shape[1],), (grad.shape[1],))
        updates.append(grad * lax.rsqrt(row[:, None] * col[None, :] / mean_row))
        counts.append(grad.size * parts)
    update_tot = lax.psum(jnp.stack([jnp.sum(u * u) for u in updates]), "fsdp")
    sizes = np.asarray(counts, np.float32)
    size_rms = jnp.sqrt(update_tot / sizes)
    factor = step_rate * jnp.sqrt(square_tot / sizes) / jnp.maximum(1.0, size_rms / clip_level)
    new = [masters[s] - factor[s] * updates[s] for s in range(10)]
    result = [jnp.stack([new[0], plain[0]])]
    for slot in range(8):
        result += [new[slot + 1], fresh[slot]]
    return tuple(result) + (jnp.stack([new[9], plain[1]]), loss, size_rms)


def solution(mesh):
    images = P(None, ("rep", "fsdp"), None, None)
    singles = P(None, ("rep", "fsdp"))
    rows, cols = P("fsdp", None), P(None, "fsdp")
    placed = (images, images, singles, singles, P(None, None, "fsdp"))
    placed += (rows, P(), rows, P(), cols, P()) + (rows, P()) * 5 + (P(None, "fsdp", None),)
    results = (P(None, None, "fsdp"), rows, P(), rows, P(), cols, P()) + (rows, P()) * 5
    results += (P(None, "fsdp", None), P(), P())
    return jax.shard_map(per_device, mesh=mesh, in_specs=placed, out_specs=results, check_vma=False)
```

```python
import math

import jax
import jax.numpy as jnp
import numpy as np
from jax import lax
from jax.experimental import pallas as pl
from jax.experimental.pallas import tpu as pltpu
from jax.sharding import PartitionSpec as P

D = 384
HEADS = 6
HEAD_DIM = 64
FF = 1536
TFREQ = 256
GRID = 16
PIN = 16
POUT = 32
CLASSES = 1001
STEPS = 1000
TOK_IMG = 256

decay_rate = 0.5
clip_level = 1.0
step_rate = 0.5
grad_floor = 1e-30
norm_floor = 1e-06
f32 = jnp.float32
bf16 = jnp.bfloat16


def plan_table():
    s = np.arange(STEPS, dtype=np.float64)
    beta = 1e-4 + (0.02 - 1e-4) * s / (STEPS - 1)
    lbar = np.cumsum(np.log1p(-beta))
    lprev = np.concatenate([[0.0], lbar[:-1]])
    post = beta * -np.expm1(lprev) / -np.expm1(lbar)
    post[0] = post[1]
    remain = -np.expm1(lbar)
    coef = beta * beta / ((1.0 - beta) * remain)
    rows = [np.exp(0.5 * lbar), np.sqrt(remain), np.log(beta), np.log(post), coef]
    return np.stack(rows + [np.zeros(STEPS)] * 3, axis=1).astype(np.float32)


def time_table():
    half = TFREQ // 2
    freq = np.exp(np.float32(-math.log(10000.0)) * np.arange(half, dtype=np.float32) / np.float32(half)).astype(np.float32)
    angles = np.arange(STEPS, dtype=np.float32)[:, None] * freq[None, :]
    wide = angles.astype(np.float64)
    return np.concatenate([np.cos(wide), np.sin(wide)], axis=1).astype(np.float32)


def place_table():
    quarter = D // 4
    om = np.exp(np.float32(-math.log(10000.0)) * np.arange(quarter, dtype=np.float32) / np.float32(quarter)).astype(np.float32)
    n = np.arange(TOK_IMG)
    row = ((n // GRID).astype(np.float32)[:, None] * om[None, :]).astype(np.float64)
    col = ((n % GRID).astype(np.float32)[:, None] * om[None, :]).astype(np.float64)
    return np.concatenate([np.sin(row), np.cos(row), np.sin(col), np.cos(col)], axis=1).astype(np.float32)


def pick(index, count):
    return (index[:, None] == jnp.arange(count, dtype=jnp.int32)[None, :]).astype(bf16)


def silu_pair(v):
    s = 1.0 / (1.0 + jnp.exp(-v))
    return v * s, s * (1.0 + v * (1.0 - s))


def norm_parts(x):
    mean = jnp.mean(x, axis=-1, keepdims=True)
    cen = x - mean
    inv = lax.rsqrt(jnp.mean(cen * cen, axis=-1, keepdims=True) + norm_floor)
    return cen * inv, inv


def norm_back(d_norm, normed, inv):
    a = jnp.mean(d_norm, axis=-1, keepdims=True)
    b = jnp.mean(d_norm * normed, axis=-1, keepdims=True)
    return inv * (d_norm - a - normed * b)


def dot(a, b):
    return jnp.dot(a, b, preferred_element_type=f32)


def dot_nt(a, b):
    return lax.dot_general(a, b, (((1,), (1,)), ((), ())), preferred_element_type=f32)


def dot_tn(a, b):
    return lax.dot_general(a, b, (((0,), (0,)), ((), ())), preferred_element_type=f32)


def flip(x, bit, axis="fsdp"):
    size = lax.axis_size(axis)
    return lax.ppermute(x, axis, [(i, i ^ bit) for i in range(size)])


def rep_gather(x):
    size = lax.axis_size("rep")
    me = lax.axis_index("rep")
    parts = jnp.stack([x] + [flip(x, k, "rep") for k in range(1, size)])
    return jnp.stack([lax.dynamic_index_in_dim(parts, me ^ j, 0, keepdims=False) for j in range(size)])


def rep_sum(x16):
    size = lax.axis_size("rep")
    parts = [x16.astype(f32)] + [flip(x16, k, "rep").astype(f32) for k in range(1, size)]
    while len(parts) > 1:
        parts = [parts[i] + parts[i + 1] for i in range(0, len(parts), 2)]
    return parts[0]


def sum_scatter(grad):
    return lax.psum_scatter(grad, "fsdp", scatter_dimension=0, tiled=True)


def gather_rows(x):
    return lax.all_gather(x, "fsdp", axis=0, tiled=True)


def lane_half(shape, which):
    lane = lax.broadcasted_iota(jnp.int32, shape, 1)
    return (lane < HEAD_DIM) if which == 0 else (lane >= HEAD_DIM)


FLOPS_US = 1_150_000_000


def kernel_call(body, outs, operands, micros, scratch=(), places=None, after=(), room=16):
    vmem = pl.BlockSpec(memory_space=pltpu.VMEM)
    smem = pl.BlockSpec(memory_space=pltpu.SMEM)
    places = places or "v" * len(operands)
    count = len(operands)

    def run(*refs):
        body(*refs[:count], *refs[count + len(after) :])

    return pl.pallas_call(
        run,
        out_shape=[jax.ShapeDtypeStruct(s, t) for s, t in outs],
        in_specs=[{"s": smem, "v": vmem, "h": pl.BlockSpec(memory_space=pltpu.HBM)}[p] for p in places] + [pl.BlockSpec(memory_space=pl.ANY)] * len(after),
        out_specs=[vmem] * len(outs),
        scratch_shapes=list(scratch),
        compiler_params=pltpu.CompilerParams(vmem_limit_bytes=room * 2**20),
        cost_estimate=pl.CostEstimate(flops=int(micros * FLOPS_US), bytes_accessed=1_000_000, transcendentals=0),
    )(*(pltpu.with_memory_space_constraint(x, pltpu.HBM) if p == "h" else x for x, p in zip(operands, places)), *after)


HEAD = PIN + POUT
CAST_ROOM = 48
INFO = 80
BUNDLE = 96
TAIL = 3 * D + 128
SENT = TAIL + D + 2 * FF


def piece_owner(at, n):
    return jnp.bitwise_xor(at[0], 2 * (n % 4) + n // 4)


def shards_of(refs):
    own, near, core, far = refs[:4]
    return [own] + [near.at[n] for n in range(3)] + [core] + [far.at[n] for n in range(3)]


def attention_forward(tsteps, lat, noi, plan, grid, weights, shares, place, after=()):
    images = lat.shape[0]
    fast = len(weights) == 4

    def body(ts, at, lat_r, noi_r, plan_r, grid_r, share_r, *refs):
        if fast:
            wq_r, head_r, head_s = refs[4], refs[5], refs[-1]
            shards = shards_of(refs)
            for n in range(8):
                owner = piece_owner(at, n)
                rows = pl.ds(pl.multiple_of(owner * 48, 48), 48)
                wq_r[rows, :] = shards[n][:, 0 : 3 * D]
                head_s[owner] = shards[n][:, 3 * D : 3 * D + 48]
            for p in range(8):
                head_r[:, p * 48 : (p + 1) * 48] = head_s[p]
            refs = refs[6:-1]
        else:
            wq_r, head_r = refs[:2]
            refs = refs[2:]
        mod_r, con_r, noisy_r, h0_r, attn_r, qkv_r, total_r, mix_r = refs
        total = share_r[0]
        for p in range(1, share_r.shape[0]):
            total = total + share_r[p]
        width = total.shape[1]
        for n in range(8):
            i, col = divmod(n * width, 8 * D)
            mod_r[i : i + 1, col : col + width] = total[n : n + 1]
        for i in range(images):
            row = plan_r[pl.ds(ts[i], 1), :]
            con_r[i : i + 1, :] = row
            noisy = (row[:, 0:1] * lat_r[i] + row[:, 1:2] * noi_r[i]).astype(bf16)
            noisy_r[i] = noisy
            h0 = dot_tn(noisy, head_r[0:PIN, :]) + grid_r[...]
            h0_r[i] = h0
            norm, _ = norm_parts(h0)
            attn = (norm * (1.0 + mod_r[i : i + 1, D : 2 * D]) + mod_r[i : i + 1, 0:D]).astype(bf16)
            attn_r[i] = attn
            for part in range(3):
                qkv_r[i, :, part * D : (part + 1) * D] = dot(attn, wq_r[:, part * D : (part + 1) * D]).astype(bf16)
        lane = lax.broadcasted_iota(jnp.int32, (TOK_IMG, 128), 1)
        logs = [jnp.zeros((TOK_IMG, 128), f32)] * images
        for pair in range(HEADS // 2):
            for i in range(images):
                q = qkv_r[i, :, pair * 128 : pair * 128 + 128]
                k = qkv_r[i, :, D + pair * 128 : D + pair * 128 + 128]
                v = qkv_r[i, :, 2 * D + pair * 128 : 2 * D + pair * 128 + 128]
                mixed = None
                for half in range(2):
                    own = lane_half(q.shape, half)
                    zero = jnp.zeros_like(q)
                    s = dot_nt(jnp.where(own, q, zero), k) * 0.125
                    top = jnp.max(s, axis=-1, keepdims=True)
                    p = jnp.exp(s - top)
                    total = jnp.sum(p, axis=-1, keepdims=True)
                    p = p * (1.0 / total)
                    logs[i] = jnp.where(lane == pair * 2 + half, top + jnp.log(total), logs[i])
                    o = dot(p.astype(bf16), jnp.where(own, v, zero))
                    mixed = o if mixed is None else mixed + o
                mix_r[i, :, pair * 128 : pair * 128 + 128] = mixed.astype(bf16)
        for i in range(images):
            total_r[i] = logs[i]

    outs = [
        ((images, 8 * D), f32),
        ((images, 8), f32),
        ((images, PIN, TOK_IMG), bf16),
        ((images, TOK_IMG, D), f32),
        ((images, TOK_IMG, D), bf16),
        ((images, TOK_IMG, 3 * D), bf16),
        ((images, TOK_IMG, 128), f32),
        ((images, TOK_IMG, D), bf16),
    ]
    scratch = []
    if fast:
        outs = [((D, 3 * D), bf16), ((HEAD, D), bf16)] + outs
        scratch = [pltpu.VMEM((8, HEAD, 48), bf16)]
    ops = (tsteps, place, lat, noi, plan, grid, shares, *weights)
    return kernel_call(
        body, outs, ops, 8, scratch=scratch, places="ss" + "v" * (len(ops) - 2), after=after
    )


BLOCK = 384
WIDE = 768


def mlp_pass(noi, con, mod, h0_all, mix_all, head, weights, place, after=()):
    images = noi.shape[0]
    bend_scale = math.sqrt(2.0 / math.pi)
    share = 1.0 / (TOK_IMG * PIN)

    fast = len(weights) == 4

    def body(at, noi_r, con_r, mod_r, h0_r, mix_r, head_r, *refs):
        if fast:
            wp_r, w1_r, w2_r = refs[-3:]
            shards = shards_of(refs)
            for n in range(8):
                owner = piece_owner(at, n)
                rows = pl.ds(pl.multiple_of(owner * 48, 48), 48)
                wp_r[rows, :] = shards[n][:, TAIL : TAIL + D]
                w1_r[rows, :] = shards[n][:, TAIL + D : TAIL + D + FF]
                for b in range(4):
                    w2_r[pl.ds(pl.multiple_of(owner * 192 + b * 48, 48), 48), :] = shards[n][:, TAIL + D + FF + b * D : TAIL + D + FF + (b + 1) * D]
            refs = refs[4:-3]
        else:
            wp_r, w1_r, w2_r = refs[:3]
            refs = refs[3:]
        g_refs, refs = refs[: 2 if fast else 3], refs[2 if fast else 3 :]
        glast_r, dmix_r, dh1_r, dmod_r, loss_r, mlp_r, act_r, dinner_r, douter_r, dbr_r, slope_r = refs
        g_last = None
        wo = head_r[PIN:HEAD, :]
        losses = jnp.zeros((1, 1), f32)
        dmod_r[:, 0 : 2 * D] = jnp.zeros((images, 2 * D), f32)
        for i in range(images):
            def m(slot):
                return mod_r[i : i + 1, slot * D : (slot + 1) * D]

            def put(slot, value):
                dmod_r[i : i + 1, slot * D : (slot + 1) * D] = jnp.sum(value, axis=0, keepdims=True)

            branch = dot(mix_r[i], wp_r[...])
            h1 = h0_r[i] + m(2) * branch
            norm1, inv1 = norm_parts(h1)
            mlp = (norm1 * (1.0 + m(4)) + m(3)).astype(bf16)
            tokens = slice(i * TOK_IMG, (i + 1) * TOK_IMG)
            mlp_r[tokens, :] = mlp
            outer = None
            for b in range(FF // WIDE):
                cols = slice(b * WIDE, (b + 1) * WIDE)
                x = dot(mlp, w1_r[:, cols])
                sq = x * x
                t = jnp.tanh(bend_scale * x * (1.0 + 0.044715 * sq))
                hx = 0.5 * x
                act = (hx * (1.0 + t)).astype(bf16)
                act_r[tokens, cols] = act
                slope_r[:, cols] = 0.5 * (1.0 + t) + hx * (1.0 - t * t) * (bend_scale + (3 * 0.044715 * bend_scale) * sq)
                part = dot(act, w2_r[cols, :])
                outer = part if outer is None else outer + part
            h2 = h1 + m(5) * outer
            norm2, inv2 = norm_parts(h2)
            fin = (norm2 * (1.0 + m(7)) + m(6)).astype(bf16)
            out = dot_nt(wo, fin)
            log_beta, post_log, coef = (con_r[i : i + 1, n : n + 1] for n in (2, 3, 4))
            miss = out[:PIN] - noi_r[i]
            mixing = (out[PIN:] + 1.0) * 0.5
            log_var = mixing * log_beta + (1.0 - mixing) * post_log
            ratio = jnp.exp(post_log - log_var)
            square = miss * miss
            weigh = coef * jnp.exp(-log_var)
            terms = square + 0.5 * (-1.0 + log_var - post_log + ratio + weigh * square)
            losses += share * jnp.sum(jnp.sum(terms, axis=0, keepdims=True), axis=1, keepdims=True)
            d_guess = share * miss * (2.0 + weigh)
            d_mixed = (share * 0.25) * (1.0 - ratio - weigh * square) * (log_beta - post_log)
            d_out = jnp.concatenate([d_guess, d_mixed], axis=0).astype(bf16)
            piece = dot(d_out, fin)
            g_last = piece if g_last is None else g_last + piece
            d_fin = dot_tn(d_out, wo)
            put(6, d_fin)
            put(7, d_fin * norm2)
            d_h2 = norm_back(d_fin * (1.0 + m(7)), norm2, inv2)
            put(5, d_h2 * outer)
            d_outer = (m(5) * d_h2).astype(bf16)
            douter_r[tokens, :] = d_outer
            d_mlp = None
            for b in range(FF // WIDE):
                cols = slice(b * WIDE, (b + 1) * WIDE)
                d_in = (dot_nt(d_outer, w2_r[cols, :]) * slope_r[:, cols]).astype(bf16)
                dinner_r[tokens, cols] = d_in
                part = dot_nt(d_in, w1_r[:, cols])
                d_mlp = part if d_mlp is None else d_mlp + part
            put(3, d_mlp)
            put(4, d_mlp * norm1)
            d_h1 = d_h2 + norm_back(d_mlp * (1.0 + m(4)), norm1, inv1)
            dh1_r[i] = d_h1
            put(2, d_h1 * branch)
            d_br = (m(2) * d_h1).astype(bf16)
            dbr_r[tokens, :] = d_br
            dmix_r[i] = dot_nt(d_br, wp_r[...]).astype(bf16)
        loss_r[...] = jnp.broadcast_to(losses, loss_r.shape)
        glast_r[...] = g_last
        mix = jnp.concatenate([mix_r[i] for i in range(images)], axis=0)
        if not fast:
            g_refs[0][...] = dot_tn(mix, dbr_r[...])
        else:
            deal_rows(*g_refs, dot_tn(mix, dbr_r[...]), at[1], 0)
        for b in range(FF // BLOCK):
            cols = slice(b * BLOCK, (b + 1) * BLOCK)
            g_in = dot_tn(mlp_r[...], dinner_r[:, cols])
            g_out = dot_tn(act_r[:, cols], douter_r[...])
            if not fast:
                g_refs[1][:, cols] = g_in
                g_refs[2][cols, :] = g_out
                continue
            deal_rows(*g_refs, g_in, at[1], D + b * BLOCK)
            deal(*g_refs, g_out[0:192], g_out[192:384], at[1], b, D + FF, 4)

    if fast:
        outs = [((4, 48, D + 2 * FF), f32), ((4, 48, D + 2 * FF), bf16)]
    else:
        outs = [((D, D), f32), ((D, FF), f32), ((FF, D), f32)]
    outs += [
        ((POUT, D), f32),
        ((images, TOK_IMG, D), bf16),
        ((images, TOK_IMG, D), f32),
        ((images, 8 * D), f32),
        ((8, 128), f32),
    ]
    ops = (place, noi, con, mod, h0_all, mix_all, head, *weights)
    many = images * TOK_IMG
    scratch = [pltpu.VMEM((many, n), bf16) for n in (D, FF, FF, D, D)] + [pltpu.VMEM((TOK_IMG, FF), f32)]
    if fast:
        scratch += [pltpu.VMEM(shape, bf16) for shape in ((D, D), (D, FF), (FF, D))]
    return kernel_call(body, outs, ops, 13, scratch=scratch, places="s" + "v" * (len(ops) - 1), after=after, room=32)


def deal(keep_r, send_r, left, right, core, chip, lanes, blocks=1):
    rows, width = left.shape[0] // blocks, left.shape[1]
    kept = jnp.where(core == 0, left, right)
    sent = jnp.where(core == 0, right, left).astype(bf16)
    for b in range(blocks):
        cols = slice(lanes + b * width, lanes + (b + 1) * width)
        keep_r[chip, :, cols] = kept[b * rows : (b + 1) * rows]
        send_r[chip, :, cols] = sent[b * rows : (b + 1) * rows]


def deal_rows(keep_r, send_r, grad, core, lanes):
    for c in range(4):
        deal(keep_r, send_r, grad[c * 96 : c * 96 + 48], grad[c * 96 + 48 : c * 96 + 96], core, c, lanes)


MOD_ROWS, MOD_LANES = 16, 512


def heads_back(qkv_all, total_all, dmix_all, after=()):
    images = qkv_all.shape[0]

    def body(qkv_r, total_r, dmix_r, dqkv_r):
        for pair in range(HEADS // 2):
            lanes = slice(pair * 128, pair * 128 + 128)
            for i in range(images):
                q = qkv_r[i, :, pair * 128 : pair * 128 + 128]
                k = qkv_r[i, :, D + pair * 128 : D + pair * 128 + 128]
                v = qkv_r[i, :, 2 * D + pair * 128 : 2 * D + pair * 128 + 128]
                do = dmix_r[i, :, lanes]
                dq = dk = dv = None
                for half in range(2):
                    own = lane_half(q.shape, half)
                    zero = jnp.zeros_like(q)
                    do_h = jnp.where(own, do, zero)
                    q_h = jnp.where(own, q, zero)
                    head = pair * 2 + half
                    p = jnp.exp(dot_nt(q_h, k) * 0.125 - total_r[i, :, head : head + 1])
                    dp = dot_nt(do_h, v)
                    ds = (p * (dp - jnp.sum(dp * p, axis=-1, keepdims=True))).astype(bf16)
                    a = dot(ds, jnp.where(own, k, zero))
                    b = dot_tn(ds, q_h)
                    c = dot_tn(p.astype(bf16), do_h)
                    dq, dk, dv = (a, b, c) if dq is None else (dq + a, dk + b, dv + c)
                rows = slice(i * TOK_IMG, (i + 1) * TOK_IMG)
                for part, value in enumerate((dq * 0.125, dk * 0.125, dv)):
                    dqkv_r[rows, part * D + pair * 128 : part * D + pair * 128 + 128] = value.astype(bf16)

    outs = [((images * TOK_IMG, 3 * D), bf16)]
    return kernel_call(body, outs, (qkv_all, total_all, dmix_all), 4, after=after)[0]


def attention_back(place, mod, h0_all, attn_all, dqkv, dh1_all, dmod_all, w_qkv, noisy_all, g_last, loss_tile, info, after=()):
    images = mod.shape[0]

    def body(at, mod_r, h0_r, attn_r, dqkv_r, dh1_r, dmod_in, wq_r, noisy_r, last_r, loss_r, *refs):
        *g_refs, dmod_r, line = refs if info is None else refs[1:]
        patch = None
        for i in range(images):
            rows = slice(i * TOK_IMG, (i + 1) * TOK_IMG)
            d_attn = None
            for part in range(3):
                cols = slice(part * D, (part + 1) * D)
                piece = dot_nt(dqkv_r[rows, cols], wq_r[:, cols])
                d_attn = piece if d_attn is None else d_attn + piece
            norm, inv = norm_parts(h0_r[i])
            line[i : i + 1, 0:D] = jnp.sum(d_attn, axis=0, keepdims=True)
            line[i : i + 1, D : 2 * D] = jnp.sum(d_attn * norm, axis=0, keepdims=True)
            line[i : i + 1, 2 * D :] = dmod_in[i : i + 1, 2 * D :]
            d_h0 = (dh1_r[i] + norm_back(d_attn * (1.0 + mod_r[i : i + 1, D : 2 * D]), norm, inv)).astype(bf16)
            piece = dot(noisy_r[i], d_h0)
            patch = piece if patch is None else patch + piece
        if info is not None:
            each = 8 * D // MOD_LANES
            block = [line[i : i + 1, n * MOD_LANES : (n + 1) * MOD_LANES] for i in range(images) for n in range(each)]
            lane = lax.broadcasted_iota(jnp.int32, (1, MOD_LANES), 1)
            loss = loss_r[0:1, 0:1]
            high = loss.astype(bf16).astype(f32)
            mid = (loss - high).astype(bf16).astype(f32)
            low = loss - high - mid
            block.append(jnp.where(lane == 0, high, jnp.where(lane == 1, mid, jnp.where(lane == 2, low, 0.0))))
            told = refs[0][INFO:BUNDLE, :].astype(f32)[0:1]
            block.append(jnp.concatenate([told, jnp.zeros((1, MOD_LANES - D), f32)], axis=1))
            block.append(jnp.zeros((MOD_ROWS - len(block), MOD_LANES), f32))
            block = jnp.concatenate(block, axis=0).astype(bf16)
            for c in range(4):
                dmod_r[c] = block
        else:
            dmod_r[...] = line[...].astype(bf16)
        for part in range(3):
            cols = slice(part * D, (part + 1) * D)
            grad = dot_tn(attn_r[...], dqkv_r[:, cols])
            if info is not None:
                deal_rows(*g_refs, grad, at[1], part * D)
            else:
                g_refs[0][:, cols] = grad
        head = jnp.concatenate([patch, last_r[...]], axis=0)
        if info is None:
            g_refs[1][...] = head
            return
        none = jnp.zeros((HEAD, 128 - 48), f32)
        for c in range(4):
            left = jnp.concatenate([head[:, c * 96 : c * 96 + 48], none], axis=1)
            right = jnp.concatenate([head[:, c * 96 + 48 : c * 96 + 96], none], axis=1)
            deal(*g_refs, left, right, at[1], c, 3 * D)

    if info is None:
        outs = [((D, 3 * D), f32), ((HEAD, D), f32), ((images, 8 * D), bf16)]
    else:
        outs = [((4, 48, TAIL), f32), ((4, 48, TAIL), bf16), ((4, MOD_ROWS, MOD_LANES), bf16)]
    ops = (place, mod, h0_all, attn_all.reshape(-1, D), dqkv, dh1_all, dmod_all, w_qkv, noisy_all, g_last, loss_tile)
    if info is not None:
        ops += (info,)
    scratch = [pltpu.VMEM((images, 8 * D), f32)]
    return kernel_call(body, outs, ops, 4, scratch=scratch, places="s" + "v" * (len(ops) - 1), after=after)


def bundle_rows(tsteps, labels, time1_w, time2_w):
    images = tsteps.shape[0]

    def body(ts_h, lab_h, t1_h, t2_h, out_r, ts, lab, t1_r, t2_r, sems):
        copies = [
            pltpu.make_async_copy(a, b, sems.at[n])
            for n, (a, b) in enumerate(((ts_h, ts), (lab_h, lab), (t1_h, t1_r), (t2_h, t2_r)))
        ]
        for copy in copies:
            copy.start()
        for copy in copies:
            copy.wait()
        rows = t1_r.shape[0]
        out_r[0:rows, :] = t1_r[...].astype(bf16)
        out_r[rows:INFO, :] = t2_r[...].astype(bf16)
        lane = lax.broadcasted_iota(jnp.int32, (BUNDLE - INFO, D), 1)
        info = jnp.zeros((BUNDLE - INFO, D), jnp.int32)
        for i in range(images):
            for n, value in enumerate((ts[i] // 32, ts[i] % 32, lab[i] // 32, lab[i] % 32)):
                info = jnp.where(lane == n * images + i, value, info)
        out_r[INFO:BUNDLE, :] = info.astype(f32).astype(bf16)

    ops = (tsteps, labels, time1_w, time2_w)
    scratch = [pltpu.SMEM((images,), jnp.int32)] * 2 + [pltpu.VMEM(a.shape, f32) for a in ops[2:]] + [pltpu.SemaphoreType.DMA((4,))]
    return kernel_call(body, [((BUNDLE, D), bf16)], ops, 1.5, places="hhhh", scratch=scratch)[0]


def lay_shard(w_r, pa, ou, qk, pr, f1, f2):
    w_r[:, 0 : 3 * D] = qk[...].astype(bf16)
    head = jnp.concatenate([pa[0], ou[0]], axis=0)
    w_r[:, 3 * D : TAIL] = jnp.concatenate([head, jnp.zeros((HEAD, 128 - 48), f32)], axis=1).astype(bf16)
    w_r[:, TAIL : TAIL + D] = pr[...].astype(bf16)
    w_r[:, TAIL + D : TAIL + D + FF] = f1[...].astype(bf16)
    for b in range(4):
        w_r[:, TAIL + D + FF + b * D : TAIL + D + FF + (b + 1) * D] = f2[b * 48 : (b + 1) * 48, :].astype(bf16)


def cast_weights(patch_state, out_t, time1_w, time2_w, table_t, mod_w, qkv_w, proj_w, fc1_w, fc2_w, after=()):
    def body(pa, ou, t1, t2, ta, mo, qk, pr, f1, f2, w_r, mod16, tab16, sums):
        lay_shard(w_r, pa, ou, qk, pr, f1, f2)
        mod16[...] = mo[...].astype(bf16)
        tab16[...] = ta[...].astype(bf16)
        lane = lax.broadcasted_iota(jnp.int32, (8, D), 1)
        line = jnp.zeros((8, D), f32)
        for n, m in enumerate((pa[0], t1[...], t2[...], ta[...], mo[...], qk[...], pr[...], f1[...], f2[...], ou[0])):
            line = jnp.where(lane == n, jnp.sum(jnp.sum(m * m, axis=0, keepdims=True), axis=1, keepdims=True), line)
        sums[...] = line

    outs = [((48, SENT), bf16), (mod_w.shape, bf16), (table_t.shape, bf16), ((8, D), f32)]
    ops = (patch_state, out_t, time1_w, time2_w, table_t, mod_w, qkv_w, proj_w, fc1_w, fc2_w)
    return kernel_call(body, outs, ops, 2.5, after=after, room=CAST_ROOM)


def picked(index, count):
    lane = lax.broadcasted_iota(jnp.int32, (index.shape[0], count), 1)
    return (lane == index).astype(f32).astype(bf16)


def one_hot(shape, test):
    row, col = lax.broadcasted_iota(jnp.int32, shape, 0), lax.broadcasted_iota(jnp.int32, shape, 1)
    return test(row, col).astype(f32).astype(bf16)


def condition_body(infos, images, w1, w2, times_r, tab_r, position):
    own_d = tab_r.shape[0]
    ts, lab = [], []
    for i in range(images):
        for whole in infos:
            ts.append((whole[:, i : i + 1] * 32.0 + whole[:, images + i : images + i + 1]).astype(jnp.int32))
            lab.append((whole[:, 2 * images + i : 2 * images + i + 1] * 32.0 + whole[:, 3 * images + i : 3 * images + i + 1]).astype(jnp.int32))
    ts, lab = jnp.concatenate(ts, axis=0), jnp.concatenate(lab, axis=0)
    feats = dot(picked(ts, STEPS), times_r[...]).astype(bf16)
    act, time_slope = silu_pair(dot(feats, w1))
    act = act.astype(bf16)
    own = one_hot((D, own_d), lambda r, c: r == c + position * own_d)
    emb = dot(act, dot(w2, own).astype(bf16))
    picks = picked(lab, CLASSES)
    cond, cond_slope = silu_pair(emb + dot_nt(picks, tab_r[...]))
    return feats, act, time_slope, picks, cond.astype(bf16), cond_slope, own


def modulation_shares(place, pieces, times, tab16, mod16, images):
    parts = 8
    width = images * D

    def body(at, *refs):
        times_r, tab_r, mod_r, out_r, w1_r, w2_r, info_r = refs[8:]
        for n in range(8):
            owner = piece_owner(at, n)
            w1_r[pl.ds(pl.multiple_of(owner * 32, 32), 32), :] = refs[n][0:32, :]
            w2_r[pl.ds(pl.multiple_of(owner * 48, 48), 48), :] = refs[n][32:INFO, :]
            info_r[pl.ds(owner, 1), :] = refs[n][INFO:BUNDLE, 0:128].astype(f32)[0:1]
        cond = condition_body([info_r[...]], images, w1_r[...], w2_r[...], times_r, tab_r, at[0])[4]
        for s in range(8):
            i, col = divmod(s * width, 8 * D)
            value = dot(cond[i * parts : (i + 1) * parts], mod_r[:, col : col + width])
            for p in range(parts):
                out_r[p, s : s + 1, :] = value[p : p + 1]

    outs = [((parts, 8, width), f32), ((TFREQ, D), bf16), ((D, D), bf16)]
    ops = (place, *pieces, times, tab16, mod16)
    return kernel_call(body, outs, ops, 3, places="s" + "v" * 11, scratch=[pltpu.VMEM((parts, 128), f32)])


def condition_back(place, own_mod, oth_mod, w1, w2, times, tab16, mod16, passed, reps, parts, images):
    devices = reps * parts
    count = devices * images
    own_t, own_d = TFREQ // parts, D // parts
    each = 8 * D // MOD_LANES

    def body(at, own_r, oth_r, w1_r, w2_r, times_r, tab_r, mod_r, in_r, gm_r, gt_r, dc_r, loss_r, feat_r, act_r, slope_r, out_r, all_s, dmod_s):
        out_r[...] = in_r[...]
        for r in range(reps):
            block = slice(r * MOD_ROWS, (r + 1) * MOD_ROWS)
            for c in range(parts // 2):
                mine = pl.multiple_of((r * parts + 2 * c + at[1]) * MOD_ROWS, MOD_ROWS)
                its = pl.multiple_of((r * parts + 2 * c + 1 - at[1]) * MOD_ROWS, MOD_ROWS)
                all_s[pl.ds(mine, MOD_ROWS), :] = own_r[c, block, :]
                all_s[pl.ds(its, MOD_ROWS), :] = oth_r[c, block, :]
        rows = all_s[...]
        take = one_hot((devices, devices * MOD_ROWS), lambda r, c: c == r * MOD_ROWS + images * each + 1)
        infos = dot(take, rows)
        feats, act, time_slope, picks, cond, cond_slope, own = condition_body([infos], images, w1_r[...], w2_r[...], times_r, tab_r, at[0])
        near = one_hot((TFREQ, own_t), lambda r, c: r == c + at[0] * own_t)
        feat_r[...] = dot(feats, near).astype(bf16)
        act_r[...] = dot(act, own).astype(bf16)
        slope_r[...] = time_slope
        for n in range(each):
            take = one_hot((count, devices * MOD_ROWS), lambda r, c: c == (r % devices) * MOD_ROWS + (r // devices) * each + n)
            dmod_s[:, n * MOD_LANES : (n + 1) * MOD_LANES] = dot(take, rows).astype(bf16)
        take = one_hot((8, devices * MOD_ROWS), lambda r, c: c % MOD_ROWS == images * each)
        loss = dot(take, rows)
        loss_r[...] = jnp.broadcast_to(loss[:, 0:1] + loss[:, 1:2] + loss[:, 2:3], loss_r.shape)
        d_mod = dmod_s[...]
        d_cond = dot_nt(d_mod, mod_r[...]) * cond_slope
        wide = jnp.concatenate([d_cond, jnp.zeros((count, 128 - own_d), f32)], axis=1).astype(bf16)
        for p in range(parts):
            dc_r[p] = wide
        gm_r[...] = dot_tn(cond, d_mod)
        high = d_cond.astype(bf16)
        rest = d_cond - high.astype(f32)
        mid = rest.astype(bf16)
        low = (rest - mid.astype(f32)).astype(bf16)
        gt_r[...] = dot_tn(high, picks) + (dot_tn(mid, picks) + dot_tn(low, picks))

    outs = [((own_d, 8 * D), f32), ((own_d, CLASSES), f32), ((parts, count, 128), bf16), ((8, 128), f32)]
    outs += [((count, own_t), bf16), ((count, own_d), bf16), ((count, D), f32), (passed.shape, passed.dtype)]
    ops = (place, own_mod, oth_mod, w1, w2, times, tab16, mod16, passed)
    scratch = [pltpu.VMEM((devices * MOD_ROWS, MOD_LANES), bf16), pltpu.VMEM((count, 8 * D), bf16)]
    return kernel_call(body, outs, ops, 4, scratch=scratch, places="s" + "v" * 8)


def time_back(d_time, w2, act16, slope, feat16):
    parts, own_d = d_time.shape[0], act16.shape[1]
    own_t = TFREQ // parts

    def body(dt_r, w2_r, act_r, slope_r, feat_r, g1_r, g2_r):
        d_all = jnp.concatenate([dt_r[p, :, 0:own_d].astype(f32) for p in range(parts)], axis=1).astype(bf16)
        g2_r[...] = dot_tn(act_r[...], d_all)
        d_hid = (dot_nt(d_all, w2_r[...]) * slope_r[...]).astype(bf16)
        g1_r[...] = dot_tn(feat_r[...], d_hid)

    outs = [((own_t, D), f32), ((own_d, D), f32)]
    return kernel_call(body, outs, (d_time, w2, act16, slope, feat16), 2)


FAR = {"time1": (0, 1), "time2": (1, 1), "mod": (2, 8), "qkv": (10, 3), "proj": (13, 1), "fc1": (14, 4), "fc2": (18, 1), "table": (26, 3)}
NEAR = {"time1": 19, "time2": 20, "mod": 21, "qkv": 22, "proj": 23, "fc1": 24, "fc2": 25, "table": 29}
SUMS, LINES = 30, 32
ORDER = ("time1", "time2", "table", "mod", "qkv", "proj", "fc1", "fc2")


def lanes_of(rows_by_cols):
    ones = jnp.ones((8, rows_by_cols.shape[1]), f32)
    return lax.dot_general(ones, rows_by_cols, (((1,), (1,)), ((), ())), precision=lax.Precision.HIGHEST, preferred_element_type=f32)[0:1]


def put_sums(pack, name, g):
    sq = g * g + grad_floor
    line, count = FAR[name]
    col = jnp.sum(sq, axis=0, keepdims=True)
    for n in range(count):
        size = min(D, g.shape[1] - n * D)
        pack[line + n : line + n + 1, 0:size] = col[:, n * D : n * D + size]
    pack[NEAR[name] : NEAR[name] + 1, 0 : g.shape[0]] = lanes_of(sq)


def copies_sum(refs):
    a, b, c, d = (r[...].astype(f32) for r in refs)
    return (a + b) + (c + d)


def sums_early(place, parts):
    def body(at, a, b, c, d, gm, gf, pack, cuts):
        for n, part in enumerate((a, b, c, d)):
            cuts[jnp.bitwise_xor(at[2], n)] = part[...].astype(f32)
        pack[...] = jnp.zeros((LINES, D), f32)
        gm[:, 0:D] = jnp.concatenate([cuts[j][:, 768 : 768 + 96] for j in range(4)], axis=1)
        for j in range(4):
            gm[:, D + j * 384 : D + (j + 1) * 384] = cuts[j][:, 0:384]
            gf[j * 48 : (j + 1) * 48, :] = cuts[j][:, 384:768]
        put_sums(pack, "proj", gm[:, 0:D])
        put_sums(pack, "fc1", gm[:, D : D + FF])
        put_sums(pack, "fc2", gf[...])

    outs = [((48, D + FF), f32), ((192, D), f32), ((LINES, D), f32)]
    return kernel_call(body, outs, (place, *parts), 2, scratch=[pltpu.VMEM((4, 48, Z_LANES), f32)], places="svvvv")


def sums_middle(pack, g_table, g_mod, sums, loss, after=()):
    def body(old, tab, mod, sums_r, loss_r, pack_r):
        pack_r[...] = old[...]
        put_sums(pack_r, "mod", mod[...])
        put_sums(pack_r, "table", tab[...])
        lane = lax.broadcasted_iota(jnp.int32, (1, D), 1)
        pack_r[SUMS : SUMS + 1, :] = jnp.where(lane == 10, loss_r[0:1, 0:1], sums_r[0:1, :])

    return kernel_call(body, [((LINES, D), f32)], (pack, g_table, g_mod, sums, loss), 2, after=after)[0]


def sums_late(pack, tail, g_time1, g_time2):
    def body(old, q0, q1, q2, q3, t1, t2, gq, pack_r):
        pack_r[...] = old[...]
        gq[...] = copies_sum((q0, q1, q2, q3))
        put_sums(pack_r, "qkv", gq[:, 0 : 3 * D])
        put_sums(pack_r, "time1", t1[...])
        put_sums(pack_r, "time2", t2[...])

    outs = [(tail[0].shape, f32), ((LINES, D), f32)]
    return kernel_call(body, outs, (pack, *tail, g_time1, g_time2), 2)


def scaled_updates(place, packs, g_time1, g_time2, g_table, g_mod, gq, gm, gf, olds, patch_state, out_t):
    parts = packs.shape[0]
    shapes = [(g_time1.shape), g_time2.shape, g_table.shape, g_mod.shape, (48, 3 * D), (48, D), (48, FF), gf.shape]

    def body(at, pk, t1, t2, tab, mod, q, m, f, *refs):
        old_rs, (pat, ost), fresh_rs, u_rs = refs[0:8], refs[8:10], refs[10:18], refs[18:26]
        u_pat, u_out, m_pat, m_out, usq, head, line_s = refs[26:]
        total = jnp.sum(pk[...], axis=0)
        lane = lax.broadcasted_iota(jnp.int32, (1, D), 1)
        grads = (t1[...], t2[...], tab[...], mod[...], q[:, 0 : 3 * D], m[:, 0:D], m[:, D : D + FF], f[...])
        sizes = []

        def size_of(u):
            return jnp.sum(jnp.sum(u * u, axis=0, keepdims=True), axis=1, keepdims=True)

        for name, g, old_r, fresh_r, u_r in zip(ORDER, grads, old_rs, fresh_rs, u_rs):
            rows, cols = g.shape
            many = rows * parts
            line, count = FAR[name]
            far_at, near_at = (0, cols) if name == "table" else (many, 0)
            for p in range(parts):
                line_s[:, near_at + p * rows : near_at + (p + 1) * rows] = pk[p, NEAR[name] : NEAR[name] + 1, 0:rows] / cols
            for n in range(count):
                wide = min(D, cols - n * D)
                line_s[:, far_at + n * D : far_at + n * D + wide] = total[line + n : line + n + 1, 0:wide] / many
            fresh = line_s[:, 0 : many + cols]
            fresh_r[...] = jnp.sum(fresh, axis=0)
            renewed = decay_rate * old_r[...].reshape(1, many + cols) + (1.0 - decay_rate) * fresh
            near, far = renewed[:, near_at : near_at + many], renewed[:, far_at : far_at + cols]
            mean = jnp.mean(far if name == "table" else near, axis=1, keepdims=True)
            shape = (rows, many)
            mine = lax.broadcasted_iota(jnp.int32, shape, 1) == lax.broadcasted_iota(jnp.int32, shape, 0) + at[0] * rows
            own = jnp.sum(jnp.where(mine, near, 0.0), axis=1, keepdims=True)
            u = g * lax.rsqrt(own / mean) * lax.rsqrt(far)
            u_r[...] = u
            sizes.append(size_of(u))
        ends = []
        for lo, wide, old, moment_r, u_r in ((0, PIN, pat, m_pat, u_pat), (PIN, POUT, ost, m_out, u_out)):
            g = q[lo : lo + wide, 3 * D : 3 * D + 48]
            moment = decay_rate * old[1] + (1.0 - decay_rate) * (g * g + grad_floor)
            moment_r[...] = moment
            u = g * lax.rsqrt(moment)
            u_r[...] = u
            ends.append(size_of(u))
        line = jnp.zeros((1, D), f32)
        for n, value in enumerate([ends[0], *sizes, ends[1]]):
            line = jnp.where(lane == n, value, line)
        for p in range(parts):
            usq[p] = jnp.broadcast_to(line[:, 0:128], (8, 128))
        head[...] = total[SUMS : SUMS + 1, :] * jnp.where(lane == 10, 1.0 / parts, 1.0)

    outs = [((o.shape[0],), f32) for o in olds] + [(s, f32) for s in shapes]
    outs += [((PIN, 48), f32), ((POUT, 48), f32)] * 2 + [((parts, 8, 128), f32), ((1, D), f32)]
    ops = (place, packs, g_time1, g_time2, g_table, g_mod, gq, gm, gf, *olds, patch_state, out_t)
    scratch = [pltpu.VMEM((1, 9 * D + 128), f32)]
    return kernel_call(body, outs, ops, 3.5, scratch=scratch, places="s" + "v" * (len(ops) - 1))


def new_weights(usq, head, counts, images, updates, weights, patch_state, out_t, m_patch, m_out):
    def body(usq_r, head_r, mp, mo, pat, ost, *refs):
        us, ms, news = refs[0:10], refs[10:18], refs[18:26]
        new_p, new_o, loss_r, rms_r = refs[26:]
        total = usq_r[0, 0:1, :]
        for p in range(1, usq_r.shape[0]):
            total = total + usq_r[p, 0:1, :]
        lane = lax.broadcasted_iota(jnp.int32, (1, 128), 1)
        size = jnp.ones((1, 128), f32)
        for n, count in enumerate(counts):
            size = jnp.where(lane == n, float(count), size)
        rms = jnp.sqrt(total / size)
        step = step_rate * jnp.sqrt(head_r[:, 0:128] / size) / jnp.maximum(1.0, rms / clip_level)
        for n in range(8):
            news[n][...] = ms[n][...] - step[:, n + 1 : n + 2] * us[n + 1][...]
        new_p[0] = pat[0] - step[:, 0:1] * us[0][...]
        new_p[1] = mp[...]
        new_o[0] = ost[0] - step[:, 9:10] * us[9][...]
        new_o[1] = mo[...]
        rms_r[...] = jnp.sum(rms[:, 0:10], axis=0)
        loss_r[...] = jnp.sum(head_r[:, 10:11], axis=0) / images

    outs = [(m.shape, f32) for m in weights] + [(patch_state.shape, f32), (out_t.shape, f32), ((1,), f32), ((10,), f32)]
    ops = (usq, head, m_patch, m_out, patch_state, out_t, *updates, *weights)
    return kernel_call(body, outs, ops, 3.5)


def gather_pieces(x):
    near = [x, flip(x, 2), flip(x, 4), flip(x, 6)]
    return near + [flip(a, 1) for a in near]


HALF = 2432


def half_shard(place, patch_state, out_t, qkv_w, proj_w, fc1_w, fc2_w, after=()):
    def body(at, pa, ou, qk, pr, f1, f2, out, all_s):
        lay_shard(all_s, pa, ou, qk, pr, f1, f2)
        for j in range(2):

            @pl.when(at[2] % 2 == j)
            def _():
                out[...] = all_s[:, j * HALF : (j + 1) * HALF]

    ops = (place, patch_state, out_t, qkv_w, proj_w, fc1_w, fc2_w)
    scratch = [pltpu.VMEM((48, 2 * HALF), bf16)]
    return kernel_call(body, [((48, HALF), bf16)], ops, 1, scratch=scratch, places="s" + "v" * 6, after=after)[0]


def stacked_pieces(place, two, halves, after=()):
    def body(at, x, y, a, b, out, cuts):
        out[0] = x[...]
        out[1] = y[...]
        for n, ref in enumerate((a, b)):
            cuts[jnp.bitwise_xor(at[2] % 2, n)] = ref[...]
        for j in range(2):
            size = min(HALF, SENT - j * HALF)
            out[2, :, j * HALF : j * HALF + size] = cuts[j][:, 0:size]

    ops = (place, *two, *halves)
    scratch = [pltpu.VMEM((2, 48, HALF), bf16)]
    return kernel_call(body, [((3, 48, SENT), bf16)], ops, 1, scratch=scratch, places="s" + "v" * 4, after=after)[0]


def chip_blocks(place, keep, sent, micros, after=()):
    def body(at, keep_r, sent_r, *refs):
        for n, out in enumerate(refs):
            chip = jnp.bitwise_xor(at[0] // 2, n)
            out[...] = (keep_r[chip] + sent_r[chip].astype(f32)).astype(out.dtype)

    shape = keep.shape[1:]
    return kernel_call(body, [(shape, f32)] + [(shape, bf16)] * 3, (place, keep, sent), micros, places="svv", after=after)


def tail_blocks(place, keep, sent, d_mods, after=()):
    side = 4 * MOD_ROWS

    def body(at, keep_r, sent_r, *refs):
        outs, mods = refs[1:5], refs[5]
        for n in range(4):
            mods[n * MOD_ROWS : (n + 1) * MOD_ROWS, :] = refs[0][n]
        for n, out in enumerate(outs):
            chip = jnp.bitwise_xor(at[0] // 2, n)
            value = (keep_r[chip] + sent_r[chip].astype(f32)).astype(out.dtype)
            if n == 0:
                out[...] = value
                continue
            out[0:48, 0:TAIL] = value
            out[48:side, 0:TAIL] = jnp.zeros((side - 48, TAIL), bf16)
            out[:, TAIL:] = mods[...]

    outs = [((48, TAIL), f32)] + [((side, TAIL + MOD_LANES), bf16)] * 3 + [((side, MOD_LANES), bf16)]
    return kernel_call(body, outs, (place, keep, sent, d_mods), 1, places="svvv", after=after)


def tail_sum(place, own, arrived, mods, after=()):
    def body(at, own_r, a, b, c, mod_r, out, all_r):
        total = own_r[...] + a[0:48, 0:TAIL].astype(f32)
        out[...] = (total + (b[0:48, 0:TAIL].astype(f32) + c[0:48, 0:TAIL].astype(f32))).astype(bf16)
        chip = at[0] // 2
        all_r[chip] = mod_r[...]
        for n, ref in enumerate((a, b, c)):
            all_r[jnp.bitwise_xor(chip, n + 1)] = ref[:, TAIL:]

    outs = [((48, TAIL), bf16), ((4,) + mods.shape, bf16)]
    return kernel_call(body, outs, (place, own, *arrived, mods), 1, places="svvvvv", after=after)


Z_LANES = 384 + 384 + 128


def copy_blocks(place, parts, after=()):
    def body(at, a, b, c, d, own, one, two, three, cuts):
        total = (a[...] + b[...].astype(f32)) + (c[...].astype(f32) + d[...].astype(f32))
        none = jnp.zeros((48, 32), f32)
        for j in range(4):
            cuts[j, :, 0:384] = total[:, D + j * 384 : D + (j + 1) * 384]
            cuts[j, :, 384:768] = total[:, D + FF + j * 384 : D + FF + (j + 1) * 384]
            cuts[j, :, 768:] = jnp.concatenate([total[:, j * 96 : (j + 1) * 96], none], axis=1)
        for n, out in enumerate((own, one, two, three)):
            out[...] = cuts[jnp.bitwise_xor(at[2], n)].astype(out.dtype)

    outs = [((48, Z_LANES), f32)] + [((48, Z_LANES), bf16)] * 3
    return kernel_call(body, outs, (place, *parts), 2, scratch=[pltpu.VMEM((4, 48, Z_LANES), f32)], places="svvvv", after=after)


def four_sum(parts, after=()):
    def body(a, b, c, d, out):
        out[...] = ((a[...].astype(f32) + b[...].astype(f32)) + (c[...].astype(f32) + d[...].astype(f32))).astype(bf16)

    return kernel_call(body, [(parts[0].shape, bf16)], parts, 1, after=after)[0]


def other_copies(total):
    return (total, flip(total, 1, "rep"), flip(total, 2, "rep"), flip(total, 3, "rep"))


def eight_by_four(
    latents, noise, tsteps, labels, patch_state, time1_w, time2_w, table_t, mod_w, qkv_w, proj_w, fc1_w, fc2_w, out_t, olds, place, plan, grid, times
):
    reps, parts = 4, 8
    images = tsteps.shape[0]
    bundle = bundle_rows(tsteps, labels, time1_w, time2_w)
    pieces = gather_pieces(bundle)
    w_own, mod16, tab16, sums = cast_weights(
        patch_state, out_t, time1_w, time2_w, table_t, mod_w, qkv_w, proj_w, fc1_w, fc2_w, after=pieces[1:4]
    )
    half = half_shard(place, patch_state, out_t, qkv_w, proj_w, fc1_w, fc2_w, after=(bundle,))
    half = flip(half, 6)
    halves = [half, flip(half, 1, "rep")]
    w_two = [flip(w_own, k) for k in (2, 4)]
    w_core = flip(w_own, 1)
    shares, w1, w2 = modulation_shares(place, pieces, times, tab16, mod16, images)
    shares = lax.all_to_all(shares, "fsdp", 0, 0)
    w_near = stacked_pieces(place, w_two, halves, after=(shares,))
    w_pieces = [w_own, w_near, w_core, flip(w_near, 1)]

    w_qkv, head, mod, con, noisy, hidden0, attn16, qkv16, totals, mixture16 = attention_forward(
        tsteps, latents, noise, plan, grid, w_pieces, shares, place
    )
    keep, send, g_last, d_mix16, d_h1, d_mod, loss_tile = mlp_pass(
        noise, con, mod, hidden0, mixture16, head, w_pieces, place
    )
    send = flip(send, 1)
    d_qkv16 = heads_back(qkv16, totals, d_mix16, after=(keep,))
    blocks = chip_blocks(place, keep, send, 2, after=(d_qkv16,))
    q_keep, q_send, d_mod16 = attention_back(
        place, mod, hidden0, attn16, d_qkv16, d_h1, d_mod, w_qkv, noisy, g_last, loss_tile, bundle, after=(blocks[1],)
    )
    q_send = flip(q_send, 1)
    arrived = [flip(blocks[n], 2 * n) for n in range(1, 4)]
    cuts = copy_blocks(place, [blocks[0]] + arrived)
    q_own, *q_blocks, d_mods = tail_blocks(place, q_keep, q_send, lax.all_to_all(d_mod16, "rep", 0, 0), after=(cuts[1],))
    q_sum, own_mod = tail_sum(place, q_own, [flip(q_blocks[n], 2 * (n + 1)) for n in range(3)], d_mods)
    oth_mod = flip(own_mod, 1)
    g_mod, g_table, d_time, loss, feat16, act16_t, time_slope, q_sum = condition_back(
        place, own_mod, oth_mod, w1, w2, times, tab16, mod16, q_sum, reps, parts, images
    )
    mid = four_sum([cuts[0]] + [flip(cuts[n], n, "rep") for n in range(1, 4)])
    mid = other_copies(mid)
    tail = other_copies(q_sum)
    gm, gf, pack = sums_early(place, mid)
    d_time = lax.all_to_all(d_time, "fsdp", 0, 0)
    pack = sums_middle(pack, g_table, g_mod, sums, loss)
    g_time1, g_time2 = time_back(d_time, w2, act16_t, time_slope, feat16)
    gq, pack = sums_late(pack, tail, g_time1, g_time2)
    packs = gather_rows(pack).reshape(parts, LINES, D)
    result = scaled_updates(place, packs, g_time1, g_time2, g_table, g_mod, gq, gm, gf, olds, patch_state, out_t)
    fresh, updates = result[:8], result[8:16]
    u_patch, u_out, m_patch, m_out, usq, sums = result[16:]
    usq = lax.all_to_all(usq, "fsdp", 0, 0)
    weights = (time1_w, time2_w, table_t, mod_w, qkv_w, proj_w, fc1_w, fc2_w)
    counts = [w.size * parts for w in (patch_state[0], *weights, out_t[0])]
    *news, new_patch, new_out, loss, rms = new_weights(
        usq, sums, counts, images * reps * parts, (u_patch, *updates, u_out), weights, patch_state, out_t, m_patch, m_out
    )
    news[2] = news[2].T
    outs = [new_patch]
    for n in range(8):
        outs += [news[n], fresh[n]]
    return tuple(outs) + (new_out.transpose(0, 2, 1), loss.reshape(()), rms)


def per_device(
    latents,
    noise,
    timesteps,
    labels,
    patch_state,
    time1_w,
    time1_f,
    time2_w,
    time2_f,
    table_w,
    table_f,
    mod_w,
    mod_f,
    qkv_w,
    qkv_f,
    proj_w,
    proj_f,
    fc1_w,
    fc1_f,
    fc2_w,
    fc2_f,
    out_state,
):
    reps, parts = lax.axis_size("rep"), lax.axis_size("fsdp")
    position = lax.axis_index("fsdp")
    masters = (patch_state[0], time1_w, time2_w, table_w, mod_w, qkv_w, proj_w, fc1_w, fc2_w, out_state[0])
    images = latents.shape[0] * latents.shape[1]
    latents = latents.reshape(images, TOK_IMG, PIN).transpose(0, 2, 1)
    noise = noise.reshape(images, TOK_IMG, PIN).transpose(0, 2, 1)
    out_t = out_state.transpose(0, 2, 1)
    tsteps = timesteps.reshape(images)
    labels = labels.reshape(images)
    own_d = D // parts
    own_t = TFREQ // parts
    place = jnp.stack([position, position & 1, lax.axis_index("rep")]).astype(jnp.int32)
    plan, grid = jnp.asarray(plan_table()), jnp.asarray(place_table())
    times = jnp.asarray(time_table(), bf16)
    olds = (time1_f, time2_f, table_f, mod_f, qkv_f, proj_f, fc1_f, fc2_f)

    if parts == 8 and reps == 4:
        return eight_by_four(
            latents, noise, tsteps, labels, patch_state, time1_w, time2_w, table_w.T, mod_w, qkv_w, proj_w, fc1_w, fc2_w, out_t, olds, place, plan, grid, times
        )

    info = jnp.stack([tsteps // 32, tsteps % 32, labels // 32, labels % 32]).reshape(1, 4 * images)
    info_row = jnp.pad(info.astype(bf16), ((0, 0), (0, D - 4 * images)))
    bundle = jnp.concatenate([time1_w.astype(bf16), time2_w.astype(bf16), info_row], axis=0)
    bundle = gather_rows(bundle).reshape(parts, own_t + own_d + 1, D)
    w_time1 = bundle[:, :own_t].reshape(TFREQ, D)
    w_time2 = bundle[:, own_t : own_t + own_d].reshape(D, D)
    info_rep = bundle[:, own_t + own_d, : 4 * images]

    head = lax.all_gather(jnp.concatenate([patch_state[0], out_t[0]], axis=0).astype(bf16), "fsdp", axis=1, tiled=True)
    w_rows = gather_rows(jnp.concatenate([qkv_w, proj_w, fc1_w], axis=1).astype(bf16))
    w_fc2 = gather_rows(fc2_w.astype(bf16))
    w_qkv, w_proj, w_fc1 = w_rows[:, : 3 * D], w_rows[:, 3 * D : 4 * D], w_rows[:, 4 * D :]

    info_all = rep_gather(info_rep).reshape(reps * parts, 4, images).astype(jnp.int32)
    w_mod16 = mod_w.astype(bf16)
    w_table16 = table_w.astype(bf16)

    def condition_path(info_any):
        ts = (info_any[:, 0] * 32 + info_any[:, 1]).reshape(-1)
        lab = (info_any[:, 2] * 32 + info_any[:, 3]).reshape(-1)
        feats16 = dot(pick(ts, STEPS), times).astype(bf16)
        time_act, time_slope = silu_pair(dot(feats16, w_time1))
        time_act16 = time_act.astype(bf16)
        time_emb = dot(time_act16, w_time2)
        own_emb = lax.dynamic_slice(time_emb, (0, position * own_d), (time_emb.shape[0], own_d))
        picks = pick(lab, CLASSES)
        cond_act, cond_slope = silu_pair(own_emb + dot(picks, w_table16))
        return feats16, time_act16, time_slope, picks, cond_act.astype(bf16), cond_slope

    info_here = info_rep.reshape(parts, 4, images).astype(jnp.int32)
    cond_here = condition_path(info_here)[4]
    shares = dot(cond_here, w_mod16).reshape(parts, 8, images * D)
    shares = lax.all_to_all(shares, "fsdp", 0, 0, tiled=True)

    mod, con, noisy, hidden0, attn16, qkv16, totals, mixture16 = attention_forward(
        tsteps, latents, noise, plan, grid, (w_qkv, head), shares, place
    )
    g_proj, g_fc1, g_fc2, g_last, d_mix16, d_h1, d_mod, loss_tile = mlp_pass(
        noise, con, mod, hidden0, mixture16, head, (w_proj, w_fc1, w_fc2), place
    )
    loss_part = loss_tile[0, 0]
    g_tail, g_head, d_mod16 = attention_back(
        place, mod, hidden0, attn16, heads_back(qkv16, totals, d_mix16), d_h1, d_mod, w_qkv, noisy, g_last, loss_tile, None
    )

    d_mod_all = rep_gather(d_mod16).reshape(1, -1)
    d_mod_all = gather_rows(d_mod_all).reshape(parts, reps, images, 8 * D)
    d_mod_all = d_mod_all.transpose(1, 0, 2, 3).reshape(reps * parts * images, 8 * D)
    feats16, time_act16, time_slope, picks, cond16, cond_slope = condition_path(info_all)
    d_cond = dot_nt(d_mod_all, w_mod16) * cond_slope
    g_mod = dot_tn(cond16, d_mod_all)
    g_table = lax.dot_general(
        picks.astype(f32), d_cond, (((0,), (0,)), ((), ())), precision=lax.Precision.HIGHEST
    )
    d_time16 = lax.all_gather(d_cond.astype(bf16), "fsdp", axis=0)
    d_time16 = d_time16.transpose(1, 0, 2).reshape(-1, D)
    own_act16 = lax.dynamic_slice(time_act16, (0, position * own_d), (time_act16.shape[0], own_d))
    g_time2 = dot_tn(own_act16, d_time16)
    d_hid16 = (dot_nt(d_time16, w_time2) * time_slope).astype(bf16)
    own_feat16 = lax.dynamic_slice(feats16, (0, position * own_t), (feats16.shape[0], own_t))
    g_time1 = dot_tn(own_feat16, d_hid16)

    g_head = lax.psum_scatter(g_head, "fsdp", scatter_dimension=1, tiled=True)
    g_tail, g_proj, g_fc1, g_fc2 = (sum_scatter(g) for g in (g_tail, g_proj, g_fc1, g_fc2))
    g_proj, g_fc1, g_fc2 = (rep_sum(g.astype(bf16)) for g in (g_proj, g_fc1, g_fc2))
    g_tail = rep_sum(g_tail.astype(bf16))
    g_head = rep_sum(g_head)
    grads = (
        g_head[:PIN],
        g_time1,
        g_time2,
        g_table,
        g_mod,
        g_tail,
        g_proj,
        g_fc1,
        g_fc2,
        g_head[PIN:].T,
    )
    loss_part = lax.psum(loss_part, "rep")
    dims = (0, 0, 1, 0, 0, 0, 0, 0)

    packs = []
    for slot in range(8):
        grad, dim = grads[slot + 1], dims[slot]
        squares = grad * grad + grad_floor
        near = jnp.sum(squares, axis=1 - dim)
        far = jnp.sum(squares, axis=dim)
        spread = lax.dynamic_update_slice(
            jnp.zeros((near.shape[0] * parts,), f32), near / far.shape[0], (position * near.shape[0],)
        )
        far = far / (near.shape[0] * parts)
        packs.append(jnp.concatenate([spread, far] if dim == 0 else [far, spread]))
    tail = jnp.stack([jnp.sum(m * m) for m in masters] + [loss_part])
    lengths = [pack.shape[0] for pack in packs]
    totals = lax.psum(jnp.concatenate(packs + [tail]), "fsdp")
    fresh = []
    start = 0
    for length in lengths:
        fresh.append(totals[start : start + length])
        start += length
    square_tot = totals[start : start + 10]
    loss = totals[start + 10] / (images * reps * parts)

    updates, counts = [], []
    plain = []
    for slot in range(10):
        grad = grads[slot]
        if slot in (0, 9):
            state = patch_state if slot == 0 else out_state
            moment = decay_rate * state[1] + (1.0 - decay_rate) * (grad * grad + grad_floor)
            plain.append(moment)
            updates.append(grad * lax.rsqrt(moment))
            counts.append(grad.size * parts)
            continue
        dim = dims[slot - 1]
        renewed = decay_rate * olds[slot - 1] + (1.0 - decay_rate) * fresh[slot - 1]
        rows = grad.shape[0] * (parts if dim == 0 else 1)
        row, col = renewed[:rows], renewed[rows:]
        mean_row = jnp.mean(row)
        if dim == 0:
            row = lax.dynamic_slice(row, (position * grad.shape[0],), (grad.shape[0],))
        else:
            col = lax.dynamic_slice(col, (position * grad.shape[1],), (grad.shape[1],))
        updates.append(grad * lax.rsqrt(row[:, None] * col[None, :] / mean_row))
        counts.append(grad.size * parts)
    update_tot = lax.psum(jnp.stack([jnp.sum(u * u) for u in updates]), "fsdp")
    sizes = np.asarray(counts, np.float32)
    size_rms = jnp.sqrt(update_tot / sizes)
    factor = step_rate * jnp.sqrt(square_tot / sizes) / jnp.maximum(1.0, size_rms / clip_level)
    new = [masters[s] - factor[s] * updates[s] for s in range(10)]
    result = [jnp.stack([new[0], plain[0]])]
    for slot in range(8):
        result += [new[slot + 1], fresh[slot]]
    return tuple(result) + (jnp.stack([new[9], plain[1]]), loss, size_rms)


def solution(mesh):
    images = P(None, ("rep", "fsdp"), None, None)
    singles = P(None, ("rep", "fsdp"))
    rows, cols = P("fsdp", None), P(None, "fsdp")
    placed = (images, images, singles, singles, P(None, None, "fsdp"))
    placed += (rows, P(), rows, P(), cols, P()) + (rows, P()) * 5 + (P(None, "fsdp", None),)
    results = (P(None, None, "fsdp"), rows, P(), rows, P(), cols, P()) + (rows, P()) * 5
    results += (P(None, "fsdp", None), P(), P())
    return jax.shard_map(per_device, mesh=mesh, in_specs=placed, out_specs=results, check_vma=False)
```

```python
import math

import jax
import jax.numpy as jnp
import numpy as np
from jax import lax
from jax.experimental import pallas as pl
from jax.experimental.pallas import tpu as pltpu
from jax.sharding import PartitionSpec as P

D = 384
HEADS = 6
HEAD_DIM = 64
FF = 1536
TFREQ = 256
GRID = 16
PIN = 16
POUT = 32
CLASSES = 1001
STEPS = 1000
TOK_IMG = 256

decay_rate = 0.5
clip_level = 1.0
step_rate = 0.5
grad_floor = 1e-30
norm_floor = 1e-06
f32 = jnp.float32
bf16 = jnp.bfloat16


def plan_table():
    s = np.arange(STEPS, dtype=np.float64)
    beta = 1e-4 + (0.02 - 1e-4) * s / (STEPS - 1)
    lbar = np.cumsum(np.log1p(-beta))
    lprev = np.concatenate([[0.0], lbar[:-1]])
    post = beta * -np.expm1(lprev) / -np.expm1(lbar)
    post[0] = post[1]
    remain = -np.expm1(lbar)
    coef = beta * beta / ((1.0 - beta) * remain)
    rows = [np.exp(0.5 * lbar), np.sqrt(remain), np.log(beta), np.log(post), coef]
    return np.stack(rows + [np.zeros(STEPS)] * 3, axis=1).astype(np.float32)


def time_table():
    half = TFREQ // 2
    freq = np.exp(np.float32(-math.log(10000.0)) * np.arange(half, dtype=np.float32) / np.float32(half)).astype(np.float32)
    angles = np.arange(STEPS, dtype=np.float32)[:, None] * freq[None, :]
    wide = angles.astype(np.float64)
    return np.concatenate([np.cos(wide), np.sin(wide)], axis=1).astype(np.float32)


def place_table():
    quarter = D // 4
    om = np.exp(np.float32(-math.log(10000.0)) * np.arange(quarter, dtype=np.float32) / np.float32(quarter)).astype(np.float32)
    n = np.arange(TOK_IMG)
    row = ((n // GRID).astype(np.float32)[:, None] * om[None, :]).astype(np.float64)
    col = ((n % GRID).astype(np.float32)[:, None] * om[None, :]).astype(np.float64)
    return np.concatenate([np.sin(row), np.cos(row), np.sin(col), np.cos(col)], axis=1).astype(np.float32)


def pick(index, count):
    return (index[:, None] == jnp.arange(count, dtype=jnp.int32)[None, :]).astype(bf16)


def silu_pair(v):
    s = 1.0 / (1.0 + jnp.exp(-v))
    return v * s, s * (1.0 + v * (1.0 - s))


def norm_parts(x):
    mean = jnp.mean(x, axis=-1, keepdims=True)
    cen = x - mean
    inv = lax.rsqrt(jnp.mean(cen * cen, axis=-1, keepdims=True) + norm_floor)
    return cen * inv, inv


def norm_back(d_norm, normed, inv):
    a = jnp.mean(d_norm, axis=-1, keepdims=True)
    b = jnp.mean(d_norm * normed, axis=-1, keepdims=True)
    return inv * (d_norm - a - normed * b)


def dot(a, b):
    return jnp.dot(a, b, preferred_element_type=f32)


def dot_nt(a, b):
    return lax.dot_general(a, b, (((1,), (1,)), ((), ())), preferred_element_type=f32)


def dot_tn(a, b):
    return lax.dot_general(a, b, (((0,), (0,)), ((), ())), preferred_element_type=f32)


def flip(x, bit, axis="fsdp"):
    size = lax.axis_size(axis)
    return lax.ppermute(x, axis, [(i, i ^ bit) for i in range(size)])


def rep_gather(x):
    size = lax.axis_size("rep")
    me = lax.axis_index("rep")
    parts = jnp.stack([x] + [flip(x, k, "rep") for k in range(1, size)])
    return jnp.stack([lax.dynamic_index_in_dim(parts, me ^ j, 0, keepdims=False) for j in range(size)])


def rep_sum(x16):
    size = lax.axis_size("rep")
    parts = [x16.astype(f32)] + [flip(x16, k, "rep").astype(f32) for k in range(1, size)]
    while len(parts) > 1:
        parts = [parts[i] + parts[i + 1] for i in range(0, len(parts), 2)]
    return parts[0]


def sum_scatter(grad):
    return lax.psum_scatter(grad, "fsdp", scatter_dimension=0, tiled=True)


def gather_rows(x):
    return lax.all_gather(x, "fsdp", axis=0, tiled=True)


def lane_half(shape, which):
    lane = lax.broadcasted_iota(jnp.int32, shape, 1)
    return (lane < HEAD_DIM) if which == 0 else (lane >= HEAD_DIM)


FLOPS_US = 5000_000_000


def kernel_call(body, outs, operands, micros, scratch=(), places=None, after=(), room=16):
    vmem = pl.BlockSpec(memory_space=pltpu.VMEM)
    smem = pl.BlockSpec(memory_space=pltpu.SMEM)
    places = places or "v" * len(operands)
    count = len(operands)

    def run(*refs):
        body(*refs[:count], *refs[count + len(after) :])

    return pl.pallas_call(
        run,
        out_shape=[jax.ShapeDtypeStruct(s, t) for s, t in outs],
        in_specs=[{"s": smem, "v": vmem, "h": pl.BlockSpec(memory_space=pltpu.HBM)}[p] for p in places] + [pl.BlockSpec(memory_space=pl.ANY)] * len(after),
        out_specs=[vmem] * len(outs),
        scratch_shapes=list(scratch),
        compiler_params=pltpu.CompilerParams(vmem_limit_bytes=room * 2**20),
        cost_estimate=pl.CostEstimate(flops=int(micros * FLOPS_US), bytes_accessed=1_000_000, transcendentals=0),
    )(*(pltpu.with_memory_space_constraint(x, pltpu.HBM) if p == "h" else x for x, p in zip(operands, places)), *after)


HEAD = PIN + POUT
CAST_ROOM = 48
INFO = 80
BUNDLE = 96
TAIL = 3 * D + 128
SENT = TAIL + D + 2 * FF


def piece_owner(at, n):
    return jnp.bitwise_xor(at[0], 2 * (n % 4) + n // 4)


def shards_of(refs):
    near, far = refs[:2]
    return [near.at[n] for n in range(4)] + [far.at[n] for n in range(4)]


def attention_forward(tsteps, lat, noi, plan, grid, weights, shares, place, after=()):
    images = lat.shape[0]
    fast = len(weights[0].shape) == 3

    def body(ts, at, lat_r, noi_r, plan_r, grid_r, share_r, *refs):
        if fast:
            wq_r, head_r, head_s = refs[2], refs[3], refs[-1]
            shards = shards_of(refs)
            for n in range(8):
                owner = piece_owner(at, n)
                rows = pl.ds(pl.multiple_of(owner * 48, 48), 48)
                wq_r[rows, :] = shards[n][:, 0 : 3 * D]
                head_s[owner] = shards[n][:, 3 * D : 3 * D + 48]
            for p in range(8):
                head_r[:, p * 48 : (p + 1) * 48] = head_s[p]
            refs = refs[4:-1]
        else:
            wq_r, head_r = refs[:2]
            refs = refs[2:]
        mod_r, con_r, noisy_r, h0_r, attn_r, qkv_r, total_r, mix_r = refs
        total = share_r[0]
        for p in range(1, share_r.shape[0]):
            total = total + share_r[p]
        width = total.shape[1]
        for n in range(8):
            i, col = divmod(n * width, 8 * D)
            mod_r[i : i + 1, col : col + width] = total[n : n + 1]
        for i in range(images):
            row = plan_r[pl.ds(ts[i], 1), :]
            con_r[i : i + 1, :] = row
            noisy = (row[:, 0:1] * lat_r[i] + row[:, 1:2] * noi_r[i]).astype(bf16)
            noisy_r[i] = noisy
            h0 = dot_tn(noisy, head_r[0:PIN, :]) + grid_r[...]
            h0_r[i] = h0
            norm, _ = norm_parts(h0)
            attn = (norm * (1.0 + mod_r[i : i + 1, D : 2 * D]) + mod_r[i : i + 1, 0:D]).astype(bf16)
            attn_r[i] = attn
            for part in range(3):
                qkv_r[i, :, part * D : (part + 1) * D] = dot(attn, wq_r[:, part * D : (part + 1) * D]).astype(bf16)
        lane = lax.broadcasted_iota(jnp.int32, (TOK_IMG, 128), 1)
        logs = [jnp.zeros((TOK_IMG, 128), f32)] * images
        for pair in range(HEADS // 2):
            for i in range(images):
                q = qkv_r[i, :, pair * 128 : pair * 128 + 128]
                k = qkv_r[i, :, D + pair * 128 : D + pair * 128 + 128]
                v = qkv_r[i, :, 2 * D + pair * 128 : 2 * D + pair * 128 + 128]
                mixed = None
                for half in range(2):
                    own = lane_half(q.shape, half)
                    zero = jnp.zeros_like(q)
                    s = dot_nt(jnp.where(own, q, zero), k) * 0.125
                    top = jnp.max(s, axis=-1, keepdims=True)
                    p = jnp.exp(s - top)
                    total = jnp.sum(p, axis=-1, keepdims=True)
                    p = p * (1.0 / total)
                    logs[i] = jnp.where(lane == pair * 2 + half, top + jnp.log(total), logs[i])
                    o = dot(p.astype(bf16), jnp.where(own, v, zero))
                    mixed = o if mixed is None else mixed + o
                mix_r[i, :, pair * 128 : pair * 128 + 128] = mixed.astype(bf16)
        for i in range(images):
            total_r[i] = logs[i]

    outs = [
        ((images, 8 * D), f32),
        ((images, 8), f32),
        ((images, PIN, TOK_IMG), bf16),
        ((images, TOK_IMG, D), f32),
        ((images, TOK_IMG, D), bf16),
        ((images, TOK_IMG, 3 * D), bf16),
        ((images, TOK_IMG, 128), f32),
        ((images, TOK_IMG, D), bf16),
    ]
    scratch = []
    if fast:
        outs = [((D, 3 * D), bf16), ((HEAD, D), bf16)] + outs
        scratch = [pltpu.VMEM((8, HEAD, 48), bf16)]
    ops = (tsteps, place, lat, noi, plan, grid, shares, *weights)
    return kernel_call(
        body, outs, ops, 8, scratch=scratch, places="ss" + "v" * (len(ops) - 2), after=after
    )


BLOCK = 384
WIDE = 768


def mlp_pass(noi, con, mod, h0_all, mix_all, head, weights, place, after=()):
    images = noi.shape[0]
    bend_scale = math.sqrt(2.0 / math.pi)
    share = 1.0 / (TOK_IMG * PIN)

    fast = len(weights[0].shape) == 3

    def body(at, noi_r, con_r, mod_r, h0_r, mix_r, head_r, *refs):
        if fast:
            wp_r, w1_r, w2_r = refs[-3:]
            shards = shards_of(refs)
            for n in range(8):
                owner = piece_owner(at, n)
                rows = pl.ds(pl.multiple_of(owner * 48, 48), 48)
                wp_r[rows, :] = shards[n][:, 0:D]
                w1_r[rows, :] = shards[n][:, D : D + FF]
                for b in range(4):
                    w2_r[pl.ds(pl.multiple_of(owner * 192 + b * 48, 48), 48), :] = shards[n][:, D + FF + b * D : D + FF + (b + 1) * D]
            refs = refs[2:-3]
        else:
            wp_r, w1_r, w2_r = refs[:3]
            refs = refs[3:]
        g_refs, refs = refs[: 2 if fast else 3], refs[2 if fast else 3 :]
        glast_r, dmix_r, dh1_r, dmod_r, loss_r, mlp_r, act_r, dinner_r, douter_r, dbr_r, slope_r = refs
        g_last = None
        wo = head_r[PIN:HEAD, :]
        losses = jnp.zeros((1, 1), f32)
        dmod_r[:, 0 : 2 * D] = jnp.zeros((images, 2 * D), f32)
        for i in range(images):
            def m(slot):
                return mod_r[i : i + 1, slot * D : (slot + 1) * D]

            def put(slot, value):
                dmod_r[i : i + 1, slot * D : (slot + 1) * D] = jnp.sum(value, axis=0, keepdims=True)

            branch = dot(mix_r[i], wp_r[...])
            h1 = h0_r[i] + m(2) * branch
            norm1, inv1 = norm_parts(h1)
            mlp = (norm1 * (1.0 + m(4)) + m(3)).astype(bf16)
            tokens = slice(i * TOK_IMG, (i + 1) * TOK_IMG)
            mlp_r[tokens, :] = mlp
            outer = None
            for b in range(FF // WIDE):
                cols = slice(b * WIDE, (b + 1) * WIDE)
                x = dot(mlp, w1_r[:, cols])
                sq = x * x
                t = jnp.tanh(bend_scale * x * (1.0 + 0.044715 * sq))
                hx = 0.5 * x
                act = (hx * (1.0 + t)).astype(bf16)
                act_r[tokens, cols] = act
                slope_r[:, cols] = 0.5 * (1.0 + t) + hx * (1.0 - t * t) * (bend_scale + (3 * 0.044715 * bend_scale) * sq)
                part = dot(act, w2_r[cols, :])
                outer = part if outer is None else outer + part
            h2 = h1 + m(5) * outer
            norm2, inv2 = norm_parts(h2)
            fin = (norm2 * (1.0 + m(7)) + m(6)).astype(bf16)
            out = dot_nt(wo, fin)
            log_beta, post_log, coef = (con_r[i : i + 1, n : n + 1] for n in (2, 3, 4))
            miss = out[:PIN] - noi_r[i]
            mixing = (out[PIN:] + 1.0) * 0.5
            log_var = mixing * log_beta + (1.0 - mixing) * post_log
            ratio = jnp.exp(post_log - log_var)
            square = miss * miss
            weigh = coef * jnp.exp(-log_var)
            terms = square + 0.5 * (-1.0 + log_var - post_log + ratio + weigh * square)
            losses += share * jnp.sum(jnp.sum(terms, axis=0, keepdims=True), axis=1, keepdims=True)
            d_guess = share * miss * (2.0 + weigh)
            d_mixed = (share * 0.25) * (1.0 - ratio - weigh * square) * (log_beta - post_log)
            d_out = jnp.concatenate([d_guess, d_mixed], axis=0).astype(bf16)
            piece = dot(d_out, fin)
            g_last = piece if g_last is None else g_last + piece
            d_fin = dot_tn(d_out, wo)
            put(6, d_fin)
            put(7, d_fin * norm2)
            d_h2 = norm_back(d_fin * (1.0 + m(7)), norm2, inv2)
            put(5, d_h2 * outer)
            d_outer = (m(5) * d_h2).astype(bf16)
            douter_r[tokens, :] = d_outer
            d_mlp = None
            for b in range(FF // WIDE):
                cols = slice(b * WIDE, (b + 1) * WIDE)
                d_in = (dot_nt(d_outer, w2_r[cols, :]) * slope_r[:, cols]).astype(bf16)
                dinner_r[tokens, cols] = d_in
                part = dot_nt(d_in, w1_r[:, cols])
                d_mlp = part if d_mlp is None else d_mlp + part
            put(3, d_mlp)
            put(4, d_mlp * norm1)
            d_h1 = d_h2 + norm_back(d_mlp * (1.0 + m(4)), norm1, inv1)
            dh1_r[i] = d_h1
            put(2, d_h1 * branch)
            d_br = (m(2) * d_h1).astype(bf16)
            dbr_r[tokens, :] = d_br
            dmix_r[i] = dot_nt(d_br, wp_r[...]).astype(bf16)
        loss_r[...] = jnp.broadcast_to(losses, loss_r.shape)
        glast_r[...] = g_last
        mix = jnp.concatenate([mix_r[i] for i in range(images)], axis=0)
        if not fast:
            g_refs[0][...] = dot_tn(mix, dbr_r[...])
        else:
            deal_rows(*g_refs, dot_tn(mix, dbr_r[...]), at[1], 0)
        for b in range(FF // BLOCK):
            cols = slice(b * BLOCK, (b + 1) * BLOCK)
            g_in = dot_tn(mlp_r[...], dinner_r[:, cols])
            g_out = dot_tn(act_r[:, cols], douter_r[...])
            if not fast:
                g_refs[1][:, cols] = g_in
                g_refs[2][cols, :] = g_out
                continue
            deal_rows(*g_refs, g_in, at[1], D + b * BLOCK)
            deal(*g_refs, g_out[0:192], g_out[192:384], at[1], b, D + FF, 4)

    if fast:
        outs = [((4, 48, D + 2 * FF), f32), ((4, 48, D + 2 * FF), bf16)]
    else:
        outs = [((D, D), f32), ((D, FF), f32), ((FF, D), f32)]
    outs += [
        ((POUT, D), f32),
        ((images, TOK_IMG, D), bf16),
        ((images, TOK_IMG, D), f32),
        ((images, 8 * D), f32),
        ((8, 128), f32),
    ]
    ops = (place, noi, con, mod, h0_all, mix_all, head, *weights)
    many = images * TOK_IMG
    scratch = [pltpu.VMEM((many, n), bf16) for n in (D, FF, FF, D, D)] + [pltpu.VMEM((TOK_IMG, FF), f32)]
    if fast:
        scratch += [pltpu.VMEM(shape, bf16) for shape in ((D, D), (D, FF), (FF, D))]
    return kernel_call(body, outs, ops, 13, scratch=scratch, places="s" + "v" * (len(ops) - 1), after=after, room=32)


def deal(keep_r, send_r, left, right, core, chip, lanes, blocks=1):
    rows, width = left.shape[0] // blocks, left.shape[1]
    kept = jnp.where(core == 0, left, right)
    sent = jnp.where(core == 0, right, left).astype(bf16)
    for b in range(blocks):
        cols = slice(lanes + b * width, lanes + (b + 1) * width)
        keep_r[chip, :, cols] = kept[b * rows : (b + 1) * rows]
        send_r[chip, :, cols] = sent[b * rows : (b + 1) * rows]


def deal_rows(keep_r, send_r, grad, core, lanes):
    for c in range(4):
        deal(keep_r, send_r, grad[c * 96 : c * 96 + 48], grad[c * 96 + 48 : c * 96 + 96], core, c, lanes)


MOD_ROWS, MOD_LANES = 16, 512


def heads_back(qkv_all, total_all, dmix_all, after=()):
    images = qkv_all.shape[0]

    def body(qkv_r, total_r, dmix_r, dqkv_r):
        for pair in range(HEADS // 2):
            lanes = slice(pair * 128, pair * 128 + 128)
            for i in range(images):
                q = qkv_r[i, :, pair * 128 : pair * 128 + 128]
                k = qkv_r[i, :, D + pair * 128 : D + pair * 128 + 128]
                v = qkv_r[i, :, 2 * D + pair * 128 : 2 * D + pair * 128 + 128]
                do = dmix_r[i, :, lanes]
                dq = dk = dv = None
                for half in range(2):
                    own = lane_half(q.shape, half)
                    zero = jnp.zeros_like(q)
                    do_h = jnp.where(own, do, zero)
                    q_h = jnp.where(own, q, zero)
                    head = pair * 2 + half
                    p = jnp.exp(dot_nt(q_h, k) * 0.125 - total_r[i, :, head : head + 1])
                    dp = dot_nt(do_h, v)
                    ds = (p * (dp - jnp.sum(dp * p, axis=-1, keepdims=True))).astype(bf16)
                    a = dot(ds, jnp.where(own, k, zero))
                    b = dot_tn(ds, q_h)
                    c = dot_tn(p.astype(bf16), do_h)
                    dq, dk, dv = (a, b, c) if dq is None else (dq + a, dk + b, dv + c)
                rows = slice(i * TOK_IMG, (i + 1) * TOK_IMG)
                for part, value in enumerate((dq * 0.125, dk * 0.125, dv)):
                    dqkv_r[rows, part * D + pair * 128 : part * D + pair * 128 + 128] = value.astype(bf16)

    outs = [((images * TOK_IMG, 3 * D), bf16)]
    return kernel_call(body, outs, (qkv_all, total_all, dmix_all), 4, after=after)[0]


def attention_back(place, mod, h0_all, attn_all, dqkv, dh1_all, dmod_all, w_qkv, noisy_all, g_last, loss_tile, info, after=()):
    images = mod.shape[0]

    def body(at, mod_r, h0_r, attn_r, dqkv_r, dh1_r, dmod_in, wq_r, noisy_r, last_r, loss_r, *refs):
        *g_refs, dmod_r, line = refs if info is None else refs[1:]
        patch = None
        for i in range(images):
            rows = slice(i * TOK_IMG, (i + 1) * TOK_IMG)
            d_attn = None
            for part in range(3):
                cols = slice(part * D, (part + 1) * D)
                piece = dot_nt(dqkv_r[rows, cols], wq_r[:, cols])
                d_attn = piece if d_attn is None else d_attn + piece
            norm, inv = norm_parts(h0_r[i])
            line[i : i + 1, 0:D] = jnp.sum(d_attn, axis=0, keepdims=True)
            line[i : i + 1, D : 2 * D] = jnp.sum(d_attn * norm, axis=0, keepdims=True)
            line[i : i + 1, 2 * D :] = dmod_in[i : i + 1, 2 * D :]
            d_h0 = (dh1_r[i] + norm_back(d_attn * (1.0 + mod_r[i : i + 1, D : 2 * D]), norm, inv)).astype(bf16)
            piece = dot(noisy_r[i], d_h0)
            patch = piece if patch is None else patch + piece
        if info is not None:
            each = 8 * D // MOD_LANES
            block = [line[i : i + 1, n * MOD_LANES : (n + 1) * MOD_LANES] for i in range(images) for n in range(each)]
            lane = lax.broadcasted_iota(jnp.int32, (1, MOD_LANES), 1)
            loss = loss_r[0:1, 0:1]
            high = loss.astype(bf16).astype(f32)
            mid = (loss - high).astype(bf16).astype(f32)
            low = loss - high - mid
            block.append(jnp.where(lane == 0, high, jnp.where(lane == 1, mid, jnp.where(lane == 2, low, 0.0))))
            told = refs[0][INFO:BUNDLE, :].astype(f32)[0:1]
            block.append(jnp.concatenate([told, jnp.zeros((1, MOD_LANES - D), f32)], axis=1))
            block.append(jnp.zeros((MOD_ROWS - len(block), MOD_LANES), f32))
            block = jnp.concatenate(block, axis=0).astype(bf16)
            for c in range(4):
                dmod_r[c] = block
        else:
            dmod_r[...] = line[...].astype(bf16)
        for part in range(3):
            cols = slice(part * D, (part + 1) * D)
            grad = dot_tn(attn_r[...], dqkv_r[:, cols])
            if info is not None:
                deal_rows(*g_refs, grad, at[1], part * D)
            else:
                g_refs[0][:, cols] = grad
        head = jnp.concatenate([patch, last_r[...]], axis=0)
        if info is None:
            g_refs[1][...] = head
            return
        none = jnp.zeros((HEAD, 128 - 48), f32)
        for c in range(4):
            left = jnp.concatenate([head[:, c * 96 : c * 96 + 48], none], axis=1)
            right = jnp.concatenate([head[:, c * 96 + 48 : c * 96 + 96], none], axis=1)
            deal(*g_refs, left, right, at[1], c, 3 * D)

    if info is None:
        outs = [((D, 3 * D), f32), ((HEAD, D), f32), ((images, 8 * D), bf16)]
    else:
        outs = [((4, 48, TAIL), f32), ((4, 48, TAIL), bf16), ((4, MOD_ROWS, MOD_LANES), bf16)]
    ops = (place, mod, h0_all, attn_all.reshape(-1, D), dqkv, dh1_all, dmod_all, w_qkv, noisy_all, g_last, loss_tile)
    if info is not None:
        ops += (info,)
    scratch = [pltpu.VMEM((images, 8 * D), f32)]
    return kernel_call(body, outs, ops, 4, scratch=scratch, places="s" + "v" * (len(ops) - 1), after=after)


def bundle_rows(tsteps, labels, time1_w, time2_w):
    images = tsteps.shape[0]

    def body(ts_h, lab_h, t1_h, t2_h, out_r, ts, lab, t1_r, t2_r, sems):
        copies = [
            pltpu.make_async_copy(a, b, sems.at[n])
            for n, (a, b) in enumerate(((ts_h, ts), (lab_h, lab), (t1_h, t1_r), (t2_h, t2_r)))
        ]
        for copy in copies:
            copy.start()
        for copy in copies:
            copy.wait()
        rows = t1_r.shape[0]
        out_r[0:rows, :] = t1_r[...].astype(bf16)
        out_r[rows:INFO, :] = t2_r[...].astype(bf16)
        lane = lax.broadcasted_iota(jnp.int32, (BUNDLE - INFO, D), 1)
        info = jnp.zeros((BUNDLE - INFO, D), jnp.int32)
        for i in range(images):
            for n, value in enumerate((ts[i] // 32, ts[i] % 32, lab[i] // 32, lab[i] % 32)):
                info = jnp.where(lane == n * images + i, value, info)
        out_r[INFO:BUNDLE, :] = info.astype(f32).astype(bf16)

    ops = (tsteps, labels, time1_w, time2_w)
    scratch = [pltpu.SMEM((images,), jnp.int32)] * 2 + [pltpu.VMEM(a.shape, f32) for a in ops[2:]] + [pltpu.SemaphoreType.DMA((4,))]
    return kernel_call(body, [((BUNDLE, D), bf16)], ops, 1.5, places="hhhh", scratch=scratch)[0]


def lay_shard(w_r, pa, ou, qk, pr, f1, f2):
    w_r[:, 0 : 3 * D] = qk[...].astype(bf16)
    head = jnp.concatenate([pa[0], ou[0]], axis=0)
    w_r[:, 3 * D : TAIL] = jnp.concatenate([head, jnp.zeros((HEAD, 128 - 48), f32)], axis=1).astype(bf16)
    w_r[:, TAIL : TAIL + D] = pr[...].astype(bf16)
    w_r[:, TAIL + D : TAIL + D + FF] = f1[...].astype(bf16)
    for b in range(4):
        w_r[:, TAIL + D + FF + b * D : TAIL + D + FF + (b + 1) * D] = f2[b * 48 : (b + 1) * 48, :].astype(bf16)


def cast_weights(patch_state, out_t, time1_w, time2_w, table_t, mod_w, qkv_w, proj_w, fc1_w, fc2_w, after=()):
    def body(pa, ou, t1, t2, ta, mo, qk, pr, f1, f2, w_r, mod16, tab16, sums):
        lay_shard(w_r, pa, ou, qk, pr, f1, f2)
        mod16[...] = mo[...].astype(bf16)
        tab16[...] = ta[...].astype(bf16)
        lane = lax.broadcasted_iota(jnp.int32, (8, D), 1)
        line = jnp.zeros((8, D), f32)
        for n, m in enumerate((pa[0], t1[...], t2[...], ta[...], mo[...], qk[...], pr[...], f1[...], f2[...], ou[0])):
            line = jnp.where(lane == n, jnp.sum(jnp.sum(m * m, axis=0, keepdims=True), axis=1, keepdims=True), line)
        sums[...] = line

    outs = [((48, SENT), bf16), (mod_w.shape, bf16), (table_t.shape, bf16), ((8, D), f32)]
    ops = (patch_state, out_t, time1_w, time2_w, table_t, mod_w, qkv_w, proj_w, fc1_w, fc2_w)
    return kernel_call(body, outs, ops, 2.5, after=after, room=CAST_ROOM)


def picked(index, count):
    lane = lax.broadcasted_iota(jnp.int32, (index.shape[0], count), 1)
    return (lane == index).astype(f32).astype(bf16)


def one_hot(shape, test):
    row, col = lax.broadcasted_iota(jnp.int32, shape, 0), lax.broadcasted_iota(jnp.int32, shape, 1)
    return test(row, col).astype(f32).astype(bf16)


def condition_body(infos, images, w1, w2, times_r, tab_r, position):
    own_d = tab_r.shape[0]
    ts, lab = [], []
    for i in range(images):
        for whole in infos:
            ts.append((whole[:, i : i + 1] * 32.0 + whole[:, images + i : images + i + 1]).astype(jnp.int32))
            lab.append((whole[:, 2 * images + i : 2 * images + i + 1] * 32.0 + whole[:, 3 * images + i : 3 * images + i + 1]).astype(jnp.int32))
    ts, lab = jnp.concatenate(ts, axis=0), jnp.concatenate(lab, axis=0)
    feats = dot(picked(ts, STEPS), times_r[...]).astype(bf16)
    act, time_slope = silu_pair(dot(feats, w1))
    act = act.astype(bf16)
    own = one_hot((D, own_d), lambda r, c: r == c + position * own_d)
    emb = dot(act, dot(w2, own).astype(bf16))
    picks = picked(lab, CLASSES)
    cond, cond_slope = silu_pair(emb + dot_nt(picks, tab_r[...]))
    return feats, act, time_slope, picks, cond.astype(bf16), cond_slope, own


def modulation_shares(place, pieces, times, tab16, mod16, images):
    parts = 8
    width = images * D

    def body(at, *refs):
        times_r, tab_r, mod_r, out_r, w1_r, w2_r, info_r = refs[8:]
        for n in range(8):
            owner = piece_owner(at, n)
            w1_r[pl.ds(pl.multiple_of(owner * 32, 32), 32), :] = refs[n][0:32, :]
            w2_r[pl.ds(pl.multiple_of(owner * 48, 48), 48), :] = refs[n][32:INFO, :]
            info_r[pl.ds(owner, 1), :] = refs[n][INFO:BUNDLE, 0:128].astype(f32)[0:1]
        cond = condition_body([info_r[...]], images, w1_r[...], w2_r[...], times_r, tab_r, at[0])[4]
        for s in range(8):
            i, col = divmod(s * width, 8 * D)
            value = dot(cond[i * parts : (i + 1) * parts], mod_r[:, col : col + width])
            for p in range(parts):
                out_r[p, s : s + 1, :] = value[p : p + 1]

    outs = [((parts, 8, width), f32), ((TFREQ, D), bf16), ((D, D), bf16)]
    ops = (place, *pieces, times, tab16, mod16)
    return kernel_call(body, outs, ops, 3, places="s" + "v" * 11, scratch=[pltpu.VMEM((parts, 128), f32)])


def condition_back(place, own_mod, oth_mod, w1, w2, times, tab16, mod16, passed, reps, parts, images):
    devices = reps * parts
    count = devices * images
    own_t, own_d = TFREQ // parts, D // parts
    each = 8 * D // MOD_LANES

    def body(at, own_r, oth_r, w1_r, w2_r, times_r, tab_r, mod_r, in_r, gm_r, gt_r, dc_r, loss_r, feat_r, act_r, slope_r, out_r, all_s, dmod_s):
        out_r[...] = in_r[...]
        for r in range(reps):
            block = slice(r * MOD_ROWS, (r + 1) * MOD_ROWS)
            for c in range(parts // 2):
                mine = pl.multiple_of((r * parts + 2 * c + at[1]) * MOD_ROWS, MOD_ROWS)
                its = pl.multiple_of((r * parts + 2 * c + 1 - at[1]) * MOD_ROWS, MOD_ROWS)
                all_s[pl.ds(mine, MOD_ROWS), :] = own_r[c, block, :]
                all_s[pl.ds(its, MOD_ROWS), :] = oth_r[c, block, :]
        rows = all_s[...]
        take = one_hot((devices, devices * MOD_ROWS), lambda r, c: c == r * MOD_ROWS + images * each + 1)
        infos = dot(take, rows)
        feats, act, time_slope, picks, cond, cond_slope, own = condition_body([infos], images, w1_r[...], w2_r[...], times_r, tab_r, at[0])
        near = one_hot((TFREQ, own_t), lambda r, c: r == c + at[0] * own_t)
        feat_r[...] = dot(feats, near).astype(bf16)
        act_r[...] = dot(act, own).astype(bf16)
        slope_r[...] = time_slope
        for n in range(each):
            take = one_hot((count, devices * MOD_ROWS), lambda r, c: c == (r % devices) * MOD_ROWS + (r // devices) * each + n)
            dmod_s[:, n * MOD_LANES : (n + 1) * MOD_LANES] = dot(take, rows).astype(bf16)
        take = one_hot((8, devices * MOD_ROWS), lambda r, c: c % MOD_ROWS == images * each)
        loss = dot(take, rows)
        loss_r[...] = jnp.broadcast_to(loss[:, 0:1] + loss[:, 1:2] + loss[:, 2:3], loss_r.shape)
        d_mod = dmod_s[...]
        d_cond = dot_nt(d_mod, mod_r[...]) * cond_slope
        wide = jnp.concatenate([d_cond, jnp.zeros((count, 128 - own_d), f32)], axis=1).astype(bf16)
        for p in range(parts):
            dc_r[p] = wide
        gm_r[...] = dot_tn(cond, d_mod)
        high = d_cond.astype(bf16)
        rest = d_cond - high.astype(f32)
        mid = rest.astype(bf16)
        low = (rest - mid.astype(f32)).astype(bf16)
        gt_r[...] = dot_tn(high, picks) + (dot_tn(mid, picks) + dot_tn(low, picks))

    outs = [((own_d, 8 * D), f32), ((own_d, CLASSES), f32), ((parts, count, 128), bf16), ((8, 128), f32)]
    outs += [((count, own_t), bf16), ((count, own_d), bf16), ((count, D), f32), (passed.shape, passed.dtype)]
    ops = (place, own_mod, oth_mod, w1, w2, times, tab16, mod16, passed)
    scratch = [pltpu.VMEM((devices * MOD_ROWS, MOD_LANES), bf16), pltpu.VMEM((count, 8 * D), bf16)]
    return kernel_call(body, outs, ops, 4, scratch=scratch, places="s" + "v" * 8)


def time_back(d_time, w2, act16, slope, feat16):
    parts, own_d = d_time.shape[0], act16.shape[1]
    own_t = TFREQ // parts

    def body(dt_r, w2_r, act_r, slope_r, feat_r, g1_r, g2_r):
        d_all = jnp.concatenate([dt_r[p, :, 0:own_d].astype(f32) for p in range(parts)], axis=1).astype(bf16)
        g2_r[...] = dot_tn(act_r[...], d_all)
        d_hid = (dot_nt(d_all, w2_r[...]) * slope_r[...]).astype(bf16)
        g1_r[...] = dot_tn(feat_r[...], d_hid)

    outs = [((own_t, D), f32), ((own_d, D), f32)]
    return kernel_call(body, outs, (d_time, w2, act16, slope, feat16), 2)


FAR = {"time1": (0, 1), "time2": (1, 1), "mod": (2, 8), "qkv": (10, 3), "proj": (13, 1), "fc1": (14, 4), "fc2": (18, 1), "table": (26, 3)}
NEAR = {"time1": 19, "time2": 20, "mod": 21, "qkv": 22, "proj": 23, "fc1": 24, "fc2": 25, "table": 29}
SUMS, LINES = 30, 32
ORDER = ("time1", "time2", "table", "mod", "qkv", "proj", "fc1", "fc2")


def lanes_of(rows_by_cols):
    ones = jnp.ones((8, rows_by_cols.shape[1]), f32)
    return lax.dot_general(ones, rows_by_cols, (((1,), (1,)), ((), ())), precision=lax.Precision.HIGHEST, preferred_element_type=f32)[0:1]


def put_sums(pack, name, g):
    sq = g * g + grad_floor
    line, count = FAR[name]
    col = jnp.sum(sq, axis=0, keepdims=True)
    for n in range(count):
        size = min(D, g.shape[1] - n * D)
        pack[line + n : line + n + 1, 0:size] = col[:, n * D : n * D + size]
    pack[NEAR[name] : NEAR[name] + 1, 0 : g.shape[0]] = lanes_of(sq)


def copies_sum(refs):
    a, b, c, d = (r[...].astype(f32) for r in refs)
    return (a + b) + (c + d)


def sums_early(place, parts):
    def body(at, a, b, c, d, gm, gf, pack, cuts):
        for n, part in enumerate((a, b, c, d)):
            cuts[jnp.bitwise_xor(at[2], n)] = part[...].astype(f32)
        pack[...] = jnp.zeros((LINES, D), f32)
        gm[:, 0:D] = jnp.concatenate([cuts[j][:, 768 : 768 + 96] for j in range(4)], axis=1)
        for j in range(4):
            gm[:, D + j * 384 : D + (j + 1) * 384] = cuts[j][:, 0:384]
            gf[j * 48 : (j + 1) * 48, :] = cuts[j][:, 384:768]
        put_sums(pack, "proj", gm[:, 0:D])
        put_sums(pack, "fc1", gm[:, D : D + FF])
        put_sums(pack, "fc2", gf[...])

    outs = [((48, D + FF), f32), ((192, D), f32), ((LINES, D), f32)]
    return kernel_call(body, outs, (place, *parts), 2, scratch=[pltpu.VMEM((4, 48, Z_LANES), f32)], places="svvvv")


def sums_middle(pack, g_table, g_mod, sums, loss, after=()):
    def body(old, tab, mod, sums_r, loss_r, pack_r):
        pack_r[...] = old[...]
        put_sums(pack_r, "mod", mod[...])
        put_sums(pack_r, "table", tab[...])
        lane = lax.broadcasted_iota(jnp.int32, (1, D), 1)
        pack_r[SUMS : SUMS + 1, :] = jnp.where(lane == 10, loss_r[0:1, 0:1], sums_r[0:1, :])

    return kernel_call(body, [((LINES, D), f32)], (pack, g_table, g_mod, sums, loss), 2, after=after)[0]


def sums_late(pack, tail, g_time1, g_time2):
    def body(old, q0, q1, q2, q3, t1, t2, gq, pack_r):
        pack_r[...] = old[...]
        gq[...] = copies_sum((q0, q1, q2, q3))
        put_sums(pack_r, "qkv", gq[:, 0 : 3 * D])
        put_sums(pack_r, "time1", t1[...])
        put_sums(pack_r, "time2", t2[...])

    outs = [(tail[0].shape, f32), ((LINES, D), f32)]
    return kernel_call(body, outs, (pack, *tail, g_time1, g_time2), 2)


def scaled_updates(place, packs, g_time1, g_time2, g_table, g_mod, gq, gm, gf, olds, patch_state, out_t):
    parts = packs.shape[0]
    shapes = [(g_time1.shape), g_time2.shape, g_table.shape, g_mod.shape, (48, 3 * D), (48, D), (48, FF), gf.shape]

    def body(at, pk, t1, t2, tab, mod, q, m, f, *refs):
        old_rs, (pat, ost), fresh_rs, u_rs = refs[0:8], refs[8:10], refs[10:18], refs[18:26]
        u_pat, u_out, m_pat, m_out, usq, head, line_s = refs[26:]
        total = jnp.sum(pk[...], axis=0)
        lane = lax.broadcasted_iota(jnp.int32, (1, D), 1)
        grads = (t1[...], t2[...], tab[...], mod[...], q[:, 0 : 3 * D], m[:, 0:D], m[:, D : D + FF], f[...])
        sizes = []

        def size_of(u):
            return jnp.sum(jnp.sum(u * u, axis=0, keepdims=True), axis=1, keepdims=True)

        for name, g, old_r, fresh_r, u_r in zip(ORDER, grads, old_rs, fresh_rs, u_rs):
            rows, cols = g.shape
            many = rows * parts
            line, count = FAR[name]
            far_at, near_at = (0, cols) if name == "table" else (many, 0)
            for p in range(parts):
                line_s[:, near_at + p * rows : near_at + (p + 1) * rows] = pk[p, NEAR[name] : NEAR[name] + 1, 0:rows] / cols
            for n in range(count):
                wide = min(D, cols - n * D)
                line_s[:, far_at + n * D : far_at + n * D + wide] = total[line + n : line + n + 1, 0:wide] / many
            fresh = line_s[:, 0 : many + cols]
            fresh_r[...] = jnp.sum(fresh, axis=0)
            renewed = decay_rate * old_r[...].reshape(1, many + cols) + (1.0 - decay_rate) * fresh
            near, far = renewed[:, near_at : near_at + many], renewed[:, far_at : far_at + cols]
            mean = jnp.mean(far if name == "table" else near, axis=1, keepdims=True)
            shape = (rows, many)
            mine = lax.broadcasted_iota(jnp.int32, shape, 1) == lax.broadcasted_iota(jnp.int32, shape, 0) + at[0] * rows
            own = jnp.sum(jnp.where(mine, near, 0.0), axis=1, keepdims=True)
            u = g * lax.rsqrt(own / mean) * lax.rsqrt(far)
            u_r[...] = u
            sizes.append(size_of(u))
        ends = []
        for lo, wide, old, moment_r, u_r in ((0, PIN, pat, m_pat, u_pat), (PIN, POUT, ost, m_out, u_out)):
            g = q[lo : lo + wide, 3 * D : 3 * D + 48]
            moment = decay_rate * old[1] + (1.0 - decay_rate) * (g * g + grad_floor)
            moment_r[...] = moment
            u = g * lax.rsqrt(moment)
            u_r[...] = u
            ends.append(size_of(u))
        line = jnp.zeros((1, D), f32)
        for n, value in enumerate([ends[0], *sizes, ends[1]]):
            line = jnp.where(lane == n, value, line)
        for p in range(parts):
            usq[p] = jnp.broadcast_to(line[:, 0:128], (8, 128))
        head[...] = total[SUMS : SUMS + 1, :] * jnp.where(lane == 10, 1.0 / parts, 1.0)

    outs = [((o.shape[0],), f32) for o in olds] + [(s, f32) for s in shapes]
    outs += [((PIN, 48), f32), ((POUT, 48), f32)] * 2 + [((parts, 8, 128), f32), ((1, D), f32)]
    ops = (place, packs, g_time1, g_time2, g_table, g_mod, gq, gm, gf, *olds, patch_state, out_t)
    scratch = [pltpu.VMEM((1, 9 * D + 128), f32)]
    return kernel_call(body, outs, ops, 3.5, scratch=scratch, places="s" + "v" * (len(ops) - 1))


def new_weights(usq, head, counts, images, updates, weights, patch_state, out_t, m_patch, m_out):
    def body(usq_r, head_r, mp, mo, pat, ost, *refs):
        us, ms, news = refs[0:10], refs[10:18], refs[18:26]
        new_p, new_o, loss_r, rms_r = refs[26:]
        total = usq_r[0, 0:1, :]
        for p in range(1, usq_r.shape[0]):
            total = total + usq_r[p, 0:1, :]
        lane = lax.broadcasted_iota(jnp.int32, (1, 128), 1)
        size = jnp.ones((1, 128), f32)
        for n, count in enumerate(counts):
            size = jnp.where(lane == n, float(count), size)
        rms = jnp.sqrt(total / size)
        step = step_rate * jnp.sqrt(head_r[:, 0:128] / size) / jnp.maximum(1.0, rms / clip_level)
        for n in range(8):
            news[n][...] = ms[n][...] - step[:, n + 1 : n + 2] * us[n + 1][...]
        new_p[0] = pat[0] - step[:, 0:1] * us[0][...]
        new_p[1] = mp[...]
        new_o[0] = ost[0] - step[:, 9:10] * us[9][...]
        new_o[1] = mo[...]
        rms_r[...] = jnp.sum(rms[:, 0:10], axis=0)
        loss_r[...] = jnp.sum(head_r[:, 10:11], axis=0) / images

    outs = [(m.shape, f32) for m in weights] + [(patch_state.shape, f32), (out_t.shape, f32), ((1,), f32), ((10,), f32)]
    ops = (usq, head, m_patch, m_out, patch_state, out_t, *updates, *weights)
    return kernel_call(body, outs, ops, 3.5)


def gather_pieces(x):
    near = [x, flip(x, 2), flip(x, 4), flip(x, 6)]
    return near + [flip(a, 1) for a in near]


HALF = 2432


def half_shard(place, patch_state, out_t, qkv_w, proj_w, fc1_w, fc2_w, after=()):
    def body(at, pa, ou, qk, pr, f1, f2, out, all_s):
        lay_shard(all_s, pa, ou, qk, pr, f1, f2)
        for j in range(2):

            @pl.when(at[2] % 2 == j)
            def _():
                out[...] = all_s[:, j * HALF : (j + 1) * HALF]

    ops = (place, patch_state, out_t, qkv_w, proj_w, fc1_w, fc2_w)
    scratch = [pltpu.VMEM((48, 2 * HALF), bf16)]
    return kernel_call(body, [((48, HALF), bf16)], ops, 1, scratch=scratch, places="s" + "v" * 6, after=after)[0]


def stacked_pieces(place, three, halves, after=()):
    def body(at, own, x, y, a, b, first, second, cuts):
        for n, ref in enumerate((own, x, y)):
            first[n] = ref[:, 0:TAIL]
            second[n] = ref[:, TAIL:]
        for n, ref in enumerate((a, b)):
            cuts[jnp.bitwise_xor(at[2] % 2, n)] = ref[...]
        first[3] = cuts[0][:, 0:TAIL]
        second[3, :, 0 : HALF - TAIL] = cuts[0][:, TAIL:]
        second[3, :, HALF - TAIL :] = cuts[1][:, 0 : SENT - HALF]

    ops = (place, *three, *halves)
    scratch = [pltpu.VMEM((2, 48, HALF), bf16)]
    outs = [((4, 48, TAIL), bf16), ((4, 48, SENT - TAIL), bf16)]
    return kernel_call(body, outs, ops, 1, scratch=scratch, places="s" + "v" * 5, after=after)


def chip_blocks(place, keep, sent, micros, after=()):
    def body(at, keep_r, sent_r, *refs):
        for n, out in enumerate(refs):
            chip = jnp.bitwise_xor(at[0] // 2, n)
            out[...] = (keep_r[chip] + sent_r[chip].astype(f32)).astype(out.dtype)

    shape = keep.shape[1:]
    return kernel_call(body, [(shape, f32)] + [(shape, bf16)] * 3, (place, keep, sent), micros, places="svv", after=after)


def tail_blocks(place, keep, sent, d_mods, after=()):
    side = 4 * MOD_ROWS

    def body(at, keep_r, sent_r, *refs):
        outs, mods = refs[1:5], refs[5]
        for n in range(4):
            mods[n * MOD_ROWS : (n + 1) * MOD_ROWS, :] = refs[0][n]
        for n, out in enumerate(outs):
            chip = jnp.bitwise_xor(at[0] // 2, n)
            value = (keep_r[chip] + sent_r[chip].astype(f32)).astype(out.dtype)
            if n == 0:
                out[...] = value
                continue
            out[0:48, 0:TAIL] = value
            out[48:side, 0:TAIL] = jnp.zeros((side - 48, TAIL), bf16)
            out[:, TAIL:] = mods[...]

    outs = [((48, TAIL), f32)] + [((side, TAIL + MOD_LANES), bf16)] * 3 + [((side, MOD_LANES), bf16)]
    return kernel_call(body, outs, (place, keep, sent, d_mods), 1, places="svvv", after=after)


def tail_sum(place, own, arrived, mods, after=()):
    def body(at, own_r, a, b, c, mod_r, out, all_r):
        total = own_r[...] + a[0:48, 0:TAIL].astype(f32)
        out[...] = (total + (b[0:48, 0:TAIL].astype(f32) + c[0:48, 0:TAIL].astype(f32))).astype(bf16)
        chip = at[0] // 2
        all_r[chip] = mod_r[...]
        for n, ref in enumerate((a, b, c)):
            all_r[jnp.bitwise_xor(chip, n + 1)] = ref[:, TAIL:]

    outs = [((48, TAIL), bf16), ((4,) + mods.shape, bf16)]
    return kernel_call(body, outs, (place, own, *arrived, mods), 1, places="svvvvv", after=after)


Z_LANES = 384 + 384 + 128


def copy_blocks(place, parts, after=()):
    def body(at, a, b, c, d, own, one, two, three, cuts):
        total = (a[...] + b[...].astype(f32)) + (c[...].astype(f32) + d[...].astype(f32))
        none = jnp.zeros((48, 32), f32)
        for j in range(4):
            cuts[j, :, 0:384] = total[:, D + j * 384 : D + (j + 1) * 384]
            cuts[j, :, 384:768] = total[:, D + FF + j * 384 : D + FF + (j + 1) * 384]
            cuts[j, :, 768:] = jnp.concatenate([total[:, j * 96 : (j + 1) * 96], none], axis=1)
        for n, out in enumerate((own, one, two, three)):
            out[...] = cuts[jnp.bitwise_xor(at[2], n)].astype(out.dtype)

    outs = [((48, Z_LANES), f32)] + [((48, Z_LANES), bf16)] * 3
    return kernel_call(body, outs, (place, *parts), 2, scratch=[pltpu.VMEM((4, 48, Z_LANES), f32)], places="svvvv", after=after)


def four_sum(parts, after=()):
    def body(a, b, c, d, out):
        out[...] = ((a[...].astype(f32) + b[...].astype(f32)) + (c[...].astype(f32) + d[...].astype(f32))).astype(bf16)

    return kernel_call(body, [(parts[0].shape, bf16)], parts, 1, after=after)[0]


def other_copies(total):
    return (total, flip(total, 1, "rep"), flip(total, 2, "rep"), flip(total, 3, "rep"))


def eight_by_four(
    latents, noise, tsteps, labels, patch_state, time1_w, time2_w, table_t, mod_w, qkv_w, proj_w, fc1_w, fc2_w, out_t, olds, place, plan, grid, times
):
    reps, parts = 4, 8
    images = tsteps.shape[0]
    bundle = bundle_rows(tsteps, labels, time1_w, time2_w)
    pieces = gather_pieces(bundle)
    w_own, mod16, tab16, sums = cast_weights(
        patch_state, out_t, time1_w, time2_w, table_t, mod_w, qkv_w, proj_w, fc1_w, fc2_w, after=pieces[1:4]
    )
    half = half_shard(place, patch_state, out_t, qkv_w, proj_w, fc1_w, fc2_w, after=(bundle,))
    half = flip(half, 6)
    halves = [half, flip(half, 1, "rep")]
    w_three = [w_own, flip(w_own, 2), flip(w_own, 4)]
    shares, w1, w2 = modulation_shares(place, pieces, times, tab16, mod16, images)
    shares = lax.all_to_all(shares, "fsdp", 0, 0)
    w_near = stacked_pieces(place, w_three, halves, after=(shares,))
    q_pieces, w_pieces = ([near, flip(near, 1)] for near in w_near)

    w_qkv, head, mod, con, noisy, hidden0, attn16, qkv16, totals, mixture16 = attention_forward(
        tsteps, latents, noise, plan, grid, q_pieces, shares, place
    )
    keep, send, g_last, d_mix16, d_h1, d_mod, loss_tile = mlp_pass(
        noise, con, mod, hidden0, mixture16, head, w_pieces, place
    )
    send = flip(send, 1)
    d_qkv16 = heads_back(qkv16, totals, d_mix16, after=(keep,))
    blocks = chip_blocks(place, keep, send, 2, after=(d_qkv16,))
    q_keep, q_send, d_mod16 = attention_back(
        place, mod, hidden0, attn16, d_qkv16, d_h1, d_mod, w_qkv, noisy, g_last, loss_tile, bundle, after=(blocks[1],)
    )
    q_send = flip(q_send, 1)
    arrived = [flip(blocks[n], 2 * n) for n in range(1, 4)]
    cuts = copy_blocks(place, [blocks[0]] + arrived)
    q_own, *q_blocks, d_mods = tail_blocks(place, q_keep, q_send, lax.all_to_all(d_mod16, "rep", 0, 0), after=(cuts[1],))
    q_sum, own_mod = tail_sum(place, q_own, [flip(q_blocks[n], 2 * (n + 1)) for n in range(3)], d_mods)
    oth_mod = flip(own_mod, 1)
    g_mod, g_table, d_time, loss, feat16, act16_t, time_slope, q_sum = condition_back(
        place, own_mod, oth_mod, w1, w2, times, tab16, mod16, q_sum, reps, parts, images
    )
    mid = four_sum([cuts[0]] + [flip(cuts[n], n, "rep") for n in range(1, 4)])
    mid = other_copies(mid)
    tail = other_copies(q_sum)
    gm, gf, pack = sums_early(place, mid)
    d_time = lax.all_to_all(d_time, "fsdp", 0, 0)
    pack = sums_middle(pack, g_table, g_mod, sums, loss)
    g_time1, g_time2 = time_back(d_time, w2, act16_t, time_slope, feat16)
    gq, pack = sums_late(pack, tail, g_time1, g_time2)
    packs = gather_rows(pack).reshape(parts, LINES, D)
    result = scaled_updates(place, packs, g_time1, g_time2, g_table, g_mod, gq, gm, gf, olds, patch_state, out_t)
    fresh, updates = result[:8], result[8:16]
    u_patch, u_out, m_patch, m_out, usq, sums = result[16:]
    usq = lax.all_to_all(usq, "fsdp", 0, 0)
    weights = (time1_w, time2_w, table_t, mod_w, qkv_w, proj_w, fc1_w, fc2_w)
    counts = [w.size * parts for w in (patch_state[0], *weights, out_t[0])]
    *news, new_patch, new_out, loss, rms = new_weights(
        usq, sums, counts, images * reps * parts, (u_patch, *updates, u_out), weights, patch_state, out_t, m_patch, m_out
    )
    news[2] = news[2].T
    outs = [new_patch]
    for n in range(8):
        outs += [news[n], fresh[n]]
    return tuple(outs) + (new_out.transpose(0, 2, 1), loss.reshape(()), rms)


def per_device(
    latents,
    noise,
    timesteps,
    labels,
    patch_state,
    time1_w,
    time1_f,
    time2_w,
    time2_f,
    table_w,
    table_f,
    mod_w,
    mod_f,
    qkv_w,
    qkv_f,
    proj_w,
    proj_f,
    fc1_w,
    fc1_f,
    fc2_w,
    fc2_f,
    out_state,
):
    reps, parts = lax.axis_size("rep"), lax.axis_size("fsdp")
    position = lax.axis_index("fsdp")
    masters = (patch_state[0], time1_w, time2_w, table_w, mod_w, qkv_w, proj_w, fc1_w, fc2_w, out_state[0])
    images = latents.shape[0] * latents.shape[1]
    latents = latents.reshape(images, TOK_IMG, PIN).transpose(0, 2, 1)
    noise = noise.reshape(images, TOK_IMG, PIN).transpose(0, 2, 1)
    out_t = out_state.transpose(0, 2, 1)
    tsteps = timesteps.reshape(images)
    labels = labels.reshape(images)
    own_d = D // parts
    own_t = TFREQ // parts
    place = jnp.stack([position, position & 1, lax.axis_index("rep")]).astype(jnp.int32)
    plan, grid = jnp.asarray(plan_table()), jnp.asarray(place_table())
    times = jnp.asarray(time_table(), bf16)
    olds = (time1_f, time2_f, table_f, mod_f, qkv_f, proj_f, fc1_f, fc2_f)

    if parts == 8 and reps == 4:
        return eight_by_four(
            latents, noise, tsteps, labels, patch_state, time1_w, time2_w, table_w.T, mod_w, qkv_w, proj_w, fc1_w, fc2_w, out_t, olds, place, plan, grid, times
        )

    info = jnp.stack([tsteps // 32, tsteps % 32, labels // 32, labels % 32]).reshape(1, 4 * images)
    info_row = jnp.pad(info.astype(bf16), ((0, 0), (0, D - 4 * images)))
    bundle = jnp.concatenate([time1_w.astype(bf16), time2_w.astype(bf16), info_row], axis=0)
    bundle = gather_rows(bundle).reshape(parts, own_t + own_d + 1, D)
    w_time1 = bundle[:, :own_t].reshape(TFREQ, D)
    w_time2 = bundle[:, own_t : own_t + own_d].reshape(D, D)
    info_rep = bundle[:, own_t + own_d, : 4 * images]

    head = lax.all_gather(jnp.concatenate([patch_state[0], out_t[0]], axis=0).astype(bf16), "fsdp", axis=1, tiled=True)
    w_rows = gather_rows(jnp.concatenate([qkv_w, proj_w, fc1_w], axis=1).astype(bf16))
    w_fc2 = gather_rows(fc2_w.astype(bf16))
    w_qkv, w_proj, w_fc1 = w_rows[:, : 3 * D], w_rows[:, 3 * D : 4 * D], w_rows[:, 4 * D :]

    info_all = rep_gather(info_rep).reshape(reps * parts, 4, images).astype(jnp.int32)
    w_mod16 = mod_w.astype(bf16)
    w_table16 = table_w.astype(bf16)

    def condition_path(info_any):
        ts = (info_any[:, 0] * 32 + info_any[:, 1]).reshape(-1)
        lab = (info_any[:, 2] * 32 + info_any[:, 3]).reshape(-1)
        feats16 = dot(pick(ts, STEPS), times).astype(bf16)
        time_act, time_slope = silu_pair(dot(feats16, w_time1))
        time_act16 = time_act.astype(bf16)
        time_emb = dot(time_act16, w_time2)
        own_emb = lax.dynamic_slice(time_emb, (0, position * own_d), (time_emb.shape[0], own_d))
        picks = pick(lab, CLASSES)
        cond_act, cond_slope = silu_pair(own_emb + dot(picks, w_table16))
        return feats16, time_act16, time_slope, picks, cond_act.astype(bf16), cond_slope

    info_here = info_rep.reshape(parts, 4, images).astype(jnp.int32)
    cond_here = condition_path(info_here)[4]
    shares = dot(cond_here, w_mod16).reshape(parts, 8, images * D)
    shares = lax.all_to_all(shares, "fsdp", 0, 0, tiled=True)

    mod, con, noisy, hidden0, attn16, qkv16, totals, mixture16 = attention_forward(
        tsteps, latents, noise, plan, grid, (w_qkv, head), shares, place
    )
    g_proj, g_fc1, g_fc2, g_last, d_mix16, d_h1, d_mod, loss_tile = mlp_pass(
        noise, con, mod, hidden0, mixture16, head, (w_proj, w_fc1, w_fc2), place
    )
    loss_part = loss_tile[0, 0]
    g_tail, g_head, d_mod16 = attention_back(
        place, mod, hidden0, attn16, heads_back(qkv16, totals, d_mix16), d_h1, d_mod, w_qkv, noisy, g_last, loss_tile, None
    )

    d_mod_all = rep_gather(d_mod16).reshape(1, -1)
    d_mod_all = gather_rows(d_mod_all).reshape(parts, reps, images, 8 * D)
    d_mod_all = d_mod_all.transpose(1, 0, 2, 3).reshape(reps * parts * images, 8 * D)
    feats16, time_act16, time_slope, picks, cond16, cond_slope = condition_path(info_all)
    d_cond = dot_nt(d_mod_all, w_mod16) * cond_slope
    g_mod = dot_tn(cond16, d_mod_all)
    g_table = lax.dot_general(
        picks.astype(f32), d_cond, (((0,), (0,)), ((), ())), precision=lax.Precision.HIGHEST
    )
    d_time16 = lax.all_gather(d_cond.astype(bf16), "fsdp", axis=0)
    d_time16 = d_time16.transpose(1, 0, 2).reshape(-1, D)
    own_act16 = lax.dynamic_slice(time_act16, (0, position * own_d), (time_act16.shape[0], own_d))
    g_time2 = dot_tn(own_act16, d_time16)
    d_hid16 = (dot_nt(d_time16, w_time2) * time_slope).astype(bf16)
    own_feat16 = lax.dynamic_slice(feats16, (0, position * own_t), (feats16.shape[0], own_t))
    g_time1 = dot_tn(own_feat16, d_hid16)

    g_head = lax.psum_scatter(g_head, "fsdp", scatter_dimension=1, tiled=True)
    g_tail, g_proj, g_fc1, g_fc2 = (sum_scatter(g) for g in (g_tail, g_proj, g_fc1, g_fc2))
    g_proj, g_fc1, g_fc2 = (rep_sum(g.astype(bf16)) for g in (g_proj, g_fc1, g_fc2))
    g_tail = rep_sum(g_tail.astype(bf16))
    g_head = rep_sum(g_head)
    grads = (
        g_head[:PIN],
        g_time1,
        g_time2,
        g_table,
        g_mod,
        g_tail,
        g_proj,
        g_fc1,
        g_fc2,
        g_head[PIN:].T,
    )
    loss_part = lax.psum(loss_part, "rep")
    dims = (0, 0, 1, 0, 0, 0, 0, 0)

    packs = []
    for slot in range(8):
        grad, dim = grads[slot + 1], dims[slot]
        squares = grad * grad + grad_floor
        near = jnp.sum(squares, axis=1 - dim)
        far = jnp.sum(squares, axis=dim)
        spread = lax.dynamic_update_slice(
            jnp.zeros((near.shape[0] * parts,), f32), near / far.shape[0], (position * near.shape[0],)
        )
        far = far / (near.shape[0] * parts)
        packs.append(jnp.concatenate([spread, far] if dim == 0 else [far, spread]))
    tail = jnp.stack([jnp.sum(m * m) for m in masters] + [loss_part])
    lengths = [pack.shape[0] for pack in packs]
    totals = lax.psum(jnp.concatenate(packs + [tail]), "fsdp")
    fresh = []
    start = 0
    for length in lengths:
        fresh.append(totals[start : start + length])
        start += length
    square_tot = totals[start : start + 10]
    loss = totals[start + 10] / (images * reps * parts)

    updates, counts = [], []
    plain = []
    for slot in range(10):
        grad = grads[slot]
        if slot in (0, 9):
            state = patch_state if slot == 0 else out_state
            moment = decay_rate * state[1] + (1.0 - decay_rate) * (grad * grad + grad_floor)
            plain.append(moment)
            updates.append(grad * lax.rsqrt(moment))
            counts.append(grad.size * parts)
            continue
        dim = dims[slot - 1]
        renewed = decay_rate * olds[slot - 1] + (1.0 - decay_rate) * fresh[slot - 1]
        rows = grad.shape[0] * (parts if dim == 0 else 1)
        row, col = renewed[:rows], renewed[rows:]
        mean_row = jnp.mean(row)
        if dim == 0:
            row = lax.dynamic_slice(row, (position * grad.shape[0],), (grad.shape[0],))
        else:
            col = lax.dynamic_slice(col, (position * grad.shape[1],), (grad.shape[1],))
        updates.append(grad * lax.rsqrt(row[:, None] * col[None, :] / mean_row))
        counts.append(grad.size * parts)
    update_tot = lax.psum(jnp.stack([jnp.sum(u * u) for u in updates]), "fsdp")
    sizes = np.asarray(counts, np.float32)
    size_rms = jnp.sqrt(update_tot / sizes)
    factor = step_rate * jnp.sqrt(square_tot / sizes) / jnp.maximum(1.0, size_rms / clip_level)
    new = [masters[s] - factor[s] * updates[s] for s in range(10)]
    result = [jnp.stack([new[0], plain[0]])]
    for slot in range(8):
        result += [new[slot + 1], fresh[slot]]
    return tuple(result) + (jnp.stack([new[9], plain[1]]), loss, size_rms)


def solution(mesh):
    images = P(None, ("rep", "fsdp"), None, None)
    singles = P(None, ("rep", "fsdp"))
    rows, cols = P("fsdp", None), P(None, "fsdp")
    placed = (images, images, singles, singles, P(None, None, "fsdp"))
    placed += (rows, P(), rows, P(), cols, P()) + (rows, P()) * 5 + (P(None, "fsdp", None),)
    results = (P(None, None, "fsdp"), rows, P(), rows, P(), cols, P()) + (rows, P()) * 5
    results += (P(None, "fsdp", None), P(), P())
    return jax.shard_map(per_device, mesh=mesh, in_specs=placed, out_specs=results, check_vma=False)
```
